32 devices in a mesh: subj: 2 (over x), tr: 16 (over z, y, core).
Axes of the slice: x: 2, y: 2, z: 4, core: 2. Of those that a mesh axis runs over, the one named last changes fastest.
Arguments:
- features: bfloat16 [1024, 2048], P('tr', 'subj'), may hold values from -6 to 6
- block_orders: int32 [4, 16], replicated, may hold values from 0 to 15, each once within a row
- offsets: int32 [4, 4], replicated, may hold values from 0 to 8
- tap_gains: float32 [4, 4], replicated, may hold values from 0.2 to 1
- weights: bfloat16 [2, 2048, 256], P('subj'), may hold values from -0.125 to 0.125
- signal: bfloat16 [2, 1024, 256], P('subj', 'tr')
- block_owner: int32 [2, 64, 1], P('subj'), may hold values from 0 to 15; in each aligned block of 64 rows (0 to 63, 64 to 127, ..., all dimensions but the last counted through in order) at most 8 rows name the same one
Outputs:
- energy: float32 [2, 1024, 5], P('subj', 'tr')
- scores: float32 [2, 128, 5], P('subj', 'tr')
The draws below stay inside these ranges and needn't reach their ends.
Inputs may be any that keep to these rules, and one draw needn't show every extreme that they name: `block_orders`: each row names every 1024 block once. `block_owner`: no owner is named by more than 8 voxel blocks of one subject.
All inputs are finite; a program needn't handle non-finite values.
Results may differ from the reference program's by a relative error of at most 0.0003.
Values may be sent and summed in bfloat16 or wider, within the bound.
No kernel may reach another device: no remote copies, remote signals or barrier semaphores. Data moves between devices by JAX's collectives and lax.ppermute only.
A program may use at most 64 MiB of HBM per device.

```python
import math
import jax
import jax.numpy as jnp
import numpy as np
from jax import lax

F = 2048
NBAND = 4
NLAG = 4
MAXLAG = 8
NPERM = 4
VB = 4
TRD = 64
NSUBJ = 2
TR = 1024
NB = 64
V = 256
CAP = 8
SLOTS = 128
KC = 5
N_TR = 16


def draw_offsets(key, part):
    keys = jax.random.split(key, 2)
    taps = jax.random.randint(keys[0], (NBAND * NLAG,), 0, MAXLAG + 1)
    spot = jax.random.randint(keys[1], (), 0, NBAND * NLAG)
    taps = jnp.where(jnp.arange(NBAND * NLAG) == spot, MAXLAG, taps)
    return taps.reshape(NBAND, NLAG).astype(jnp.int32)


def draw_signal(key, part):
    keys = jax.random.split(key, 2)
    times = jnp.arange(TR, dtype=jnp.float32) / (TR - 1)
    base = jax.random.normal(keys[0], (NSUBJ, TR, V), jnp.float32)
    rise = jnp.sqrt(3.0 ** times)
    scale = 0.3 * 10.0 ** jax.random.uniform(keys[1], (NSUBJ, 1, V), jnp.float32)
    return (base * rise[None, :, None] * scale).astype(jnp.bfloat16)


def level_of(own_key, extent, cuts, least, top_value):
    level, own = 1.0, jax.random.fold_in(own_key, 6)
    for position, parts in cuts:
        draws = jnp.exp(jax.random.uniform(jax.random.fold_in(own, position), (parts,), jnp.float32, least / len(cuts), top_value / len(cuts)))
        level = level * jnp.repeat(draws, extent[position] // parts).reshape([-1 if axis == position else 1 for axis in range(len(extent))])
    return level


def routed_block(own_key, own, number, rows, count, top, bound, lean):
    order = jax.random.permutation(own_key, count)
    heavy_load, usual = portions_of(count, rows * top, bound, lean, True), portions_of(count, rows * top, bound, lean, False)
    places = jnp.arange(count)

    def named(sizes, offset_by):
        used = int((sizes > 0).sum())
        fixed = max(1, used // 4)
        passed = fixed + (places - fixed + offset_by * (used - fixed)) % max(1, count - fixed)
        return jnp.zeros((count,), jnp.int32).at[order[jnp.where(places < fixed, places, passed)]].set(jnp.asarray(sizes, jnp.int32))

    sizes = jnp.where(number % 4 == 0, named(heavy_load, number // 4), named(usual, number - number // 4 - 1))
    mixed = jax.random.permutation(jax.random.fold_in(own, 3), count)
    giver, receiver = mixed[0:count // 2 * 2:2], mixed[1:count // 2 * 2:2]
    margin = jnp.minimum(sizes[giver] - 1, bound - sizes[receiver]) // 2
    margin = jnp.where((giver == order[0]) | (receiver == order[0]) | (sizes[receiver] == 0), 0, jnp.maximum(margin, 0))
    passed = jax.random.randint(jax.random.fold_in(own, 4), (count // 2,), 0, 1 << 20) % (margin + 1)
    sizes = sizes.at[giver].add(-passed).at[receiver].add(passed)
    items = jnp.searchsorted(jnp.cumsum(sizes), jnp.arange(rows * top), side="right").astype(jnp.int32)
    table = items.reshape(top, rows).T
    table = table[jax.random.permutation(jax.random.fold_in(own, 1), rows)]
    offset_by = jax.random.randint(jax.random.fold_in(own, 2), (rows, 1), 0, top)
    return jnp.take_along_axis(table, (jnp.arange(top)[None, :] + offset_by) % top, axis=1)


def portions_of(count, total, reach, skew, full):
    weights = [(1 << 20) // math.isqrt(standing ** skew) + 1 for standing in range(1, count + 1)]
    largest = reach if full else min(reach, max(-(-total // count), total * weights[0] // sum(weights)))
    least = 1 if total - largest >= count - 1 else 0
    counts, spare = [largest] + [least] * (count - 1), total - largest - least * (count - 1)
    while spare > 0:
        candidates = [i for i in range(1, count) if counts[i] < largest] or [i for i in range(1, count) if counts[i] < reach]
        whole, budget = sum([weights[i] for i in candidates]), spare
        for i in candidates:
            extra = min(reach - counts[i], max(1, budget * weights[i] // whole), spare)
            counts[i] = counts[i] + extra
            spare = spare - extra
    return np.array(counts)


def gaussian(own_key, shape, spread, most, cuts=(), held_as=jnp.bfloat16):
    array = spread * jax.random.normal(own_key, shape, jnp.float32)
    if cuts:
        array = array * level_of(own_key, shape, cuts, -0.22, 0.18)
    return jnp.clip(array, -most, most).astype(held_as)


def setup_inputs(seed: int = 0) -> dict:
    key_list = jax.random.split(jax.random.key(seed), 8)
    features = gaussian(key_list[0], (TR, F), 1.0, 6.0, ((0, 16), (1, 2)))
    block_orders = jax.vmap(lambda own: jax.random.permutation(own, N_TR))(jax.random.split(key_list[1], NPERM)).reshape((NPERM, N_TR)).astype(jnp.int32)
    offsets = draw_offsets(jax.random.fold_in(key_list[7], 71), 0)
    tap_gains = jnp.clip(jax.random.uniform(key_list[3], (NBAND, NLAG), jnp.float32, 0.2, 1.0), 0.2, 1.0)
    weights = gaussian(key_list[4], (NSUBJ, F, V), F ** -0.5, 0.125, ((0, 2),))
    signal = draw_signal(jax.random.fold_in(key_list[7], 71), 0)
    block_owner_keys = jax.random.split(jax.random.fold_in(key_list[6], 1), NSUBJ * NB // NB)
    block_owner_turns = jax.random.permutation(jax.random.fold_in(key_list[6], 3), NSUBJ * NB // NB)
    block_owner = jax.vmap(lambda own, number: routed_block(jax.random.fold_in(key_list[6], 2), own, number, NB, N_TR, 1, CAP, 2))(block_owner_keys, block_owner_turns).reshape((NSUBJ, NB, 1))
    return {"features": features, "block_orders": block_orders, "offsets": offsets, "tap_gains": tap_gains, "weights": weights, "signal": signal, "block_owner": block_owner}


def filter_series(series, offsets, tap_gains):
    width = F // NBAND
    padded = jnp.concatenate([jnp.zeros((KC, MAXLAG, F), jnp.bfloat16), series], axis=1)
    pieces = []
    for band in range(NBAND):
        part = padded[:, :, band * width:(band + 1) * width]
        total = jnp.zeros((KC, TR, width), jnp.float32)
        for lag in range(NLAG):
            start = (MAXLAG - offsets[band, lag]).astype(jnp.int32)
            total = total + tap_gains[band, lag] * lax.dynamic_slice_in_dim(part, start, TR, 1).astype(jnp.float32)
        pieces.append(total)
    return jnp.concatenate(pieces, axis=2).astype(jnp.bfloat16)


def reference(features, block_orders, offsets, tap_gains, weights, signal, block_owner):
    blocked = features.reshape(N_TR, TRD, F)
    moved = [blocked[block_orders[k]].reshape(TR, F) for k in range(NPERM)]
    series = jnp.stack([features] + moved, axis=0)
    filtered = filter_series(series, offsets, tap_gains).astype(jnp.float32)

    def one_subject(inputs):
        weight, measured, owners = inputs
        predicted = jnp.einsum("ctf,fv->ctv", filtered, weight.astype(jnp.float32))
        values = measured.astype(jnp.float32)
        residual = values[None] - predicted
        squared = residual * residual
        energy = jnp.mean(squared, axis=2).T
        rss = jnp.sum(squared, axis=1)
        tss = jnp.sum(values * values, axis=0)
        fit = jnp.log((rss + 1e-6) / (tss + 1e-6)[None, :])
        block_fit = jnp.mean(fit.reshape(KC, NB, VB), axis=2).T
        owner_list = owners[:, 0].astype(jnp.int32)
        order = jnp.arange(NB, dtype=jnp.int32)
        rank = jnp.sum(((owner_list[:, None] == owner_list[None, :]) & (order[:, None] > order[None, :])).astype(jnp.int32), axis=1)
        slot = (owner_list * CAP + rank).astype(jnp.int32)
        scores = jnp.zeros((SLOTS, KC), jnp.float32).at[slot].set(block_fit)
        return energy, scores

    return lax.map(one_subject, (weights, signal, block_owner))
```

```python
import functools

import jax
import jax.numpy as jnp
from jax import lax
from jax.experimental import pallas as pl
from jax.experimental.pallas import tpu as pltpu
from jax.sharding import PartitionSpec as P

MAXLAG = 8
VB = 4
CAP = 8
LANES = 128
EPSILON = 1e-6

f32 = jnp.float32
bf16 = jnp.bfloat16
i32 = jnp.int32

VMEM = pl.BlockSpec(memory_space=pltpu.VMEM)
SMEM = pl.BlockSpec(memory_space=pltpu.SMEM)


def iota(shape, axis):
    return lax.broadcasted_iota(i32, shape, axis)


def dot(a, b):
    return jnp.dot(a, b, preferred_element_type=f32)


def thirds(x):
    first = x.astype(bf16)
    rest = x - first.astype(f32)
    second = rest.astype(bf16)
    return first, second, (rest - second.astype(f32)).astype(bf16)


def params(**more):
    return pltpu.CompilerParams(vmem_limit_bytes=48 * 1024 * 1024, **more)


def cost(flops, nbytes):
    return pl.CostEstimate(flops=flops, bytes_accessed=nbytes, transcendentals=0)


class Sizes:
    def __init__(self, features, block_orders, offsets, weights, block_owner):
        self.subjects = lax.axis_size("subj")
        self.n = lax.axis_size("tr")
        self.rows, self.width = features.shape
        self.columns, self.voxels = weights.shape[1:]
        self.bands, self.taps = offsets.shape
        self.band_width = self.columns // self.bands
        self.piece = min(self.width, self.band_width)
        self.conditions = block_orders.shape[0] + 1
        self.blocks = block_owner.shape[1]
        self.own_rows = self.rows // self.n
        self.own_ext = self.own_rows + 1
        self.ext = self.own_ext * self.n
        self.slots = 2 * self.own_ext + self.own_rows
        self.slots_padded = -(-self.slots // 16) * 16
        self.residual_rows = (self.conditions + 1) * self.own_rows * self.n
        self.owned = CAP * VB
        self.energy_lane = (self.conditions + 1) * self.owned
        used = self.energy_lane + self.conditions * self.own_rows
        self.lanes = -(-used // LANES) * LANES
        assert self.rows % self.n == 0 and self.n >= MAXLAG


def filtered_product(z, x_ref, w_ref, table_ref, source):
    total = jnp.zeros((z.ext, z.voxels), f32)
    for part in range(z.width // z.piece):
        first = source * z.width + part * z.piece
        first = pl.multiple_of(first, z.piece)
        x = x_ref[:, part * z.piece : (part + 1) * z.piece]
        table = table_ref[lax.div(first, z.band_width)]
        stacked = jnp.concatenate([x] * (table.shape[1] // z.rows), axis=0)
        filtered = dot(table, stacked)
        high = filtered.astype(bf16)
        low = filtered - high.astype(f32)
        tail = z.rows + MAXLAG
        edges = [filtered, low[:MAXLAG], low[z.rows : tail]]
        edges = jnp.concatenate(edges, axis=0).astype(bf16)
        product = dot(edges, w_ref[pl.ds(first, z.piece), :])
        total = total + product[: z.ext]
        head = product[z.ext : z.ext + MAXLAG]
        rim = product[z.ext + MAXLAG :]
        parts = [head, jnp.zeros((z.rows - MAXLAG, z.voxels), f32), rim]
        if z.ext > tail:
            parts.append(jnp.zeros((z.ext - tail, z.voxels), f32))
        total = total + jnp.concatenate(parts, axis=0)
    return total


def fill_table(z, offsets_ref, gains_ref, table_ref):
    lanes = table_ref.shape[2]
    column = iota((z.ext, lanes), 1)
    lag = iota((z.ext, lanes), 0) - column % z.rows
    term = column // z.rows
    for band in range(z.bands):
        value = jnp.zeros((z.ext, lanes), f32)
        for tap in range(z.taps):
            hit = lag == offsets_ref[band, tap]
            value = value + jnp.where(hit, gains_ref[band, tap], 0.0)
        first, second, third = (t.astype(f32) for t in thirds(value))
        chosen = jnp.where(term == 0, first, jnp.where(term == 1, second, third))
        chosen = jnp.where(term > 2, 0.0, chosen)
        table_ref[band] = chosen.astype(bf16)


def fill_choice(z, orders_ref, choice_ref):
    shape = (z.residual_rows, z.slots_padded * z.n)
    per = z.own_rows * z.n
    permutations = z.conditions - 1
    row = iota((z.residual_rows, 1), 0)
    condition = row // per
    own = (row % per) // z.n
    position = row % z.n
    which = iota((z.residual_rows, permutations), 1)
    wanted = (which == condition - 1).astype(f32).astype(bf16)
    orders = dot(wanted, orders_ref[...].astype(f32).astype(bf16))
    place = iota((z.residual_rows, z.n), 1)
    here = jnp.sum(jnp.where(place == position, orders, 0.0), axis=1, keepdims=True)
    ahead = jnp.where(place == position - 1, orders, 0.0)
    ahead = jnp.sum(ahead, axis=1, keepdims=True)
    observed = condition == 0
    here = jnp.where(observed, position, here.astype(i32))
    ahead = jnp.where(observed, position - 1, ahead.astype(i32))
    ahead = jnp.where((position == 0) | (own > 0), -1, ahead)
    signal_only = condition == z.conditions
    here = jnp.where(signal_only, -1, here)
    ahead = jnp.where(signal_only, -1, ahead)
    column = iota(shape, 1)
    source = column // z.slots_padded
    slot = column % z.slots_padded
    half = jnp.where(slot >= z.own_ext, slot - z.own_ext, slot)
    predicted = (source == here) & (half == own) & (slot < 2 * z.own_ext)
    rim = (source == ahead) & (half == z.own_rows) & (slot < 2 * z.own_ext)
    measured = (source == position) & (slot == 2 * z.own_ext + own)
    value = jnp.where(measured, 1.0, jnp.where(predicted | rim, -1.0, 0.0))
    choice_ref[...] = value.astype(bf16)


def fill_owners(z, owners_ref, mine_ref, place_ref):
    owners = owners_ref[...]
    other = iota((z.voxels, z.blocks), 1)
    block = iota((z.voxels, 1), 0) // VB
    owner = jnp.sum(jnp.where(other == block, owners, 0), axis=1, keepdims=True)
    before = (owners == owner) & (other < block)
    rank = jnp.sum(before.astype(i32), axis=1, keepdims=True)
    lane = rank * VB + iota((z.voxels, 1), 0) % VB
    place = iota((z.voxels, LANES), 1) == lane
    place_ref[...] = place.astype(f32).astype(bf16)
    square = (z.blocks, z.blocks)
    diagonal = iota(square, 0) == iota(square, 1)
    down = jnp.sum(jnp.where(diagonal, owners, 0), axis=1, keepdims=True)
    shape = (z.blocks, z.voxels)
    held = iota(shape, 0) == iota(shape, 1) // VB
    along = jnp.sum(jnp.where(held, down, 0), axis=0, keepdims=True)
    mine_ref[...] = (iota((z.n, z.voxels), 0) == along).astype(f32)


def first_kernel(
    z, orders_ref, offsets_ref, gains_ref, owners_ref, x_ref, w_ref,
    table_ref, choice_ref, mine_ref, place_ref, total_ref,
):
    fill_table(z, offsets_ref, gains_ref, table_ref)
    me = lax.axis_index("subj")
    total_ref[...] = filtered_product(z, x_ref, w_ref, table_ref, me)
    fill_choice(z, orders_ref, choice_ref)
    fill_owners(z, owners_ref, mine_ref, place_ref)


def second_kernel(z, table_ref, w_ref, total_ref, signal_ref, *refs):
    others, out_ref = refs[:-1], refs[-1]
    me = lax.axis_index("subj")
    total = total_ref[...]
    for step, x_ref in enumerate(others):
        source = lax.rem(me + step + 1, z.subjects)
        total = total + filtered_product(z, x_ref, w_ref, table_ref, source)
    high = total.astype(bf16)
    low = total - high.astype(f32)
    stacked = jnp.concatenate([total, low, signal_ref[0].astype(f32)], axis=0)
    stacked = stacked.astype(bf16)
    shape = (z.n * z.slots_padded, z.slots * z.n)
    row = iota(shape, 0)
    column = (row % z.slots_padded) * z.n + row // z.slots_padded
    hit = (iota(shape, 1) == column) & (row % z.slots_padded < z.slots)
    order = hit.astype(f32).astype(bf16)
    out_ref[...] = dot(order, stacked).astype(bf16)


def third_kernel(z, choice_ref, mine_ref, place_ref, received_ref, out_ref):
    residual = dot(choice_ref[...], received_ref[...])
    squared = residual * residual
    per = z.own_rows * z.n
    spread = []
    for index in range(z.conditions + 1):
        stat = jnp.sum(squared[index * per : (index + 1) * per], axis=0, keepdims=True)
        spread.append(stat * mine_ref[...])
    spread = jnp.concatenate(spread, axis=0)
    terms = jnp.concatenate(thirds(spread), axis=0)
    placed = dot(terms, place_ref[...])
    count = (z.conditions + 1) * z.n
    placed = placed[:count] + placed[count : 2 * count] + placed[2 * count :]
    energy = jnp.sum(squared[: z.conditions * per], axis=1, keepdims=True)
    energy = energy * (1.0 / z.voxels)
    tiles = [jnp.zeros((z.n, LANES), f32) for _ in range(z.lanes // LANES)]
    for index in range(z.conditions + 1):
        tile, lane = divmod(index * z.owned, LANES)
        value = placed[index * z.n : (index + 1) * z.n]
        tiles[tile] = tiles[tile] + pltpu.roll(value, lane, 1)
    lanes = iota((z.n, LANES), 1)
    for own in range(z.own_rows):
        for index in range(z.conditions):
            tile, lane = divmod(z.energy_lane + own * z.conditions + index, LANES)
            start = index * per + own * z.n
            value = energy[start : start + z.n]
            tiles[tile] = jnp.where(lanes == lane, value, tiles[tile])
    out_ref[...] = jnp.concatenate(tiles, axis=1)


def fourth_kernel(z, received_ref, energy_ref, scores_ref):
    tiles = [
        received_ref[:, start : start + LANES] for start in range(0, z.lanes, LANES)
    ]
    pieces = []
    for own in range(z.own_rows):
        tile, lane = divmod(z.energy_lane + own * z.conditions, LANES)
        assert lane + z.conditions <= LANES
        pieces.append(pltpu.roll(tiles[tile], (LANES - lane) % LANES, 1))
    turned = jnp.transpose(jnp.concatenate(pieces, axis=0))
    for index in range(z.conditions):
        energy_ref[index] = turned[index : index + 1, : z.rows]
    sums = [jnp.sum(tile, axis=0, keepdims=True) for tile in tiles]
    sums = [jnp.broadcast_to(tile, (8, LANES)) for tile in sums]
    lanes = iota((8, LANES), 1)
    tile, lane = divmod(z.conditions * z.owned, LANES)
    signal = pltpu.roll(sums[tile], (LANES - lane) % LANES, 1)
    signal = jnp.where(lanes < z.owned, signal, 0.0)
    square = (LANES, LANES)
    mean = (iota(square, 0) < z.owned) & (iota(square, 0) // VB == iota(square, 1))
    mean = jnp.where(mean, 1.0 / VB, 0.0).astype(bf16)
    rows = iota((8, LANES), 0)
    fit = jnp.zeros((8, LANES), f32)
    for index in range(z.conditions):
        tile, lane = divmod(index * z.owned, LANES)
        value = pltpu.roll(sums[tile], (LANES - lane) % LANES, 1)
        fit = jnp.where(rows == index, value, fit)
    fit = jnp.where(lanes < z.owned, fit, 0.0)
    fit = jnp.log((fit + EPSILON) / (signal + EPSILON))
    terms = jnp.concatenate([t.astype(f32) for t in thirds(fit)], axis=0).astype(bf16)
    score = dot(terms, mean)
    score = score[:8] + score[8:16] + score[16:]
    for index in range(z.conditions):
        scores_ref[index] = score[index : index + 1, :CAP]


def on_device(features, block_orders, offsets, tap_gains, weights, signal, block_owner):
    z = Sizes(features, block_orders, offsets, weights, block_owner)
    assert z.conditions <= 8
    weight = weights[0]
    owners = block_owner.reshape(1, z.blocks)
    others = [
        lax.ppermute(
            features,
            "subj",
            [((i + step) % z.subjects, i) for i in range(z.subjects)],
        )
        for step in range(1, z.subjects)
    ]
    term_lanes = -(-3 * z.rows // LANES) * LANES
    work = 2 * z.ext * z.width * z.voxels
    shapes = [
        jax.ShapeDtypeStruct((z.bands, z.ext, term_lanes), bf16),
        jax.ShapeDtypeStruct((z.residual_rows, z.slots_padded * z.n), bf16),
        jax.ShapeDtypeStruct((z.n, z.voxels), f32),
        jax.ShapeDtypeStruct((z.voxels, LANES), bf16),
        jax.ShapeDtypeStruct((z.ext, z.voxels), f32),
    ]
    table, choice, mine, place, total = pl.pallas_call(
        functools.partial(first_kernel, z),
        out_shape=shapes,
        in_specs=[VMEM, SMEM, SMEM, VMEM, VMEM, VMEM],
        out_specs=[VMEM] * 5,
        compiler_params=params(),
        cost_estimate=cost(work, 3 << 20),
        name="prepare_and_own_columns",
    )(block_orders, offsets, tap_gains, owners, features, weight)
    outgoing = pl.pallas_call(
        functools.partial(second_kernel, z),
        out_shape=jax.ShapeDtypeStruct((z.n * z.slots_padded, z.voxels), bf16),
        in_specs=[VMEM] * (4 + len(others)),
        out_specs=VMEM,
        compiler_params=params(),
        cost_estimate=cost(work, 2 << 20),
        name="other_columns",
    )(table, weight, total, signal, *others)
    received = lax.all_to_all(outgoing, "tr", 0, 0, tiled=True)
    outgoing = pl.pallas_call(
        functools.partial(third_kernel, z),
        out_shape=jax.ShapeDtypeStruct((z.n, z.lanes), f32),
        in_specs=[VMEM] * 4,
        out_specs=VMEM,
        compiler_params=params(),
        cost_estimate=cost(work, 1 << 20),
        name="residuals",
    )(choice, mine, place, received)
    received = lax.all_to_all(outgoing, "tr", 0, 0, tiled=True)
    energy, scores = pl.pallas_call(
        functools.partial(fourth_kernel, z),
        out_shape=[
            jax.ShapeDtypeStruct((z.conditions, 1, z.rows), f32),
            jax.ShapeDtypeStruct((z.conditions, 1, CAP), f32),
        ],
        in_specs=[VMEM],
        out_specs=[VMEM, VMEM],
        compiler_params=params(),
        cost_estimate=cost(1 << 20, 1 << 16),
        name="scores",
    )(received)
    return energy.transpose(1, 2, 0), scores.transpose(1, 2, 0)


def solution(mesh):
    placed = (
        P("tr", "subj"),
        P(),
        P(),
        P(),
        P("subj", None, None),
        P("subj", "tr", None),
        P("subj", None, None),
    )
    return jax.shard_map(
        on_device,
        mesh=mesh,
        in_specs=placed,
        out_specs=(P("subj", "tr", None), P("subj", "tr", None)),
        check_vma=False,
    )
```

```python
import functools

import jax
import jax.numpy as jnp
from jax import lax
from jax.experimental import pallas as pl
from jax.experimental.pallas import tpu as pltpu
from jax.sharding import PartitionSpec as P

MAXLAG = 8
VB = 4
CAP = 8
LANES = 128
EPSILON = 1e-6

f32 = jnp.float32
bf16 = jnp.bfloat16
i32 = jnp.int32

VMEM = pl.BlockSpec(memory_space=pltpu.VMEM)
HBM = pl.BlockSpec(memory_space=pltpu.HBM)


def iota(shape, axis):
    return lax.broadcasted_iota(i32, shape, axis)


def dot(a, b):
    return jnp.dot(a, b, preferred_element_type=f32)


def thirds(x):
    first = x.astype(bf16)
    rest = x - first.astype(f32)
    second = rest.astype(bf16)
    return first, second, (rest - second.astype(f32)).astype(bf16)


def params(**more):
    return pltpu.CompilerParams(vmem_limit_bytes=48 * 1024 * 1024, **more)


def cost(flops, nbytes):
    return pl.CostEstimate(flops=flops, bytes_accessed=nbytes, transcendentals=0)


class Sizes:
    def __init__(self, features, block_orders, offsets, weights, block_owner):
        self.subjects = lax.axis_size("subj")
        self.n = lax.axis_size("tr")
        self.rows, self.width = features.shape
        self.columns, self.voxels = weights.shape[1:]
        self.bands, self.taps = offsets.shape
        self.band_width = self.columns // self.bands
        self.piece = min(self.width, self.band_width)
        self.conditions = block_orders.shape[0] + 1
        self.blocks = block_owner.shape[1]
        self.own_rows = self.rows // self.n
        self.own_ext = self.own_rows + 1
        self.ext = self.own_ext * self.n
        self.slots = 2 * self.own_ext + self.own_rows
        self.slots_padded = -(-self.slots // 16) * 16
        self.residual_rows = (self.conditions + 1) * self.own_rows * self.n
        self.owned = CAP * VB
        self.energy_lane = (self.conditions + 1) * self.owned
        used = self.energy_lane + self.conditions * self.own_rows
        self.lanes = -(-used // LANES) * LANES
        assert self.rows % self.n == 0 and self.n >= MAXLAG


def filtered_product(z, x_ref, w_ref, table_ref, source):
    total = jnp.zeros((z.ext, z.voxels), f32)
    for part in range(z.width // z.piece):
        columns = slice(part * z.piece, (part + 1) * z.piece)
        x = x_ref[:, columns]
        table = table_ref[lax.div(source * z.width + part * z.piece, z.band_width)]
        stacked = jnp.concatenate([x] * (table.shape[1] // z.rows), axis=0)
        filtered = dot(table, stacked)
        high = filtered.astype(bf16)
        low = filtered - high.astype(f32)
        tail = z.rows + MAXLAG
        edges = [filtered, low[:MAXLAG], low[z.rows : tail]]
        edges = jnp.concatenate(edges, axis=0).astype(bf16)
        product = dot(edges, w_ref[columns, :])
        total = total + product[: z.ext]
        head = product[z.ext : z.ext + MAXLAG]
        rim = product[z.ext + MAXLAG :]
        parts = [head, jnp.zeros((z.rows - MAXLAG, z.voxels), f32), rim]
        if z.ext > tail:
            parts.append(jnp.zeros((z.ext - tail, z.voxels), f32))
        total = total + jnp.concatenate(parts, axis=0)
    return total


def fill_table(z, offsets_ref, gains_ref, table_ref):
    lanes = table_ref.shape[2]
    column = iota((z.ext, lanes), 1)
    lag = iota((z.ext, lanes), 0) - column % z.rows
    term = column // z.rows
    for band in range(z.bands):
        value = jnp.zeros((z.ext, lanes), f32)
        for tap in range(z.taps):
            hit = lag == offsets_ref[band, tap]
            value = value + jnp.where(hit, gains_ref[band, tap], 0.0)
        first, second, third = (t.astype(f32) for t in thirds(value))
        chosen = jnp.where(term == 0, first, jnp.where(term == 1, second, third))
        chosen = jnp.where(term > 2, 0.0, chosen)
        table_ref[band] = chosen.astype(bf16)


def fill_choice(z, orders_ref, choice_ref):
    shape = (z.residual_rows, z.slots_padded * z.n)
    per = z.own_rows * z.n
    permutations = z.conditions - 1
    row = iota((z.residual_rows, 1), 0)
    condition = row // per
    own = (row % per) // z.n
    position = row % z.n
    which = iota((z.residual_rows, permutations), 1)
    wanted = (which == condition - 1).astype(f32).astype(bf16)
    orders = dot(wanted, orders_ref[...].astype(f32).astype(bf16))
    place = iota((z.residual_rows, z.n), 1)
    here = jnp.sum(jnp.where(place == position, orders, 0.0), axis=1, keepdims=True)
    ahead = jnp.where(place == position - 1, orders, 0.0)
    ahead = jnp.sum(ahead, axis=1, keepdims=True)
    observed = condition == 0
    here = jnp.where(observed, position, here.astype(i32))
    ahead = jnp.where(observed, position - 1, ahead.astype(i32))
    ahead = jnp.where((position == 0) | (own > 0), -1, ahead)
    signal_only = condition == z.conditions
    here = jnp.where(signal_only, -1, here)
    ahead = jnp.where(signal_only, -1, ahead)
    column = iota(shape, 1)
    source = column // z.slots_padded
    slot = column % z.slots_padded
    half = jnp.where(slot >= z.own_ext, slot - z.own_ext, slot)
    predicted = (source == here) & (half == own) & (slot < 2 * z.own_ext)
    rim = (source == ahead) & (half == z.own_rows) & (slot < 2 * z.own_ext)
    measured = (source == position) & (slot == 2 * z.own_ext + own)
    value = jnp.where(measured, 1.0, jnp.where(predicted | rim, -1.0, 0.0))
    choice_ref[...] = value.astype(bf16)


def fill_owners(z, owners_ref, mine_ref, place_ref):
    owners = owners_ref[...]
    other = iota((z.voxels, z.blocks), 1)
    block = iota((z.voxels, 1), 0) // VB
    owner = jnp.sum(jnp.where(other == block, owners, 0), axis=1, keepdims=True)
    before = (owners == owner) & (other < block)
    rank = jnp.sum(before.astype(i32), axis=1, keepdims=True)
    lane = rank * VB + iota((z.voxels, 1), 0) % VB
    place = iota((z.voxels, LANES), 1) == lane
    place_ref[...] = place.astype(f32).astype(bf16)
    square = (z.blocks, z.blocks)
    diagonal = iota(square, 0) == iota(square, 1)
    down = jnp.sum(jnp.where(diagonal, owners, 0), axis=1, keepdims=True)
    shape = (z.blocks, z.voxels)
    held = iota(shape, 0) == iota(shape, 1) // VB
    along = jnp.sum(jnp.where(held, down, 0), axis=0, keepdims=True)
    mine_ref[...] = (iota((z.n, z.voxels), 0) == along).astype(f32)


def first_kernel(
    z, orders_hbm, offsets_hbm, gains_hbm, owners_hbm, x_hbm, w_hbm, signal_hbm,
    table_ref, choice_ref, mine_ref, place_ref, total_ref, rest_ref, signal_ref,
    orders_ref, offsets_ref, gains_ref, owners_ref, x_ref, w_ref, sems,
):
    me = lax.axis_index("subj")

    def weight_rows(step):
        source = lax.rem(me + step, z.subjects)
        start = pl.multiple_of(source * z.width, z.width)
        return w_hbm.at[pl.ds(start, z.width), :]

    moves = [
        (offsets_hbm, offsets_ref),
        (gains_hbm, gains_ref),
        (x_hbm, x_ref),
        (weight_rows(0), w_ref),
        (orders_hbm, orders_ref),
        (owners_hbm, owners_ref),
        (signal_hbm, signal_ref),
    ]
    for step in range(1, z.subjects):
        rows = pl.ds((step - 1) * z.width, z.width)
        moves.append((weight_rows(step), rest_ref.at[rows, :]))
    copies = [
        pltpu.make_async_copy(origin, target, sems.at[index])
        for index, (origin, target) in enumerate(moves)
    ]
    for copy in copies:
        copy.start()
    copies[0].wait()
    copies[1].wait()
    fill_table(z, offsets_ref, gains_ref, table_ref)
    copies[2].wait()
    copies[3].wait()
    total_ref[...] = filtered_product(z, x_ref, w_ref, table_ref, me)
    copies[4].wait()
    fill_choice(z, orders_ref, choice_ref)
    copies[5].wait()
    fill_owners(z, owners_ref, mine_ref, place_ref)
    for copy in copies[6:]:
        copy.wait()


def second_kernel(z, table_ref, w_ref, total_ref, signal_ref, *refs):
    others, out_ref = refs[:-1], refs[-1]
    me = lax.axis_index("subj")
    total = total_ref[...]
    for step, x_ref in enumerate(others):
        source = lax.rem(me + step + 1, z.subjects)
        rows = w_ref.at[step * z.width : (step + 1) * z.width, :]
        total = total + filtered_product(z, x_ref, rows, table_ref, source)
    high = total.astype(bf16)
    low = total - high.astype(f32)
    stacked = jnp.concatenate([total, low, signal_ref[...].astype(f32)], axis=0)
    stacked = stacked.astype(bf16)
    shape = (z.n * z.slots_padded, z.slots * z.n)
    row = iota(shape, 0)
    column = (row % z.slots_padded) * z.n + row // z.slots_padded
    hit = (iota(shape, 1) == column) & (row % z.slots_padded < z.slots)
    order = hit.astype(f32).astype(bf16)
    out_ref[...] = dot(order, stacked).astype(bf16)


def third_kernel(z, choice_ref, mine_ref, place_ref, received_ref, out_ref):
    residual = dot(choice_ref[...], received_ref[...])
    squared = residual * residual
    per = z.own_rows * z.n
    spread = []
    for index in range(z.conditions + 1):
        stat = jnp.sum(squared[index * per : (index + 1) * per], axis=0, keepdims=True)
        spread.append(stat * mine_ref[...])
    spread = jnp.concatenate(spread, axis=0)
    terms = jnp.concatenate(thirds(spread), axis=0)
    placed = dot(terms, place_ref[...])
    count = (z.conditions + 1) * z.n
    placed = placed[:count] + placed[count : 2 * count] + placed[2 * count :]
    energy = jnp.sum(squared[: z.conditions * per], axis=1, keepdims=True)
    energy = energy * (1.0 / z.voxels)
    tiles = [jnp.zeros((z.n, LANES), f32) for _ in range(z.lanes // LANES)]
    for index in range(z.conditions + 1):
        tile, lane = divmod(index * z.owned, LANES)
        value = placed[index * z.n : (index + 1) * z.n]
        tiles[tile] = tiles[tile] + pltpu.roll(value, lane, 1)
    lanes = iota((z.n, LANES), 1)
    for own in range(z.own_rows):
        for index in range(z.conditions):
            tile, lane = divmod(z.energy_lane + own * z.conditions + index, LANES)
            start = index * per + own * z.n
            value = energy[start : start + z.n]
            tiles[tile] = jnp.where(lanes == lane, value, tiles[tile])
    out_ref[...] = jnp.concatenate(tiles, axis=1)


def fourth_kernel(z, received_ref, energy_ref, scores_ref):
    tiles = [
        received_ref[:, start : start + LANES] for start in range(0, z.lanes, LANES)
    ]
    pieces = []
    for own in range(z.own_rows):
        tile, lane = divmod(z.energy_lane + own * z.conditions, LANES)
        assert lane + z.conditions <= LANES
        pieces.append(pltpu.roll(tiles[tile], (LANES - lane) % LANES, 1))
    turned = jnp.transpose(jnp.concatenate(pieces, axis=0))
    for index in range(z.conditions):
        energy_ref[index] = turned[index : index + 1, : z.rows]
    sums = [jnp.sum(tile, axis=0, keepdims=True) for tile in tiles]
    sums = [jnp.broadcast_to(tile, (8, LANES)) for tile in sums]
    lanes = iota((8, LANES), 1)
    tile, lane = divmod(z.conditions * z.owned, LANES)
    signal = pltpu.roll(sums[tile], (LANES - lane) % LANES, 1)
    signal = jnp.where(lanes < z.owned, signal, 0.0)
    square = (LANES, LANES)
    mean = (iota(square, 0) < z.owned) & (iota(square, 0) // VB == iota(square, 1))
    mean = jnp.where(mean, 1.0 / VB, 0.0).astype(bf16)
    rows = iota((8, LANES), 0)
    fit = jnp.zeros((8, LANES), f32)
    for index in range(z.conditions):
        tile, lane = divmod(index * z.owned, LANES)
        value = pltpu.roll(sums[tile], (LANES - lane) % LANES, 1)
        fit = jnp.where(rows == index, value, fit)
    fit = jnp.where(lanes < z.owned, fit, 0.0)
    fit = jnp.log((fit + EPSILON) / (signal + EPSILON))
    terms = jnp.concatenate([t.astype(f32) for t in thirds(fit)], axis=0).astype(bf16)
    score = dot(terms, mean)
    score = score[:8] + score[8:16] + score[16:]
    for index in range(z.conditions):
        scores_ref[index] = score[index : index + 1, :CAP]


def on_device(features, block_orders, offsets, tap_gains, weights, signal, block_owner):
    z = Sizes(features, block_orders, offsets, weights, block_owner)
    assert z.conditions <= 8
    weight = weights[0]
    owners = block_owner.reshape(1, z.blocks)
    others = [
        lax.ppermute(
            features,
            "subj",
            [((i + step) % z.subjects, i) for i in range(z.subjects)],
        )
        for step in range(1, z.subjects)
    ]
    term_lanes = -(-3 * z.rows // LANES) * LANES
    work = 2 * z.ext * z.width * z.voxels
    shapes = [
        jax.ShapeDtypeStruct((z.bands, z.ext, term_lanes), bf16),
        jax.ShapeDtypeStruct((z.residual_rows, z.slots_padded * z.n), bf16),
        jax.ShapeDtypeStruct((z.n, z.voxels), f32),
        jax.ShapeDtypeStruct((z.voxels, LANES), bf16),
        jax.ShapeDtypeStruct((z.ext, z.voxels), f32),
        jax.ShapeDtypeStruct((z.columns - z.width, z.voxels), bf16),
        jax.ShapeDtypeStruct((z.rows, z.voxels), bf16),
    ]
    scratch = [
        pltpu.VMEM(block_orders.shape, i32),
        pltpu.SMEM(offsets.shape, i32),
        pltpu.SMEM(tap_gains.shape, f32),
        pltpu.VMEM(owners.shape, i32),
        pltpu.VMEM(features.shape, bf16),
        pltpu.VMEM((z.width, z.voxels), bf16),
        pltpu.SemaphoreType.DMA((6 + z.subjects,)),
    ]
    table, choice, mine, place, total, rest, signal = pl.pallas_call(
        functools.partial(first_kernel, z),
        out_shape=shapes,
        in_specs=[HBM] * 7,
        out_specs=[VMEM] * 7,
        scratch_shapes=scratch,
        compiler_params=params(),
        cost_estimate=cost(work, 3 << 20),
        name="prepare_and_own_columns",
    )(block_orders, offsets, tap_gains, owners, features, weight, signal[0])
    outgoing = pl.pallas_call(
        functools.partial(second_kernel, z),
        out_shape=jax.ShapeDtypeStruct((z.n * z.slots_padded, z.voxels), bf16),
        in_specs=[VMEM] * (4 + len(others)),
        out_specs=VMEM,
        compiler_params=params(),
        cost_estimate=cost(work, 2 << 20),
        name="other_columns",
    )(table, rest, total, signal, *others)
    received = lax.all_to_all(outgoing, "tr", 0, 0, tiled=True)
    outgoing = pl.pallas_call(
        functools.partial(third_kernel, z),
        out_shape=jax.ShapeDtypeStruct((z.n, z.lanes), f32),
        in_specs=[VMEM] * 4,
        out_specs=VMEM,
        compiler_params=params(),
        cost_estimate=cost(work, 1 << 20),
        name="residuals",
    )(choice, mine, place, received)
    received = lax.all_to_all(outgoing, "tr", 0, 0, tiled=True)
    energy, scores = pl.pallas_call(
        functools.partial(fourth_kernel, z),
        out_shape=[
            jax.ShapeDtypeStruct((z.conditions, 1, z.rows), f32),
            jax.ShapeDtypeStruct((z.conditions, 1, CAP), f32),
        ],
        in_specs=[VMEM],
        out_specs=[VMEM, VMEM],
        compiler_params=params(),
        cost_estimate=cost(1 << 20, 1 << 16),
        name="scores",
    )(received)
    return energy.transpose(1, 2, 0), scores.transpose(1, 2, 0)


def solution(mesh):
    placed = (
        P("tr", "subj"),
        P(),
        P(),
        P(),
        P("subj", None, None),
        P("subj", "tr", None),
        P("subj", None, None),
    )
    return jax.shard_map(
        on_device,
        mesh=mesh,
        in_specs=placed,
        out_specs=(P("subj", "tr", None), P("subj", "tr", None)),
        check_vma=False,
    )
```

```python
import functools

import jax
import jax.numpy as jnp
from jax import lax
from jax.experimental import pallas as pl
from jax.experimental.pallas import tpu as pltpu
from jax.sharding import PartitionSpec as P

MAXLAG = 8
VB = 4
CAP = 8
LANES = 128
EPSILON = 1e-6

f32 = jnp.float32
bf16 = jnp.bfloat16
i32 = jnp.int32

VMEM = pl.BlockSpec(memory_space=pltpu.VMEM)
HBM = pl.BlockSpec(memory_space=pltpu.HBM)


def iota(shape, axis):
    return lax.broadcasted_iota(i32, shape, axis)


def dot(a, b):
    return jnp.dot(a, b, preferred_element_type=f32)


def thirds(x):
    first = x.astype(bf16)
    rest = x - first.astype(f32)
    second = rest.astype(bf16)
    return first, second, (rest - second.astype(f32)).astype(bf16)


def params(**more):
    return pltpu.CompilerParams(vmem_limit_bytes=48 * 1024 * 1024, **more)


def cost(flops, nbytes):
    return pl.CostEstimate(flops=flops, bytes_accessed=nbytes, transcendentals=0)


class Sizes:
    def __init__(self, features, block_orders, offsets, weights, block_owner):
        self.subjects = lax.axis_size("subj")
        self.n = lax.axis_size("tr")
        self.rows, self.width = features.shape
        self.columns, self.voxels = weights.shape[1:]
        self.bands, self.taps = offsets.shape
        self.band_width = self.columns // self.bands
        self.piece = min(self.width, self.band_width)
        self.conditions = block_orders.shape[0] + 1
        self.blocks = block_owner.shape[1]
        self.own_rows = self.rows // self.n
        self.own_ext = self.own_rows + 1
        self.ext = self.own_ext * self.n
        self.slots = 2 * self.own_ext + self.own_rows
        self.slots_padded = -(-self.slots // 16) * 16
        self.residual_rows = (self.conditions + 1) * self.own_rows * self.n
        self.owned = CAP * VB
        self.energy_lane = (self.conditions + 1) * self.owned
        used = self.energy_lane + self.conditions * self.own_rows
        self.lanes = -(-used // LANES) * LANES
        assert self.rows % self.n == 0 and self.n >= MAXLAG


def filtered_product(z, x_ref, w_ref, table_ref, source):
    total = jnp.zeros((z.ext, z.voxels), f32)
    for part in range(z.width // z.piece):
        columns = slice(part * z.piece, (part + 1) * z.piece)
        x = x_ref[:, columns]
        table = table_ref[lax.div(source * z.width + part * z.piece, z.band_width)]
        stacked = jnp.concatenate([x] * (table.shape[1] // z.rows), axis=0)
        filtered = dot(table, stacked)
        high = filtered.astype(bf16)
        low = filtered - high.astype(f32)
        tail = z.rows + MAXLAG
        edges = [filtered, low[:MAXLAG], low[z.rows : tail]]
        edges = jnp.concatenate(edges, axis=0).astype(bf16)
        product = dot(edges, w_ref[columns, :])
        total = total + product[: z.ext]
        head = product[z.ext : z.ext + MAXLAG]
        rim = product[z.ext + MAXLAG :]
        parts = [head, jnp.zeros((z.rows - MAXLAG, z.voxels), f32), rim]
        if z.ext > tail:
            parts.append(jnp.zeros((z.ext - tail, z.voxels), f32))
        total = total + jnp.concatenate(parts, axis=0)
    return total


def fill_table(z, offsets_ref, gains_ref, table_ref):
    lanes = table_ref.shape[2]
    column = iota((z.ext, lanes), 1)
    lag = iota((z.ext, lanes), 0) - column % z.rows
    term = column // z.rows
    for band in range(z.bands):
        value = jnp.zeros((z.ext, lanes), f32)
        for tap in range(z.taps):
            hit = lag == offsets_ref[band, tap]
            value = value + jnp.where(hit, gains_ref[band, tap], 0.0)
        first, second, third = (t.astype(f32) for t in thirds(value))
        chosen = jnp.where(term == 0, first, jnp.where(term == 1, second, third))
        chosen = jnp.where(term > 2, 0.0, chosen)
        table_ref[band] = chosen.astype(bf16)


def fill_choice(z, orders_ref, choice_ref):
    shape = (z.residual_rows, z.slots_padded * z.n)
    per = z.own_rows * z.n
    permutations = z.conditions - 1
    row = iota((z.residual_rows, 1), 0)
    condition = row // per
    own = (row % per) // z.n
    position = row % z.n
    which = iota((z.residual_rows, permutations), 1)
    wanted = (which == condition - 1).astype(f32).astype(bf16)
    orders = dot(wanted, orders_ref[...].astype(f32).astype(bf16))
    place = iota((z.residual_rows, z.n), 1)
    here = jnp.sum(jnp.where(place == position, orders, 0.0), axis=1, keepdims=True)
    ahead = jnp.where(place == position - 1, orders, 0.0)
    ahead = jnp.sum(ahead, axis=1, keepdims=True)
    observed = condition == 0
    here = jnp.where(observed, position, here.astype(i32))
    ahead = jnp.where(observed, position - 1, ahead.astype(i32))
    ahead = jnp.where((position == 0) | (own > 0), -1, ahead)
    signal_only = condition == z.conditions
    here = jnp.where(signal_only, -1, here)
    ahead = jnp.where(signal_only, -1, ahead)
    column = iota(shape, 1)
    source = column // z.slots_padded
    slot = column % z.slots_padded
    half = jnp.where(slot >= z.own_ext, slot - z.own_ext, slot)
    predicted = (source == here) & (half == own) & (slot < 2 * z.own_ext)
    rim = (source == ahead) & (half == z.own_rows) & (slot < 2 * z.own_ext)
    measured = (source == position) & (slot == 2 * z.own_ext + own)
    value = jnp.where(measured, 1.0, jnp.where(predicted | rim, -1.0, 0.0))
    choice_ref[...] = value.astype(bf16)


def fill_owners(z, owners_ref, mine_ref, place_ref):
    owners = owners_ref[...]
    other = iota((z.voxels, z.blocks), 1)
    block = iota((z.voxels, 1), 0) // VB
    owner = jnp.sum(jnp.where(other == block, owners, 0), axis=1, keepdims=True)
    before = (owners == owner) & (other < block)
    rank = jnp.sum(before.astype(i32), axis=1, keepdims=True)
    lane = rank * VB + iota((z.voxels, 1), 0) % VB
    place = iota((z.voxels, LANES), 1) == lane
    place_ref[...] = place.astype(f32).astype(bf16)
    square = (z.blocks, z.blocks)
    diagonal = iota(square, 0) == iota(square, 1)
    down = jnp.sum(jnp.where(diagonal, owners, 0), axis=1, keepdims=True)
    shape = (z.blocks, z.voxels)
    held = iota(shape, 0) == iota(shape, 1) // VB
    along = jnp.sum(jnp.where(held, down, 0), axis=0, keepdims=True)
    mine_ref[...] = (iota((z.n, z.voxels), 0) == along).astype(f32)


def first_kernel(
    z, orders_hbm, offsets_hbm, gains_hbm, owners_hbm, x_hbm, w_hbm, signal_hbm,
    table_ref, choice_ref, mine_ref, place_ref, total_ref, rest_ref, signal_ref,
    orders_ref, offsets_ref, gains_ref, owners_ref, x_ref, w_ref, sems,
):
    me = lax.axis_index("subj")

    def weight_rows(step):
        source = lax.rem(me + step, z.subjects)
        start = pl.multiple_of(source * z.width, z.width)
        return w_hbm.at[pl.ds(start, z.width), :]

    moves = [
        (offsets_hbm, offsets_ref),
        (gains_hbm, gains_ref),
        (x_hbm, x_ref),
        (weight_rows(0), w_ref),
        (orders_hbm, orders_ref),
        (owners_hbm, owners_ref),
        (signal_hbm, signal_ref),
    ]
    for step in range(1, z.subjects):
        rows = pl.ds((step - 1) * z.width, z.width)
        moves.append((weight_rows(step), rest_ref.at[rows, :]))
    copies = [
        pltpu.make_async_copy(origin, target, sems.at[index])
        for index, (origin, target) in enumerate(moves)
    ]
    for copy in copies:
        copy.start()
    copies[0].wait()
    copies[1].wait()
    fill_table(z, offsets_ref, gains_ref, table_ref)
    copies[2].wait()
    copies[3].wait()
    total_ref[...] = filtered_product(z, x_ref, w_ref, table_ref, me)
    copies[4].wait()
    fill_choice(z, orders_ref, choice_ref)
    copies[5].wait()
    fill_owners(z, owners_ref, mine_ref, place_ref)
    for copy in copies[6:]:
        copy.wait()


def second_kernel(z, table_ref, w_ref, total_ref, signal_ref, *refs):
    others, out_ref = refs[:-1], refs[-1]
    me = lax.axis_index("subj")
    total = total_ref[...]
    for step, x_ref in enumerate(others):
        source = lax.rem(me + step + 1, z.subjects)
        rows = w_ref.at[step * z.width : (step + 1) * z.width, :]
        total = total + filtered_product(z, x_ref, rows, table_ref, source)
    high = total.astype(bf16)
    low = total - high.astype(f32)
    stacked = jnp.concatenate([total, low, signal_ref[...].astype(f32)], axis=0)
    stacked = stacked.astype(bf16)
    shape = (z.n * z.slots_padded, z.slots * z.n)
    row = iota(shape, 0)
    column = (row % z.slots_padded) * z.n + row // z.slots_padded
    hit = (iota(shape, 1) == column) & (row % z.slots_padded < z.slots)
    order = hit.astype(f32).astype(bf16)
    out_ref[...] = dot(order, stacked).astype(bf16)


def third_kernel(z, choice_ref, mine_ref, place_ref, received_ref, out_ref):
    residual = dot(choice_ref[...], received_ref[...])
    squared = residual * residual
    per = z.own_rows * z.n
    spread = []
    for index in range(z.conditions + 1):
        stat = jnp.sum(squared[index * per : (index + 1) * per], axis=0, keepdims=True)
        spread.append(stat * mine_ref[...])
    spread = jnp.concatenate(spread, axis=0)
    terms = jnp.concatenate(thirds(spread), axis=0)
    placed = dot(terms, place_ref[...])
    count = (z.conditions + 1) * z.n
    placed = placed[:count] + placed[count : 2 * count] + placed[2 * count :]
    energy = jnp.sum(squared[: z.conditions * per], axis=1, keepdims=True)
    energy = energy * (1.0 / z.voxels)
    tiles = [jnp.zeros((z.n, LANES), f32) for _ in range(z.lanes // LANES)]
    for index in range(z.conditions + 1):
        tile, lane = divmod(index * z.owned, LANES)
        value = placed[index * z.n : (index + 1) * z.n]
        tiles[tile] = tiles[tile] + pltpu.roll(value, lane, 1)
    lanes = iota((z.n, LANES), 1)
    for own in range(z.own_rows):
        for index in range(z.conditions):
            tile, lane = divmod(z.energy_lane + own * z.conditions + index, LANES)
            start = index * per + own * z.n
            value = energy[start : start + z.n]
            tiles[tile] = jnp.where(lanes == lane, value, tiles[tile])
    out_ref[...] = jnp.concatenate(tiles, axis=1)


def fourth_kernel(z, received_ref, energy_ref, scores_ref):
    tiles = [
        received_ref[:, start : start + LANES] for start in range(0, z.lanes, LANES)
    ]
    pieces = []
    for own in range(z.own_rows):
        tile, lane = divmod(z.energy_lane + own * z.conditions, LANES)
        assert lane + z.conditions <= LANES
        pieces.append(pltpu.roll(tiles[tile], (LANES - lane) % LANES, 1))
    turned = jnp.transpose(jnp.concatenate(pieces, axis=0))
    for index in range(z.conditions):
        energy_ref[index] = turned[index : index + 1, : z.rows]
    sums = [jnp.sum(tile, axis=0, keepdims=True) for tile in tiles]
    sums = [jnp.broadcast_to(tile, (8, LANES)) for tile in sums]
    lanes = iota((8, LANES), 1)
    tile, lane = divmod(z.conditions * z.owned, LANES)
    signal = pltpu.roll(sums[tile], (LANES - lane) % LANES, 1)
    signal = jnp.where(lanes < z.owned, signal, 0.0)
    square = (LANES, LANES)
    mean = (iota(square, 0) < z.owned) & (iota(square, 0) // VB == iota(square, 1))
    mean = jnp.where(mean, 1.0 / VB, 0.0).astype(bf16)
    rows = iota((8, LANES), 0)
    fit = jnp.zeros((8, LANES), f32)
    for index in range(z.conditions):
        tile, lane = divmod(index * z.owned, LANES)
        value = pltpu.roll(sums[tile], (LANES - lane) % LANES, 1)
        fit = jnp.where(rows == index, value, fit)
    fit = jnp.where(lanes < z.owned, fit, 0.0)
    fit = jnp.log((fit + EPSILON) / (signal + EPSILON))
    terms = jnp.concatenate([t.astype(f32) for t in thirds(fit)], axis=0).astype(bf16)
    score = dot(terms, mean)
    score = score[:8] + score[8:16] + score[16:]
    for index in range(z.conditions):
        scores_ref[index] = score[index : index + 1, :CAP]


def on_device(features, block_orders, offsets, tap_gains, weights, signal, block_owner):
    z = Sizes(features, block_orders, offsets, weights, block_owner)
    assert z.conditions <= 8
    weight = weights[0]
    owners = block_owner.reshape(1, z.blocks)
    others = [
        lax.ppermute(
            features,
            "subj",
            [((i + step) % z.subjects, i) for i in range(z.subjects)],
        )
        for step in range(1, z.subjects)
    ]
    term_lanes = -(-3 * z.rows // LANES) * LANES
    work = 2 * z.ext * z.width * z.voxels
    shapes = [
        jax.ShapeDtypeStruct((z.bands, z.ext, term_lanes), bf16),
        jax.ShapeDtypeStruct((z.residual_rows, z.slots_padded * z.n), bf16),
        jax.ShapeDtypeStruct((z.n, z.voxels), f32),
        jax.ShapeDtypeStruct((z.voxels, LANES), bf16),
        jax.ShapeDtypeStruct((z.ext, z.voxels), f32),
        jax.ShapeDtypeStruct((z.columns - z.width, z.voxels), bf16),
        jax.ShapeDtypeStruct((z.rows, z.voxels), bf16),
    ]
    scratch = [
        pltpu.VMEM(block_orders.shape, i32),
        pltpu.SMEM(offsets.shape, i32),
        pltpu.SMEM(tap_gains.shape, f32),
        pltpu.VMEM(owners.shape, i32),
        pltpu.VMEM(features.shape, bf16),
        pltpu.VMEM((z.width, z.voxels), bf16),
        pltpu.SemaphoreType.DMA((6 + z.subjects,)),
    ]
    operands = (block_orders, offsets, tap_gains, owners, features, weight, signal[0])
    operands = [pltpu.with_memory_space_constraint(x, pltpu.HBM) for x in operands]
    table, choice, mine, place, total, rest, signal = pl.pallas_call(
        functools.partial(first_kernel, z),
        out_shape=shapes,
        in_specs=[HBM] * 7,
        out_specs=[VMEM] * 7,
        scratch_shapes=scratch,
        compiler_params=params(),
        cost_estimate=cost(work, 3 << 20),
        name="prepare_and_own_columns",
    )(*operands)
    outgoing = pl.pallas_call(
        functools.partial(second_kernel, z),
        out_shape=jax.ShapeDtypeStruct((z.n * z.slots_padded, z.voxels), bf16),
        in_specs=[VMEM] * (4 + len(others)),
        out_specs=VMEM,
        compiler_params=params(),
        cost_estimate=cost(work, 2 << 20),
        name="other_columns",
    )(table, rest, total, signal, *others)
    received = lax.all_to_all(outgoing, "tr", 0, 0, tiled=True)
    outgoing = pl.pallas_call(
        functools.partial(third_kernel, z),
        out_shape=jax.ShapeDtypeStruct((z.n, z.lanes), f32),
        in_specs=[VMEM] * 4,
        out_specs=VMEM,
        compiler_params=params(),
        cost_estimate=cost(work, 1 << 20),
        name="residuals",
    )(choice, mine, place, received)
    received = lax.all_to_all(outgoing, "tr", 0, 0, tiled=True)
    energy, scores = pl.pallas_call(
        functools.partial(fourth_kernel, z),
        out_shape=[
            jax.ShapeDtypeStruct((z.conditions, 1, z.rows), f32),
            jax.ShapeDtypeStruct((z.conditions, 1, CAP), f32),
        ],
        in_specs=[VMEM],
        out_specs=[VMEM, VMEM],
        compiler_params=params(),
        cost_estimate=cost(1 << 20, 1 << 16),
        name="scores",
    )(received)
    return energy.transpose(1, 2, 0), scores.transpose(1, 2, 0)


def solution(mesh):
    placed = (
        P("tr", "subj"),
        P(),
        P(),
        P(),
        P("subj", None, None),
        P("subj", "tr", None),
        P("subj", None, None),
    )
    return jax.shard_map(
        on_device,
        mesh=mesh,
        in_specs=placed,
        out_specs=(P("subj", "tr", None), P("subj", "tr", None)),
        check_vma=False,
    )
```

```python
import functools

import jax
import jax.numpy as jnp
from jax import lax
from jax.experimental import pallas as pl
from jax.experimental.pallas import tpu as pltpu
from jax.sharding import PartitionSpec as P

MAXLAG = 8
VB = 4
CAP = 8
LANES = 128
GROUP = 4
EPSILON = 1e-6

f32 = jnp.float32
bf16 = jnp.bfloat16
i32 = jnp.int32

VMEM = pl.BlockSpec(memory_space=pltpu.VMEM)
SMEM = pl.BlockSpec(memory_space=pltpu.SMEM)
HBM = pl.BlockSpec(memory_space=pltpu.HBM)


def iota(shape, axis):
    return lax.broadcasted_iota(i32, shape, axis)


def dot(a, b):
    return jnp.dot(a, b, preferred_element_type=f32)


def thirds(x):
    first = x.astype(bf16)
    rest = x - first.astype(f32)
    second = rest.astype(bf16)
    return first, second, (rest - second.astype(f32)).astype(bf16)


def params(**more):
    return pltpu.CompilerParams(vmem_limit_bytes=48 * 1024 * 1024, **more)


def cost(flops, nbytes):
    return pl.CostEstimate(flops=flops, bytes_accessed=nbytes, transcendentals=0)


class Sizes:
    def __init__(self, features, block_orders, offsets, weights, block_owner):
        self.subjects = lax.axis_size("subj")
        self.n = lax.axis_size("tr")
        self.rows, self.width = features.shape
        self.columns, self.voxels = weights.shape[1:]
        self.bands, self.taps = offsets.shape
        self.band_width = self.columns // self.bands
        self.piece = min(self.width, self.band_width)
        self.conditions = block_orders.shape[0] + 1
        self.blocks = block_owner.shape[1]
        self.ext = self.rows + MAXLAG
        self.own = self.rows // GROUP
        self.own_tail = MAXLAG // GROUP
        self.tiles = self.voxels // LANES
        self.signal_at = self.tiles * self.own
        self.tail_at = 2 * self.signal_at
        self.scale_at = self.tail_at + self.tiles * self.own_tail
        self.signal_scale_at = self.scale_at + self.tiles
        self.message = -(-(self.signal_scale_at + self.tiles) // 8) * 8
        assert self.n % GROUP == 0 and self.own % 8 == 0 and self.conditions < 8
        assert self.own_tail <= 8 and CAP * VB <= LANES


def coded(x):
    largest = jnp.max(jnp.abs(x), axis=0, keepdims=True)
    power = jnp.floor(jnp.log2(jnp.maximum(largest, 2.0**-100))) + 1.0
    value = jnp.round(x * jnp.exp2(15.0 - power))
    return jnp.clip(value, -32767.0, 32767.0), power


def arranged(z, x, order):
    value, power = coded(x)
    upper = jnp.floor(value * (1.0 / 256.0))
    lower = value - 256.0 * upper
    powers = jnp.broadcast_to(power, (8, z.voxels))
    high, low = [], []
    for tile in range(z.tiles):
        lanes = slice(tile * LANES, (tile + 1) * LANES)
        high += [upper[:, lanes], jnp.zeros((8, LANES), f32)]
        low += [lower[:, lanes], powers[:, lanes]]
    high = jnp.concatenate(high, axis=0).astype(bf16)
    low = jnp.concatenate(low, axis=0).astype(bf16)
    return 256.0 * dot(order, high) + dot(order, low)


def filtered_product(z, x_ref, w_ref, table_ref, source):
    total = jnp.zeros((z.ext, z.voxels), f32)
    for part in range(z.width // z.piece):
        columns = slice(part * z.piece, (part + 1) * z.piece)
        x = x_ref[:, columns]
        table = table_ref[lax.div(source * z.width + part * z.piece, z.band_width)]
        stacked = jnp.concatenate([x] * (table.shape[1] // z.rows), axis=0)
        filtered = dot(table, stacked)
        high = filtered.astype(bf16)
        low = filtered - high.astype(f32)
        tail = z.rows + MAXLAG
        edges = [filtered, low[:MAXLAG], low[z.rows : tail]]
        edges = jnp.concatenate(edges, axis=0).astype(bf16)
        product = dot(edges, w_ref[columns, :])
        total = total + product[: z.ext]
        head = product[z.ext : z.ext + MAXLAG]
        rim = product[z.ext + MAXLAG :]
        parts = [head, jnp.zeros((z.rows - MAXLAG, z.voxels), f32), rim]
        if z.ext > tail:
            parts.append(jnp.zeros((z.ext - tail, z.voxels), f32))
        total = total + jnp.concatenate(parts, axis=0)
    return total


def fill_table(z, offsets_ref, gains_ref, table_ref):
    lanes = table_ref.shape[2]
    column = iota((z.ext, lanes), 1)
    lag = iota((z.ext, lanes), 0) - column % z.rows
    term = column // z.rows
    for band in range(z.bands):
        value = jnp.zeros((z.ext, lanes), f32)
        for tap in range(z.taps):
            hit = lag == offsets_ref[band, tap]
            value = value + jnp.where(hit, gains_ref[band, tap], 0.0)
        first, second, third = (t.astype(f32) for t in thirds(value))
        chosen = jnp.where(term == 0, first, jnp.where(term == 1, second, third))
        chosen = jnp.where(term > 2, 0.0, chosen)
        table_ref[band] = chosen.astype(bf16)


def fill_order(z, order_ref, rows, body_at, tail_at, scale_at):
    row = iota((GROUP * z.message, 1), 0)
    member = row // z.message
    place = row % z.message
    per = rows + 8
    body = place - body_at
    source = (body // z.own) * per + member + GROUP * (body % z.own)
    source = jnp.where((body >= 0) & (body < z.tiles * z.own), source, -1)
    if tail_at is not None:
        tail = place - tail_at
        found = (tail // z.own_tail) * per + z.rows + member
        found = found + GROUP * (tail % z.own_tail)
        source = jnp.where((tail >= 0) & (tail < z.tiles * z.own_tail), found, source)
    scale = place - scale_at
    source = jnp.where((scale >= 0) & (scale < z.tiles), scale * per + rows, source)
    column = iota((GROUP * z.message, z.tiles * per), 1)
    order_ref[...] = (column == source).astype(f32).astype(bf16)


def fill_owners(z, owners_ref, along_ref, place_ref):
    owners = owners_ref[...]
    other = iota((z.voxels, z.blocks), 1)
    block = iota((z.voxels, 1), 0) // VB
    owner = jnp.sum(jnp.where(other == block, owners, 0), axis=1, keepdims=True)
    before = (owners == owner) & (other < block)
    rank = jnp.sum(before.astype(i32), axis=1, keepdims=True)
    lane = rank * VB + iota((z.voxels, 1), 0) % VB
    place = iota((z.voxels, LANES), 1) == lane
    place_ref[...] = place.astype(f32).astype(bf16)
    square = (z.blocks, z.blocks)
    diagonal = iota(square, 0) == iota(square, 1)
    down = jnp.sum(jnp.where(diagonal, owners, 0), axis=1, keepdims=True)
    shape = (z.blocks, z.voxels)
    held = iota(shape, 0) == iota(shape, 1) // VB
    along = jnp.sum(jnp.where(held, down, 0), axis=0, keepdims=True)
    along_ref[...] = jnp.broadcast_to(along, (8, z.voxels))


def first_kernel(
    z, offsets_hbm, gains_hbm, owners_hbm, x_hbm, w_hbm, signal_hbm,
    table_ref, order_ref, base_ref, along_ref, place_ref, total_ref, rest_ref,
    offsets_ref, gains_ref, owners_ref, x_ref, w_ref, signal_ref, signal_order_ref, sems,
):
    me = lax.axis_index("subj")

    def weight_rows(step):
        source = lax.rem(me + step, z.subjects)
        start = pl.multiple_of(source * z.width, z.width)
        return w_hbm.at[pl.ds(start, z.width), :]

    moves = [
        (offsets_hbm, offsets_ref),
        (gains_hbm, gains_ref),
        (x_hbm, x_ref),
        (weight_rows(0), w_ref),
        (owners_hbm, owners_ref),
        (signal_hbm, signal_ref),
    ]
    for step in range(1, z.subjects):
        rows = pl.ds((step - 1) * z.width, z.width)
        moves.append((weight_rows(step), rest_ref.at[rows, :]))
    copies = [
        pltpu.make_async_copy(origin, target, sems.at[index])
        for index, (origin, target) in enumerate(moves)
    ]
    for copy in copies:
        copy.start()
    copies[0].wait()
    copies[1].wait()
    fill_table(z, offsets_ref, gains_ref, table_ref)
    copies[2].wait()
    copies[3].wait()
    total_ref[...] = filtered_product(z, x_ref, w_ref, table_ref, me)
    fill_order(z, order_ref, z.ext, 0, z.tail_at, z.scale_at)
    fill_order(z, signal_order_ref, z.rows, z.signal_at, None, z.signal_scale_at)
    copies[4].wait()
    fill_owners(z, owners_ref, along_ref, place_ref)
    copies[5].wait()
    base_ref[...] = arranged(z, signal_ref[...].astype(f32), signal_order_ref[...])
    for copy in copies[6:]:
        copy.wait()


def second_kernel(z, table_ref, w_ref, total_ref, order_ref, base_ref, *refs):
    others, out_ref = refs[:-1], refs[-1]
    me = lax.axis_index("subj")
    total = total_ref[...]
    for step, x_ref in enumerate(others):
        source = lax.rem(me + step + 1, z.subjects)
        rows = w_ref.at[step * z.width : (step + 1) * z.width, :]
        total = total + filtered_product(z, x_ref, rows, table_ref, source)
    messages = arranged(z, total, order_ref[...]) + base_ref[...]
    for member in range(GROUP):
        message = messages[member * z.message : (member + 1) * z.message]
        message = message.astype(i32).astype(jnp.int16)
        for index in range(member, z.n, GROUP):
            out_ref[index] = message


def third_kernel(z, orders_ref, along_ref, place_ref, received_ref, *refs):
    out_refs, (block_ref, tail_ref, signal_ref) = refs[:GROUP], refs[GROUP:]
    me = lax.axis_index("tr")
    row = iota((8, LANES), 0)

    def unpack(index, _):
        x = received_ref[index].astype(i32).astype(f32)
        scales = jnp.exp2(x[z.scale_at : z.scale_at + 2 * z.tiles] - 15.0)
        for tile in range(z.tiles):
            scale = scales[tile : tile + 1]
            own = slice(tile * z.own, (tile + 1) * z.own)
            block_ref[index, own, :] = x[own] * scale
            at = z.tail_at + tile * z.own_tail
            start = at // 8 * 8
            tail = pltpu.roll(x[start : start + 8], (8 - at % 8) % 8, 0)
            tail = jnp.where(row < z.own_tail, tail * scale, 0.0)
            tail_ref[index, tile * 8 : (tile + 1) * 8, :] = tail
            scale = scales[z.tiles + tile : z.tiles + tile + 1]
            values = x[z.signal_at + tile * z.own : z.signal_at + (tile + 1) * z.own]
            signal_ref[index, own, :] = values * scale
        return 0

    for index in range(z.n) if z.n <= 16 else ():
        unpack(index, 0)
    if z.n > 16:
        lax.fori_loop(0, z.n, unpack, 0)
    tail_ref[z.n] = jnp.zeros((z.tiles * 8, LANES), f32)

    def folded(x):
        return [
            sum(
                x[tile * z.own + start : tile * z.own + start + 8]
                for start in range(0, z.own, 8)
            )
            for tile in range(z.tiles)
        ]

    def squares(position, condition):
        signal = signal_ref[position]
        if condition == z.conditions:
            return signal * signal
        if condition == 0:
            here, ahead = position, position - 1
        else:
            here = orders_ref[condition - 1, position]
            ahead = orders_ref[condition - 1, jnp.maximum(position - 1, 0)]
        ahead = jnp.where(position == 0, z.n, ahead)
        residual = signal - block_ref[here]
        tail = tail_ref[ahead]
        parts = []
        for tile in range(z.tiles):
            start = tile * z.own
            head = residual[start : start + 8] - tail[tile * 8 : (tile + 1) * 8]
            parts += [head, residual[start + 8 : start + z.own]]
        residual = jnp.concatenate(parts, axis=0)
        return residual * residual

    def add_position(position, sums):
        added = []
        for condition in range(z.conditions + 1):
            parts = folded(squares(position, condition))
            old = sums[condition * z.tiles : (condition + 1) * z.tiles]
            added += [o + p for o, p in zip(old, parts)]
        return tuple(added)

    def add_positions(step, sums):
        for index in range(GROUP):
            sums = add_position(step * GROUP + index, sums)
        return sums

    zero = jnp.zeros((8, LANES), f32)
    sums = tuple(zero for _ in range((z.conditions + 1) * z.tiles))
    sums = lax.fori_loop(0, z.n // GROUP, add_positions, sums)
    stats = []
    for tile in range(z.tiles):
        value = zero
        for condition in range(z.conditions + 1):
            stat = jnp.sum(sums[condition * z.tiles + tile], axis=0, keepdims=True)
            value = jnp.where(row == condition, stat, value)
        stats.append(value)
    stats = jnp.concatenate(stats, axis=1)
    masked = [
        jnp.where(along_ref[...] == jnp.bitwise_xor(me, step), stats, 0.0)
        for step in range(GROUP)
    ]
    terms = jnp.concatenate(
        [t.astype(f32) for t in thirds(jnp.concatenate(masked, axis=0))], axis=0
    )
    placed = dot(terms.astype(bf16), place_ref[...])
    placed = placed[: GROUP * 8] + placed[GROUP * 8 : GROUP * 16] + placed[GROUP * 16 :]
    lanes = iota((z.own, LANES), 1)
    for step, out_ref in enumerate(out_refs):
        energy = jnp.zeros((z.own, LANES), f32)
        for condition in range(z.conditions):
            value = squares(jnp.bitwise_xor(me, step), condition)
            value = sum(
                value[tile * z.own : (tile + 1) * z.own] for tile in range(z.tiles)
            )
            value = jnp.sum(value, axis=1, keepdims=True) * (1.0 / z.voxels)
            energy = jnp.where(lanes == condition, value, energy)
        out_ref[: z.own, :] = energy
        out_ref[z.own :, :] = placed[step * 8 : (step + 1) * 8]


def fourth_kernel(z, *refs):
    parts, (energy_ref, scores_ref) = refs[:GROUP], refs[GROUP:]
    member = lax.rem(lax.axis_index("tr"), GROUP)
    turned = jnp.transpose(jnp.concatenate([p[: z.own, :] for p in parts], axis=0))
    column = iota((z.rows, LANES), 0)
    owner = jnp.bitwise_xor(column // z.own, member)
    order = iota((z.rows, LANES), 1) == owner + GROUP * (column % z.own)
    order = order.astype(f32).astype(bf16)
    terms = [t.astype(f32) for t in thirds(turned[:8, : z.rows])]
    energy = dot(jnp.concatenate(terms, axis=0).astype(bf16), order)
    energy = energy[:8] + energy[8:16] + energy[16:]
    sums = sum(p[z.own :, :] for p in parts)
    lanes = iota((8, LANES), 1)
    sums = jnp.where(lanes < CAP * VB, sums, 0.0)
    signal = sums[z.conditions : z.conditions + 1]
    square = (LANES, LANES)
    mean = iota(square, 0) // VB == iota(square, 1)
    mean = jnp.where(mean & (iota(square, 1) < CAP), 1.0 / VB, 0.0).astype(bf16)
    fit = jnp.log((sums + EPSILON) / (signal + EPSILON))
    terms = jnp.concatenate([t.astype(f32) for t in thirds(fit)], axis=0).astype(bf16)
    score = dot(terms, mean)
    score = score[:8] + score[8:16] + score[16:]
    for index in range(z.conditions):
        energy_ref[index] = energy[index : index + 1, : z.rows]
        scores_ref[index] = score[index : index + 1, :CAP]


def on_device(features, block_orders, offsets, tap_gains, weights, signal, block_owner):
    z = Sizes(features, block_orders, offsets, weights, block_owner)
    owners = block_owner.reshape(1, z.blocks)
    others = [
        lax.ppermute(
            features,
            "subj",
            [((i + step) % z.subjects, i) for i in range(z.subjects)],
        )
        for step in range(1, z.subjects)
    ]
    term_lanes = -(-3 * z.rows // LANES) * LANES
    work = 2 * z.ext * z.width * z.voxels
    messages = GROUP * z.message
    shapes = [
        jax.ShapeDtypeStruct((z.bands, z.ext, term_lanes), bf16),
        jax.ShapeDtypeStruct((messages, z.tiles * (z.ext + 8)), bf16),
        jax.ShapeDtypeStruct((messages, LANES), f32),
        jax.ShapeDtypeStruct((8, z.voxels), i32),
        jax.ShapeDtypeStruct((z.voxels, LANES), bf16),
        jax.ShapeDtypeStruct((z.ext, z.voxels), f32),
        jax.ShapeDtypeStruct((z.columns - z.width, z.voxels), bf16),
    ]
    scratch = [
        pltpu.SMEM(offsets.shape, i32),
        pltpu.SMEM(tap_gains.shape, f32),
        pltpu.VMEM(owners.shape, i32),
        pltpu.VMEM(features.shape, bf16),
        pltpu.VMEM((z.width, z.voxels), bf16),
        pltpu.VMEM((z.rows, z.voxels), bf16),
        pltpu.VMEM((messages, z.tiles * (z.rows + 8)), bf16),
        pltpu.SemaphoreType.DMA((5 + z.subjects,)),
    ]
    operands = (offsets, tap_gains, owners, features, weights[0], signal[0])
    operands = [pltpu.with_memory_space_constraint(x, pltpu.HBM) for x in operands]
    table, order, base, along, place, total, rest = pl.pallas_call(
        functools.partial(first_kernel, z),
        out_shape=shapes,
        in_specs=[HBM] * 6,
        out_specs=[VMEM] * 7,
        scratch_shapes=scratch,
        compiler_params=params(),
        cost_estimate=cost(work, 3 << 20),
        name="prepare_and_own_columns",
    )(*operands)
    outgoing = pl.pallas_call(
        functools.partial(second_kernel, z),
        out_shape=jax.ShapeDtypeStruct((z.n, z.message, LANES), jnp.int16),
        in_specs=[VMEM] * (5 + len(others)),
        out_specs=VMEM,
        compiler_params=params(),
        cost_estimate=cost(work, 2 << 20),
        name="other_columns",
    )(table, rest, total, order, base, *others)
    received = lax.all_to_all(outgoing, "tr", 0, 0, tiled=True)
    orders = pltpu.with_memory_space_constraint(block_orders, pltpu.SMEM)
    part = jax.ShapeDtypeStruct((z.own + 8, LANES), f32)
    parts = pl.pallas_call(
        functools.partial(third_kernel, z),
        out_shape=[part] * GROUP,
        in_specs=[SMEM, VMEM, VMEM, VMEM],
        out_specs=[VMEM] * GROUP,
        scratch_shapes=[
            pltpu.VMEM((z.n, z.tiles * z.own, LANES), f32),
            pltpu.VMEM((z.n + 1, z.tiles * 8, LANES), f32),
            pltpu.VMEM((z.n, z.tiles * z.own, LANES), f32),
        ],
        compiler_params=params(),
        cost_estimate=cost(work, 1 << 20),
        name="residuals",
    )(orders, along, place, received)
    parts = [parts[0]] + [
        lax.ppermute(parts[step], "tr", [(i, i ^ step) for i in range(z.n)])
        for step in range(1, GROUP)
    ]
    energy, scores = pl.pallas_call(
        functools.partial(fourth_kernel, z),
        out_shape=[
            jax.ShapeDtypeStruct((z.conditions, 1, z.rows), f32),
            jax.ShapeDtypeStruct((z.conditions, 1, CAP), f32),
        ],
        in_specs=[VMEM] * GROUP,
        out_specs=[VMEM, VMEM],
        compiler_params=params(),
        cost_estimate=cost(1 << 20, 1 << 16),
        name="scores",
    )(*parts)
    return energy.transpose(1, 2, 0), scores.transpose(1, 2, 0)


def solution(mesh):
    placed = (
        P("tr", "subj"),
        P(),
        P(),
        P(),
        P("subj", None, None),
        P("subj", "tr", None),
        P("subj", None, None),
    )
    return jax.shard_map(
        on_device,
        mesh=mesh,
        in_specs=placed,
        out_specs=(P("subj", "tr", None), P("subj", "tr", None)),
        check_vma=False,
    )
```

```python
import functools

import jax
import jax.numpy as jnp
from jax import lax
from jax.experimental import pallas as pl
from jax.experimental.pallas import tpu as pltpu
from jax.sharding import PartitionSpec as P

MAXLAG = 8
VB = 4
CAP = 8
LANES = 128
GROUP = 4
EPSILON = 1e-6

f32 = jnp.float32
bf16 = jnp.bfloat16
i32 = jnp.int32

VMEM = pl.BlockSpec(memory_space=pltpu.VMEM)
HBM = pl.BlockSpec(memory_space=pltpu.HBM)


def iota(shape, axis):
    return lax.broadcasted_iota(i32, shape, axis)


def dot(a, b):
    return jnp.dot(a, b, preferred_element_type=f32)


def thirds(x):
    first = x.astype(bf16)
    rest = x - first.astype(f32)
    second = rest.astype(bf16)
    return first, second, (rest - second.astype(f32)).astype(bf16)


def params(**more):
    return pltpu.CompilerParams(vmem_limit_bytes=48 * 1024 * 1024, **more)


def cost(flops, nbytes):
    return pl.CostEstimate(flops=flops, bytes_accessed=nbytes, transcendentals=0)


class Sizes:
    def __init__(self, features, block_orders, offsets, weights, block_owner):
        self.subjects = lax.axis_size("subj")
        self.n = lax.axis_size("tr")
        self.rows, self.width = features.shape
        self.columns, self.voxels = weights.shape[1:]
        self.bands, self.taps = offsets.shape
        self.band_width = self.columns // self.bands
        self.piece = min(self.width, self.band_width)
        self.conditions = block_orders.shape[0] + 1
        self.blocks = block_owner.shape[1]
        self.ext = self.rows + MAXLAG
        self.own = self.rows // GROUP
        self.own_tail = MAXLAG // GROUP
        self.tiles = self.voxels // LANES
        self.signal_at = self.tiles * self.own
        self.tail_at = 2 * self.signal_at
        self.scale_at = self.tail_at + self.tiles * self.own_tail
        self.signal_scale_at = self.scale_at + self.tiles
        self.message = -(-(self.signal_scale_at + self.tiles) // 8) * 8
        assert self.n % GROUP == 0 and self.own % 8 == 0 and self.conditions < 8
        assert self.own_tail <= 8 and CAP * VB <= LANES


def coded(x):
    largest = jnp.max(jnp.abs(x), axis=0, keepdims=True)
    power = jnp.floor(jnp.log2(jnp.maximum(largest, 2.0**-100))) + 1.0
    value = jnp.round(x * jnp.exp2(15.0 - power))
    return jnp.clip(value, -32767.0, 32767.0), power


def signal_messages(z, signal, order):
    value, power = coded(signal)
    upper = jnp.floor(value * (1.0 / 256.0))
    lower = value - 256.0 * upper
    powers = jnp.broadcast_to(power, (8, z.voxels))
    high, low = [], []
    for tile in range(z.tiles):
        lanes = slice(tile * LANES, (tile + 1) * LANES)
        high += [upper[:, lanes], jnp.zeros((8, LANES), f32)]
        low += [lower[:, lanes], powers[:, lanes]]
    high = jnp.concatenate(high, axis=0).astype(bf16)
    low = jnp.concatenate(low, axis=0).astype(bf16)
    return 256.0 * dot(order, high) + dot(order, low)


def filtered_product(z, x_ref, w_ref, table_ref, source):
    total = jnp.zeros((z.ext, z.voxels), f32)
    early = iota((8, z.piece), 0) < z.own_tail
    for part in range(z.width // z.piece):
        columns = slice(part * z.piece, (part + 1) * z.piece)
        x = x_ref[:, columns]
        table = table_ref[lax.div(source * z.width + part * z.piece, z.band_width)]
        stacked = jnp.concatenate([x] * (table.shape[1] // z.rows), axis=0)
        filtered = dot(table, stacked)
        low = filtered - filtered.astype(bf16).astype(f32)
        edges = [filtered]
        for start in range(0, z.rows, z.own):
            edges.append(jnp.where(early, low[start : start + 8], 0.0))
        edges.append(low[z.rows :])
        edges = jnp.concatenate(edges, axis=0).astype(bf16)
        product = dot(edges, w_ref[columns, :])
        parts = []
        for member in range(GROUP):
            start, at = member * z.own, z.ext + member * 8
            parts.append(product[start : start + 8] + product[at : at + 8])
            parts.append(product[start + 8 : start + z.own])
        parts.append(product[z.rows : z.ext] + product[z.ext + GROUP * 8 :])
        total = total + jnp.concatenate(parts, axis=0)
    return total


def fill_table(z, offsets_ref, gains_ref, table_ref):
    lanes = table_ref.shape[2]
    column = iota((z.ext, lanes), 1)
    row = iota((z.ext, 1), 0)
    after = row - z.rows
    time = row // z.own + GROUP * (row % z.own)
    time_after = z.rows + after // z.own_tail + GROUP * (after % z.own_tail)
    lag = jnp.where(after < 0, time, time_after) - column % z.rows
    term = column // z.rows
    for band in range(z.bands):
        value = jnp.zeros((z.ext, lanes), f32)
        for tap in range(z.taps):
            hit = lag == offsets_ref[band, tap]
            value = value + jnp.where(hit, gains_ref[band, tap], 0.0)
        first, second, third = (t.astype(f32) for t in thirds(value))
        chosen = jnp.where(term == 0, first, jnp.where(term == 1, second, third))
        chosen = jnp.where(term > 2, 0.0, chosen)
        table_ref[band] = chosen.astype(bf16)


def fill_order(z, order_ref):
    row = iota((GROUP * z.message, 1), 0)
    member = row // z.message
    place = row % z.message
    per = z.rows + 8
    body = place - z.signal_at
    source = (body // z.own) * per + member + GROUP * (body % z.own)
    source = jnp.where((body >= 0) & (body < z.signal_at), source, -1)
    scale = place - z.signal_scale_at
    found = scale * per + z.rows
    source = jnp.where((scale >= 0) & (scale < z.tiles), found, source)
    column = iota((GROUP * z.message, z.tiles * per), 1)
    order_ref[...] = (column == source).astype(f32).astype(bf16)


def fill_owners(z, owners_ref, along_ref, place_ref):
    owners = owners_ref[...]
    other = iota((z.voxels, z.blocks), 1)
    block = iota((z.voxels, 1), 0) // VB
    owner = jnp.sum(jnp.where(other == block, owners, 0), axis=1, keepdims=True)
    before = (owners == owner) & (other < block)
    rank = jnp.sum(before.astype(i32), axis=1, keepdims=True)
    lane = rank * VB + iota((z.voxels, 1), 0) % VB
    place = iota((z.voxels, LANES), 1) == lane
    place_ref[...] = place.astype(f32).astype(bf16)
    square = (z.blocks, z.blocks)
    diagonal = iota(square, 0) == iota(square, 1)
    down = jnp.sum(jnp.where(diagonal, owners, 0), axis=1, keepdims=True)
    shape = (z.blocks, z.voxels)
    held = iota(shape, 0) == iota(shape, 1) // VB
    along = jnp.sum(jnp.where(held, down, 0), axis=0, keepdims=True)
    along_ref[...] = jnp.broadcast_to(along, (8, z.voxels))


def first_kernel(
    z, offsets_hbm, gains_hbm, owners_hbm, x_hbm, w_hbm, signal_hbm, orders_hbm,
    table_ref, base_ref, along_ref, place_ref, total_ref, rest_ref, orders_ref,
    offsets_ref, gains_ref, owners_ref, x_ref, w_ref, signal_ref, order_ref, sems,
):
    me = lax.axis_index("subj")

    def weight_rows(step):
        source = lax.rem(me + step, z.subjects)
        start = pl.multiple_of(source * z.width, z.width)
        return w_hbm.at[pl.ds(start, z.width), :]

    moves = [
        (offsets_hbm, offsets_ref),
        (gains_hbm, gains_ref),
        (x_hbm, x_ref),
        (weight_rows(0), w_ref),
        (owners_hbm, owners_ref),
        (signal_hbm, signal_ref),
        (orders_hbm, orders_ref),
    ]
    for step in range(1, z.subjects):
        rows = pl.ds((step - 1) * z.width, z.width)
        moves.append((weight_rows(step), rest_ref.at[rows, :]))
    copies = [
        pltpu.make_async_copy(origin, target, sems.at[index])
        for index, (origin, target) in enumerate(moves)
    ]
    for copy in copies:
        copy.start()
    fill_order(z, order_ref)
    copies[0].wait()
    copies[1].wait()
    fill_table(z, offsets_ref, gains_ref, table_ref)
    copies[2].wait()
    copies[3].wait()
    total_ref[...] = filtered_product(z, x_ref, w_ref, table_ref, me)
    copies[4].wait()
    fill_owners(z, owners_ref, along_ref, place_ref)
    copies[5].wait()
    base_ref[...] = signal_messages(z, signal_ref[...].astype(f32), order_ref[...])
    for copy in copies[6:]:
        copy.wait()


def second_kernel(z, table_ref, w_ref, total_ref, base_ref, *refs):
    others, out_ref = refs[:-1], refs[-1]
    me = lax.axis_index("subj")
    total = total_ref[...]
    for step, x_ref in enumerate(others):
        source = lax.rem(me + step + 1, z.subjects)
        rows = w_ref.at[step * z.width : (step + 1) * z.width, :]
        total = total + filtered_product(z, x_ref, rows, table_ref, source)
    value, power = coded(total)
    row = iota((8, LANES), 0)
    for member in range(GROUP):
        start = member * z.message
        body, ends = [], []
        for at in range(z.tail_at, z.message, 8):
            ends.append(base_ref[start + at : start + at + 8, :])
        for tile in range(z.tiles):
            lanes = slice(tile * LANES, (tile + 1) * LANES)
            body.append(value[member * z.own : (member + 1) * z.own, lanes])
            which, place = divmod(tile * z.own_tail, 8)
            shift = (place - member * z.own_tail) % 8
            tail = pltpu.roll(value[z.rows :, lanes], shift, 0)
            here = (row >= place) & (row < place + z.own_tail)
            ends[which] = jnp.where(here, tail, ends[which])
            which, place = divmod(z.scale_at - z.tail_at + tile, 8)
            ends[which] = jnp.where(row == place, power[:, lanes], ends[which])
        body.append(base_ref[start + z.signal_at : start + z.tail_at, :])
        message = jnp.concatenate(body + ends, axis=0).astype(i32).astype(jnp.int16)
        for index in range(member, z.n, GROUP):
            out_ref[index] = message


def third_kernel(z, orders_in_ref, along_ref, place_ref, received_ref, *refs):
    out_refs, (block_ref, tail_ref, signal_ref, orders_ref, sem) = (
        refs[:GROUP],
        refs[GROUP:],
    )
    copy = pltpu.make_async_copy(orders_in_ref, orders_ref, sem)
    copy.start()
    me = lax.axis_index("tr")
    row = iota((8, LANES), 0)

    def unpack(index, _):
        x = received_ref[index].astype(i32).astype(f32)
        scales = jnp.exp2(x[z.scale_at : z.scale_at + 2 * z.tiles] - 15.0)
        for tile in range(z.tiles):
            scale = scales[tile : tile + 1]
            own = slice(tile * z.own, (tile + 1) * z.own)
            block_ref[index, own, :] = x[own] * scale
            at = z.tail_at + tile * z.own_tail
            start = at // 8 * 8
            tail = pltpu.roll(x[start : start + 8], (8 - at % 8) % 8, 0)
            tail = jnp.where(row < z.own_tail, tail * scale, 0.0)
            tail_ref[index, tile * 8 : (tile + 1) * 8, :] = tail
            scale = scales[z.tiles + tile : z.tiles + tile + 1]
            values = x[z.signal_at + tile * z.own : z.signal_at + (tile + 1) * z.own]
            signal_ref[index, own, :] = values * scale
        return 0

    for index in range(z.n) if z.n <= 16 else ():
        unpack(index, 0)
    if z.n > 16:
        lax.fori_loop(0, z.n, unpack, 0)
    tail_ref[z.n] = jnp.zeros((z.tiles * 8, LANES), f32)
    copy.wait()

    def folded(x):
        return [
            sum(
                x[tile * z.own + start : tile * z.own + start + 8]
                for start in range(0, z.own, 8)
            )
            for tile in range(z.tiles)
        ]

    def squares(signal, position, condition):
        if condition == z.conditions:
            return signal * signal
        if condition == 0:
            here, ahead = position, position - 1
        else:
            here = orders_ref[condition - 1, position]
            ahead = orders_ref[condition - 1, jnp.maximum(position - 1, 0)]
        ahead = jnp.where(position == 0, z.n, ahead)
        residual = signal - block_ref[here]
        tail = tail_ref[ahead]
        parts = []
        for tile in range(z.tiles):
            start = tile * z.own
            head = residual[start : start + 8] - tail[tile * 8 : (tile + 1) * 8]
            parts += [head, residual[start + 8 : start + z.own]]
        residual = jnp.concatenate(parts, axis=0)
        return residual * residual

    def add_position(position, sums):
        added = []
        signal = signal_ref[position]
        for condition in range(z.conditions + 1):
            parts = folded(squares(signal, position, condition))
            old = sums[condition * z.tiles : (condition + 1) * z.tiles]
            added += [o + p for o, p in zip(old, parts)]
        return tuple(added)

    def add_positions(step, sums):
        for index in range(GROUP):
            sums = add_position(step * GROUP + index, sums)
        return sums

    zero = jnp.zeros((8, LANES), f32)
    sums = tuple(zero for _ in range((z.conditions + 1) * z.tiles))
    sums = lax.fori_loop(0, z.n // GROUP, add_positions, sums)
    stats = []
    for tile in range(z.tiles):
        value = zero
        for condition in range(z.conditions + 1):
            stat = jnp.sum(sums[condition * z.tiles + tile], axis=0, keepdims=True)
            value = jnp.where(row == condition, stat, value)
        stats.append(value)
    stats = jnp.concatenate(stats, axis=1)
    masked = [
        jnp.where(along_ref[...] == jnp.bitwise_xor(me, step), stats, 0.0)
        for step in range(GROUP)
    ]
    terms = jnp.concatenate(
        [t.astype(f32) for t in thirds(jnp.concatenate(masked, axis=0))], axis=0
    )
    placed = dot(terms.astype(bf16), place_ref[...])
    placed = placed[: GROUP * 8] + placed[GROUP * 8 : GROUP * 16] + placed[GROUP * 16 :]
    lanes = iota((z.own, LANES), 1)
    for step, out_ref in enumerate(out_refs):
        energy = jnp.zeros((z.own, LANES), f32)
        position = jnp.bitwise_xor(me, step)
        signal = signal_ref[position]
        for condition in range(z.conditions):
            value = squares(signal, position, condition)
            value = sum(
                value[tile * z.own : (tile + 1) * z.own] for tile in range(z.tiles)
            )
            value = jnp.sum(value, axis=1, keepdims=True) * (1.0 / z.voxels)
            energy = jnp.where(lanes == condition, value, energy)
        out_ref[: z.own, :] = energy
        out_ref[z.own :, :] = placed[step * 8 : (step + 1) * 8]


def fourth_kernel(z, *refs):
    parts, (energy_ref, scores_ref) = refs[:GROUP], refs[GROUP:]
    member = lax.rem(lax.axis_index("tr"), GROUP)
    turned = jnp.transpose(jnp.concatenate([p[: z.own, :] for p in parts], axis=0))
    column = iota((z.rows, LANES), 0)
    owner = jnp.bitwise_xor(column // z.own, member)
    order = iota((z.rows, LANES), 1) == owner + GROUP * (column % z.own)
    order = order.astype(f32).astype(bf16)
    terms = [t.astype(f32) for t in thirds(turned[:8, : z.rows])]
    energy = dot(jnp.concatenate(terms, axis=0).astype(bf16), order)
    energy = energy[:8] + energy[8:16] + energy[16:]
    sums = sum(p[z.own :, :] for p in parts)
    lanes = iota((8, LANES), 1)
    sums = jnp.where(lanes < CAP * VB, sums, 0.0)
    signal = sums[z.conditions : z.conditions + 1]
    square = (LANES, LANES)
    mean = iota(square, 0) // VB == iota(square, 1)
    mean = jnp.where(mean & (iota(square, 1) < CAP), 1.0 / VB, 0.0).astype(bf16)
    fit = jnp.log((sums + EPSILON) / (signal + EPSILON))
    terms = jnp.concatenate([t.astype(f32) for t in thirds(fit)], axis=0).astype(bf16)
    score = dot(terms, mean)
    score = score[:8] + score[8:16] + score[16:]
    for index in range(z.conditions):
        energy_ref[index] = energy[index : index + 1, : z.rows]
        scores_ref[index] = score[index : index + 1, :CAP]


def on_device(features, block_orders, offsets, tap_gains, weights, signal, block_owner):
    z = Sizes(features, block_orders, offsets, weights, block_owner)
    owners = block_owner.reshape(1, z.blocks)
    others = [
        lax.ppermute(
            features,
            "subj",
            [((i + step) % z.subjects, i) for i in range(z.subjects)],
        )
        for step in range(1, z.subjects)
    ]
    term_lanes = -(-3 * z.rows // LANES) * LANES
    work = 2 * z.ext * z.width * z.voxels
    messages = GROUP * z.message
    shapes = [
        jax.ShapeDtypeStruct((z.bands, z.ext, term_lanes), bf16),
        jax.ShapeDtypeStruct((messages, LANES), f32),
        jax.ShapeDtypeStruct((8, z.voxels), i32),
        jax.ShapeDtypeStruct((z.voxels, LANES), bf16),
        jax.ShapeDtypeStruct((z.ext, z.voxels), f32),
        jax.ShapeDtypeStruct((z.columns - z.width, z.voxels), bf16),
        jax.ShapeDtypeStruct(block_orders.shape, i32),
    ]
    scratch = [
        pltpu.SMEM(offsets.shape, i32),
        pltpu.SMEM(tap_gains.shape, f32),
        pltpu.VMEM(owners.shape, i32),
        pltpu.VMEM(features.shape, bf16),
        pltpu.VMEM((z.width, z.voxels), bf16),
        pltpu.VMEM((z.rows, z.voxels), bf16),
        pltpu.VMEM((messages, z.tiles * (z.rows + 8)), bf16),
        pltpu.SemaphoreType.DMA((6 + z.subjects,)),
    ]
    operands = (offsets, tap_gains, owners, features, weights[0], signal[0], block_orders)
    operands = [pltpu.with_memory_space_constraint(x, pltpu.HBM) for x in operands]
    table, base, along, place, total, rest, orders = pl.pallas_call(
        functools.partial(first_kernel, z),
        out_shape=shapes,
        in_specs=[HBM] * 7,
        out_specs=[VMEM] * 7,
        scratch_shapes=scratch,
        compiler_params=params(),
        cost_estimate=cost(work, 3 << 20),
        name="prepare_and_own_columns",
    )(*operands)
    outgoing = pl.pallas_call(
        functools.partial(second_kernel, z),
        out_shape=jax.ShapeDtypeStruct((z.n, z.message, LANES), jnp.int16),
        in_specs=[VMEM] * (4 + len(others)),
        out_specs=VMEM,
        compiler_params=params(),
        cost_estimate=cost(work, 2 << 20),
        name="other_columns",
    )(table, rest, total, base, *others)
    received = lax.all_to_all(outgoing, "tr", 0, 0, tiled=True)
    part = jax.ShapeDtypeStruct((z.own + 8, LANES), f32)
    parts = pl.pallas_call(
        functools.partial(third_kernel, z),
        out_shape=[part] * GROUP,
        in_specs=[VMEM] * 4,
        out_specs=[VMEM] * GROUP,
        scratch_shapes=[
            pltpu.VMEM((z.n, z.tiles * z.own, LANES), f32),
            pltpu.VMEM((z.n + 1, z.tiles * 8, LANES), f32),
            pltpu.VMEM((z.n, z.tiles * z.own, LANES), f32),
            pltpu.SMEM(block_orders.shape, i32),
            pltpu.SemaphoreType.DMA,
        ],
        compiler_params=params(),
        cost_estimate=cost(work, 1 << 20),
        name="residuals",
    )(orders, along, place, received)
    parts = [parts[0]] + [
        lax.ppermute(parts[step], "tr", [(i, i ^ step) for i in range(z.n)])
        for step in range(1, GROUP)
    ]
    energy, scores = pl.pallas_call(
        functools.partial(fourth_kernel, z),
        out_shape=[
            jax.ShapeDtypeStruct((z.conditions, 1, z.rows), f32),
            jax.ShapeDtypeStruct((z.conditions, 1, CAP), f32),
        ],
        in_specs=[VMEM] * GROUP,
        out_specs=[VMEM, VMEM],
        compiler_params=params(),
        cost_estimate=cost(1 << 20, 1 << 16),
        name="scores",
    )(*parts)
    return energy.transpose(1, 2, 0), scores.transpose(1, 2, 0)


def solution(mesh):
    placed = (
        P("tr", "subj"),
        P(),
        P(),
        P(),
        P("subj", None, None),
        P("subj", "tr", None),
        P("subj", None, None),
    )
    return jax.shard_map(
        on_device,
        mesh=mesh,
        in_specs=placed,
        out_specs=(P("subj", "tr", None), P("subj", "tr", None)),
        check_vma=False,
    )
```

```python
import functools

import jax
import jax.numpy as jnp
from jax import lax
from jax.experimental import pallas as pl
from jax.experimental.pallas import tpu as pltpu
from jax.sharding import PartitionSpec as P

MAXLAG = 8
VB = 4
CAP = 8
LANES = 128
GROUP = 4
EPSILON = 1e-6

f32 = jnp.float32
bf16 = jnp.bfloat16
i32 = jnp.int32

VMEM = pl.BlockSpec(memory_space=pltpu.VMEM)
HBM = pl.BlockSpec(memory_space=pltpu.HBM)


def iota(shape, axis):
    return lax.broadcasted_iota(i32, shape, axis)


def dot(a, b):
    return jnp.dot(a, b, preferred_element_type=f32)


def thirds(x):
    first = x.astype(bf16)
    rest = x - first.astype(f32)
    second = rest.astype(bf16)
    return first, second, (rest - second.astype(f32)).astype(bf16)


def params(**more):
    return pltpu.CompilerParams(vmem_limit_bytes=48 * 1024 * 1024, **more)


def cost(flops, nbytes):
    return pl.CostEstimate(flops=flops, bytes_accessed=nbytes, transcendentals=0)


class Sizes:
    def __init__(self, features, block_orders, offsets, weights, block_owner):
        self.subjects = lax.axis_size("subj")
        self.n = lax.axis_size("tr")
        self.rows, self.width = features.shape
        self.columns, self.voxels = weights.shape[1:]
        self.bands, self.taps = offsets.shape
        self.band_width = self.columns // self.bands
        self.piece = min(self.width, self.band_width)
        self.conditions = block_orders.shape[0] + 1
        self.blocks = block_owner.shape[1]
        self.ext = self.rows + MAXLAG
        self.own = self.rows // GROUP
        self.own_tail = MAXLAG // GROUP
        self.tiles = self.voxels // LANES
        self.signal_at = self.tiles * self.own
        self.tail_at = 2 * self.signal_at
        self.scale_at = self.tail_at + self.tiles * self.own_tail
        self.signal_scale_at = self.scale_at + self.tiles
        self.message = -(-(self.signal_scale_at + self.tiles) // 8) * 8
        assert self.n % GROUP == 0 and self.own % 8 == 0 and self.conditions < 8
        assert self.own_tail <= 8 and CAP * VB <= LANES


def coded(x):
    largest = jnp.max(jnp.abs(x), axis=0, keepdims=True)
    power = jnp.floor(jnp.log2(jnp.maximum(largest, 2.0**-100))) + 1.0
    value = jnp.round(x * jnp.exp2(15.0 - power))
    return jnp.clip(value, -32767.0, 32767.0), power


def signal_messages(z, signal, order):
    value, power = coded(signal)
    upper = jnp.floor(value * (1.0 / 256.0))
    lower = value - 256.0 * upper
    powers = jnp.broadcast_to(power, (8, z.voxels))
    high, low = [], []
    for tile in range(z.tiles):
        lanes = slice(tile * LANES, (tile + 1) * LANES)
        high += [upper[:, lanes], jnp.zeros((8, LANES), f32)]
        low += [lower[:, lanes], powers[:, lanes]]
    high = jnp.concatenate(high, axis=0).astype(bf16)
    low = jnp.concatenate(low, axis=0).astype(bf16)
    return 256.0 * dot(order, high) + dot(order, low)


def filtered_product(z, x_ref, w_ref, table_ref, source):
    total = jnp.zeros((z.ext, z.voxels), f32)
    early = iota((8, z.piece), 0) < z.own_tail
    for part in range(z.width // z.piece):
        columns = slice(part * z.piece, (part + 1) * z.piece)
        x = x_ref[:, columns]
        table = table_ref[lax.div(source * z.width + part * z.piece, z.band_width)]
        stacked = jnp.concatenate([x] * (table.shape[1] // z.rows), axis=0)
        filtered = dot(table, stacked)
        low = filtered - filtered.astype(bf16).astype(f32)
        edges = [filtered]
        for start in range(0, z.rows, z.own):
            edges.append(jnp.where(early, low[start : start + 8], 0.0))
        edges.append(low[z.rows :])
        edges = jnp.concatenate(edges, axis=0).astype(bf16)
        product = dot(edges, w_ref[columns, :])
        parts = []
        for member in range(GROUP):
            start, at = member * z.own, z.ext + member * 8
            parts.append(product[start : start + 8] + product[at : at + 8])
            parts.append(product[start + 8 : start + z.own])
        parts.append(product[z.rows : z.ext] + product[z.ext + GROUP * 8 :])
        total = total + jnp.concatenate(parts, axis=0)
    return total


def fill_table(z, offsets_ref, gains_ref, table_ref):
    lanes = table_ref.shape[2]
    column = iota((z.ext, lanes), 1)
    row = iota((z.ext, 1), 0)
    after = row - z.rows
    time = row // z.own + GROUP * (row % z.own)
    time_after = z.rows + after // z.own_tail + GROUP * (after % z.own_tail)
    lag = jnp.where(after < 0, time, time_after) - column % z.rows
    term = column // z.rows
    for band in range(z.bands):
        value = jnp.zeros((z.ext, lanes), f32)
        for tap in range(z.taps):
            hit = lag == offsets_ref[band, tap]
            value = value + jnp.where(hit, gains_ref[band, tap], 0.0)
        first, second, third = (t.astype(f32) for t in thirds(value))
        chosen = jnp.where(term == 0, first, jnp.where(term == 1, second, third))
        chosen = jnp.where(term > 2, 0.0, chosen)
        table_ref[band] = chosen.astype(bf16)


def fill_order(z, order_ref):
    row = iota((GROUP * z.message, 1), 0)
    member = row // z.message
    place = row % z.message
    per = z.rows + 8
    body = place - z.signal_at
    source = (body // z.own) * per + member + GROUP * (body % z.own)
    source = jnp.where((body >= 0) & (body < z.signal_at), source, -1)
    scale = place - z.signal_scale_at
    found = scale * per + z.rows
    source = jnp.where((scale >= 0) & (scale < z.tiles), found, source)
    column = iota((GROUP * z.message, z.tiles * per), 1)
    order_ref[...] = (column == source).astype(f32).astype(bf16)


def fill_owners(z, owners_ref, mean_ref):
    owners = owners_ref[...]
    other = iota((z.voxels, z.blocks), 1)
    block = iota((z.voxels, 1), 0) // VB
    owner = jnp.sum(jnp.where(other == block, owners, 0), axis=1, keepdims=True)
    before = (owners == owner) & (other < block)
    rank = jnp.sum(before.astype(i32), axis=1, keepdims=True)
    rank = jnp.where(owner == lax.axis_index("tr"), rank, -1)
    mean = jnp.where(iota((z.voxels, LANES), 1) == rank, 1.0 / VB, 0.0)
    mean_ref[...] = mean.astype(bf16)


def first_kernel(
    z, offsets_hbm, gains_hbm, owners_hbm, x_hbm, w_hbm, signal_hbm, orders_hbm,
    table_ref, base_ref, mean_ref, total_ref, rest_ref, orders_ref,
    offsets_ref, gains_ref, owners_ref, x_ref, w_ref, signal_ref, order_ref, sems,
):
    me = lax.axis_index("subj")

    def weight_rows(step):
        source = lax.rem(me + step, z.subjects)
        start = pl.multiple_of(source * z.width, z.width)
        return w_hbm.at[pl.ds(start, z.width), :]

    moves = [
        (offsets_hbm, offsets_ref),
        (gains_hbm, gains_ref),
        (x_hbm, x_ref),
        (weight_rows(0), w_ref),
        (owners_hbm, owners_ref),
        (signal_hbm, signal_ref),
        (orders_hbm, orders_ref),
    ]
    for step in range(1, z.subjects):
        rows = pl.ds((step - 1) * z.width, z.width)
        moves.append((weight_rows(step), rest_ref.at[rows, :]))
    copies = [
        pltpu.make_async_copy(origin, target, sems.at[index])
        for index, (origin, target) in enumerate(moves)
    ]
    for copy in copies:
        copy.start()
    fill_order(z, order_ref)
    copies[0].wait()
    copies[1].wait()
    fill_table(z, offsets_ref, gains_ref, table_ref)
    copies[2].wait()
    copies[3].wait()
    total_ref[...] = filtered_product(z, x_ref, w_ref, table_ref, me)
    copies[4].wait()
    fill_owners(z, owners_ref, mean_ref)
    copies[5].wait()
    base_ref[...] = signal_messages(z, signal_ref[...].astype(f32), order_ref[...])
    for copy in copies[6:]:
        copy.wait()


def second_kernel(z, table_ref, w_ref, total_ref, base_ref, *refs):
    others, out_ref = refs[:-1], refs[-1]
    me = lax.axis_index("subj")
    total = total_ref[...]
    for step, x_ref in enumerate(others):
        source = lax.rem(me + step + 1, z.subjects)
        rows = w_ref.at[step * z.width : (step + 1) * z.width, :]
        total = total + filtered_product(z, x_ref, rows, table_ref, source)
    value, power = coded(total)
    row = iota((8, LANES), 0)
    for member in range(GROUP):
        start = member * z.message
        body, ends = [], []
        for at in range(z.tail_at, z.message, 8):
            ends.append(base_ref[start + at : start + at + 8, :])
        for tile in range(z.tiles):
            lanes = slice(tile * LANES, (tile + 1) * LANES)
            body.append(value[member * z.own : (member + 1) * z.own, lanes])
            which, place = divmod(tile * z.own_tail, 8)
            shift = (place - member * z.own_tail) % 8
            tail = pltpu.roll(value[z.rows :, lanes], shift, 0)
            here = (row >= place) & (row < place + z.own_tail)
            ends[which] = jnp.where(here, tail, ends[which])
            which, place = divmod(z.scale_at - z.tail_at + tile, 8)
            ends[which] = jnp.where(row == place, power[:, lanes], ends[which])
        body.append(base_ref[start + z.signal_at : start + z.tail_at, :])
        message = jnp.concatenate(body + ends, axis=0).astype(i32).astype(jnp.int16)
        for index in range(member, z.n, GROUP):
            out_ref[index] = message


def third_kernel(z, orders_in_ref, received_ref, *refs):
    out_refs, (block_ref, tail_ref, *more) = refs[:GROUP], refs[GROUP:]
    orders = orders_in_ref[...]
    if more:
        orders_ref, sem = more
        copy = pltpu.make_async_copy(orders_in_ref, orders_ref, sem)
        copy.start()
    me = lax.axis_index("tr")
    row = iota((8, LANES), 0)

    def numbers(index, start, stop):
        return received_ref[index, start:stop, :].astype(i32).astype(f32)

    def scales(index, start):
        at = start // 8 * 8
        stop = -(-(start + z.tiles) // 8) * 8
        power = numbers(index, at, stop)[start - at : start - at + z.tiles]
        return jnp.exp2(power - 15.0)

    def scaled(x, scale):
        parts = [
            x[tile * z.own : (tile + 1) * z.own] * scale[tile : tile + 1]
            for tile in range(z.tiles)
        ]
        return jnp.concatenate(parts, axis=0)

    def unpack(index, carry):
        scale = scales(index, z.scale_at)
        block_ref[index] = scaled(numbers(index, 0, z.signal_at), scale)
        end = -(-z.scale_at // 8) * 8
        tails = numbers(index, z.tail_at, end)
        for tile in range(z.tiles):
            which, place = divmod(tile * z.own_tail, 8)
            tail = pltpu.roll(tails[which * 8 : which * 8 + 8], (8 - place) % 8, 0)
            tail = jnp.where(row < z.own_tail, tail * scale[tile : tile + 1], 0.0)
            tail_ref[index, tile * 8 : (tile + 1) * 8, :] = tail
        return carry

    def signal_of(position):
        x = numbers(position, z.signal_at, z.tail_at)
        return scaled(x, scales(position, z.signal_scale_at))

    def squares(signal, here, ahead):
        residual = signal - block_ref[here]
        parts = []
        for tile in range(z.tiles):
            start = tile * z.own
            tail = tail_ref[ahead, tile * 8 : (tile + 1) * 8, :]
            parts.append(residual[start : start + 8] - tail)
            parts.append(residual[start + 8 : start + z.own])
        residual = jnp.concatenate(parts, axis=0)
        return residual * residual

    def add_position(position, sums):
        added = []
        signal = signal_of(position)
        first = position == 0
        before = jnp.maximum(position - 1, 0)
        for condition in range(z.conditions + 1):
            if condition == z.conditions:
                value = signal * signal
            else:
                if condition == 0:
                    here, ahead = position, before
                elif more:
                    here = orders_ref[condition - 1, position]
                    ahead = orders_ref[condition - 1, before]
                else:
                    here = orders[condition - 1, position]
                    ahead = orders[condition - 1, max(position - 1, 0)]
                value = squares(signal, here, jnp.where(first, z.n, ahead))
            for tile in range(z.tiles):
                total = sums[condition * z.tiles + tile]
                for start in range(tile * z.own, (tile + 1) * z.own, 8):
                    total = total + value[start : start + 8]
                added.append(total)
        return tuple(added)

    def loop(body, carry):
        if more:
            return lax.fori_loop(0, z.n, body, carry)
        for index in range(z.n):
            carry = body(index, carry)
        return carry

    loop(unpack, 0)
    tail_ref[z.n] = jnp.zeros((z.tiles * 8, LANES), f32)
    if more:
        copy.wait()
    zero = jnp.zeros((8, LANES), f32)
    sums = tuple(zero for _ in range((z.conditions + 1) * z.tiles))
    sums = loop(add_position, sums)
    stats = []
    for tile in range(z.tiles):
        value = zero
        for condition in range(z.conditions + 1):
            stat = jnp.sum(sums[condition * z.tiles + tile], axis=0, keepdims=True)
            value = jnp.where(row == condition, stat, value)
        stats.append(value)
    stats = jnp.concatenate(stats, axis=0)
    lanes = iota((z.own, LANES), 1)
    place = iota(orders.shape, 1)
    for step, out_ref in enumerate(out_refs):
        energy = jnp.zeros((z.own, LANES), f32)
        position = jnp.bitwise_xor(me, step)
        signal = signal_of(position)
        own = jnp.where(place == position, orders, 0)
        own = jnp.sum(own, axis=1, keepdims=True)
        before = jnp.where(place == position - 1, orders, 0)
        before = jnp.sum(before, axis=1, keepdims=True)
        for condition in range(z.conditions):
            if condition == 0:
                here, ahead = position, position - 1
            else:
                here, ahead = own[condition - 1, 0], before[condition - 1, 0]
            value = squares(signal, here, jnp.where(position == 0, z.n, ahead))
            value = sum(
                value[tile * z.own : (tile + 1) * z.own] for tile in range(z.tiles)
            )
            value = jnp.sum(value, axis=1, keepdims=True) * (1.0 / z.voxels)
            energy = jnp.where(lanes == condition, value, energy)
        out_ref[: z.own, :] = energy
        out_ref[z.own :, :] = stats


def fourth_kernel(z, mean_ref, *refs):
    parts, (energy_ref, scores_ref) = refs[:GROUP], refs[GROUP:]
    sums = sum(p[z.own :, :] for p in parts)
    tiles = [sums[start : start + 8] for start in range(0, z.tiles * 8, 8)]
    fit = [
        jnp.log((x + EPSILON) / (x[z.conditions : z.conditions + 1] + EPSILON))
        for x in tiles
    ]
    terms = [t.astype(f32) for t in thirds(jnp.concatenate(fit, axis=1))]
    score = dot(jnp.concatenate(terms, axis=0).astype(bf16), mean_ref[...])
    member = lax.rem(lax.axis_index("tr"), GROUP)
    turned = jnp.transpose(jnp.concatenate([p[: z.own, :] for p in parts], axis=0))
    column = iota((z.rows, LANES), 0)
    owner = jnp.bitwise_xor(column // z.own, member)
    order = iota((z.rows, LANES), 1) == owner + GROUP * (column % z.own)
    order = order.astype(f32).astype(bf16)
    terms = [t.astype(f32) for t in thirds(turned[:8, : z.rows])]
    energy = dot(jnp.concatenate(terms, axis=0).astype(bf16), order)
    energy = energy[:8] + energy[8:16] + energy[16:]
    score = score[:8] + score[8:16] + score[16:]
    for index in range(z.conditions):
        energy_ref[index] = energy[index : index + 1, : z.rows]
        scores_ref[index] = score[index : index + 1, :CAP]


def on_device(features, block_orders, offsets, tap_gains, weights, signal, block_owner):
    z = Sizes(features, block_orders, offsets, weights, block_owner)
    owners = block_owner.reshape(1, z.blocks)
    others = [
        lax.ppermute(
            features,
            "subj",
            [((i + step) % z.subjects, i) for i in range(z.subjects)],
        )
        for step in range(1, z.subjects)
    ]
    term_lanes = -(-3 * z.rows // LANES) * LANES
    work = 2 * z.ext * z.width * z.voxels
    messages = GROUP * z.message
    shapes = [
        jax.ShapeDtypeStruct((z.bands, z.ext, term_lanes), bf16),
        jax.ShapeDtypeStruct((messages, LANES), f32),
        jax.ShapeDtypeStruct((z.voxels, LANES), bf16),
        jax.ShapeDtypeStruct((z.ext, z.voxels), f32),
        jax.ShapeDtypeStruct((z.columns - z.width, z.voxels), bf16),
        jax.ShapeDtypeStruct(block_orders.shape, i32),
    ]
    scratch = [
        pltpu.SMEM(offsets.shape, i32),
        pltpu.SMEM(tap_gains.shape, f32),
        pltpu.VMEM(owners.shape, i32),
        pltpu.VMEM(features.shape, bf16),
        pltpu.VMEM((z.width, z.voxels), bf16),
        pltpu.VMEM((z.rows, z.voxels), bf16),
        pltpu.VMEM((messages, z.tiles * (z.rows + 8)), bf16),
        pltpu.SemaphoreType.DMA((6 + z.subjects,)),
    ]
    operands = (offsets, tap_gains, owners, features, weights[0], signal[0], block_orders)
    operands = [pltpu.with_memory_space_constraint(x, pltpu.HBM) for x in operands]
    table, base, mean, total, rest, orders = pl.pallas_call(
        functools.partial(first_kernel, z),
        out_shape=shapes,
        in_specs=[HBM] * 7,
        out_specs=[VMEM] * 6,
        scratch_shapes=scratch,
        compiler_params=params(),
        cost_estimate=cost(work, 3 << 20),
        name="prepare_and_own_columns",
    )(*operands)
    outgoing = pl.pallas_call(
        functools.partial(second_kernel, z),
        out_shape=jax.ShapeDtypeStruct((z.n, z.message, LANES), jnp.int16),
        in_specs=[VMEM] * (4 + len(others)),
        out_specs=VMEM,
        compiler_params=params(),
        cost_estimate=cost(work, 2 << 20),
        name="other_columns",
    )(table, rest, total, base, *others)
    received = lax.all_to_all(outgoing, "tr", 0, 0, tiled=True)
    more = [pltpu.SMEM(block_orders.shape, i32), pltpu.SemaphoreType.DMA]
    more = more if z.n > 16 else []
    part = jax.ShapeDtypeStruct((z.own + z.tiles * 8, LANES), f32)
    parts = pl.pallas_call(
        functools.partial(third_kernel, z),
        out_shape=[part] * GROUP,
        in_specs=[VMEM] * 2,
        out_specs=[VMEM] * GROUP,
        scratch_shapes=[
            pltpu.VMEM((z.n, z.tiles * z.own, LANES), f32),
            pltpu.VMEM((z.n + 1, z.tiles * 8, LANES), f32),
            *more,
        ],
        compiler_params=params(),
        cost_estimate=cost(work, 1 << 20),
        name="residuals",
    )(orders, received)
    parts = [parts[0]] + [
        lax.ppermute(parts[step], "tr", [(i, i ^ step) for i in range(z.n)])
        for step in range(1, GROUP)
    ]
    energy, scores = pl.pallas_call(
        functools.partial(fourth_kernel, z),
        out_shape=[
            jax.ShapeDtypeStruct((z.conditions, 1, z.rows), f32),
            jax.ShapeDtypeStruct((z.conditions, 1, CAP), f32),
        ],
        in_specs=[VMEM] * (1 + GROUP),
        out_specs=[VMEM, VMEM],
        compiler_params=params(),
        cost_estimate=cost(1 << 20, 1 << 16),
        name="scores",
    )(mean, *parts)
    return energy.transpose(1, 2, 0), scores.transpose(1, 2, 0)


def solution(mesh):
    placed = (
        P("tr", "subj"),
        P(),
        P(),
        P(),
        P("subj", None, None),
        P("subj", "tr", None),
        P("subj", None, None),
    )
    return jax.shard_map(
        on_device,
        mesh=mesh,
        in_specs=placed,
        out_specs=(P("subj", "tr", None), P("subj", "tr", None)),
        check_vma=False,
    )
```

```python
import functools

import jax
import jax.numpy as jnp
from jax import lax
from jax.experimental import pallas as pl
from jax.experimental.pallas import tpu as pltpu
from jax.sharding import PartitionSpec as P

MAXLAG = 8
VB = 4
CAP = 8
LANES = 128
GROUP = 2
EPSILON = 1e-6

f32 = jnp.float32
bf16 = jnp.bfloat16
i32 = jnp.int32

VMEM = pl.BlockSpec(memory_space=pltpu.VMEM)
HBM = pl.BlockSpec(memory_space=pltpu.HBM)


def iota(shape, axis):
    return lax.broadcasted_iota(i32, shape, axis)


def dot(a, b):
    return jnp.dot(a, b, preferred_element_type=f32)


def thirds(x):
    first = x.astype(bf16)
    rest = x - first.astype(f32)
    second = rest.astype(bf16)
    return first, second, (rest - second.astype(f32)).astype(bf16)


def params(**more):
    return pltpu.CompilerParams(vmem_limit_bytes=48 * 1024 * 1024, **more)


def cost(flops, nbytes):
    return pl.CostEstimate(flops=flops, bytes_accessed=nbytes, transcendentals=0)


class Sizes:
    def __init__(self, features, block_orders, offsets, weights, block_owner):
        self.subjects = lax.axis_size("subj")
        self.n = lax.axis_size("tr")
        self.rows, self.width = features.shape
        self.columns, self.voxels = weights.shape[1:]
        self.bands, self.taps = offsets.shape
        self.band_width = self.columns // self.bands
        self.piece = min(self.width, self.band_width)
        self.conditions = block_orders.shape[0] + 1
        self.blocks = block_owner.shape[1]
        self.ext = self.rows + MAXLAG
        self.own = self.rows // GROUP
        self.own_tail = MAXLAG // GROUP
        self.tiles = self.voxels // LANES
        self.groups = self.n // GROUP
        self.half = self.own // 2
        self.tail_at = self.tiles * self.own
        self.scale_at = self.tail_at + self.tiles * self.own_tail
        self.signal_scale = self.tiles
        self.signal_at = self.scale_at + -(-(self.tiles + 1) // 8) * 8
        self.message = self.signal_at + self.half
        self.source = self.own + 16
        assert GROUP * CAP * VB * 2 == LANES and self.n % GROUP == 0
        assert self.half % 8 == 0 and self.conditions < 8 and self.own_tail < 8
        assert self.tiles * self.own_tail % 8 == 0


def coded(x):
    largest = jnp.max(jnp.abs(x), axis=0, keepdims=True)
    power = jnp.floor(jnp.log2(jnp.maximum(largest, 2.0**-100))) + 1.0
    value = jnp.round(x * jnp.exp2(15.0 - power))
    return jnp.clip(value, -32767.0, 32767.0), power


def fill_signal(z, rows_ref, all_columns, base_ref):
    pieces = []
    for member in range(GROUP):
        for part in range(2):
            start = member + GROUP * part * z.half
            piece = [
                rows_ref[pl.ds(tile * z.rows + start, z.half, stride=GROUP), :]
                for tile in range(z.tiles)
            ]
            pieces.append(jnp.concatenate(piece, axis=1))
    value, power = coded(jnp.concatenate(pieces, axis=0))
    upper = jnp.floor(value * (1.0 / 256.0))
    lower = value - 256.0 * upper
    powers = jnp.broadcast_to(power, (8, z.voxels))
    terms = jnp.concatenate([upper, lower, powers], axis=0).astype(bf16)
    picked = dot(terms, all_columns)
    value = 256.0 * picked[: z.rows] + picked[z.rows : 2 * z.rows]
    left = iota((z.half, LANES), 1) < LANES // 2
    row = iota((z.signal_at - z.scale_at, LANES), 0)
    for index in range(z.n):
        lanes = slice(index // GROUP * LANES, (index // GROUP + 1) * LANES)
        start = (index % GROUP) * z.own
        first = value[start : start + z.half, lanes]
        second = value[start + z.half : start + z.own, lanes]
        power = picked[2 * z.rows : 2 * z.rows + 1, lanes]
        power = jnp.where(row == z.signal_scale, power, 0.0)
        body = jnp.where(left, first, second)
        base_ref[index] = jnp.concatenate([power, body], axis=0)


def filtered_product(z, x_ref, w_ref, table_ref, source):
    total = jnp.zeros((z.ext, z.voxels), f32)
    early = iota((8, z.piece), 0) < z.own_tail
    for part in range(z.width // z.piece):
        columns = slice(part * z.piece, (part + 1) * z.piece)
        x = x_ref[:, columns]
        table = table_ref[lax.div(source * z.width + part * z.piece, z.band_width)]
        stacked = jnp.concatenate([x] * (table.shape[1] // z.rows), axis=0)
        filtered = dot(table, stacked)
        low = filtered - filtered.astype(bf16).astype(f32)
        edges = [filtered]
        for start in range(0, z.rows, z.own):
            edges.append(jnp.where(early, low[start : start + 8], 0.0))
        edges.append(low[z.rows :])
        edges = jnp.concatenate(edges, axis=0).astype(bf16)
        product = dot(edges, w_ref[columns, :])
        parts = []
        for member in range(GROUP):
            start, at = member * z.own, z.ext + member * 8
            parts.append(product[start : start + 8] + product[at : at + 8])
            parts.append(product[start + 8 : start + z.own])
        parts.append(product[z.rows : z.ext] + product[z.ext + GROUP * 8 :])
        total = total + jnp.concatenate(parts, axis=0)
    return total


def fill_table(z, offsets_ref, gains_ref, table_ref):
    lanes = table_ref.shape[2]
    column = iota((z.ext, lanes), 1)
    row = iota((z.ext, 1), 0)
    after = row - z.rows
    time = row // z.own + GROUP * (row % z.own)
    time_after = z.rows + after // z.own_tail + GROUP * (after % z.own_tail)
    lag = jnp.where(after < 0, time, time_after) - column % z.rows
    term = column // z.rows
    for band in range(z.bands):
        value = jnp.zeros((z.ext, lanes), f32)
        for tap in range(z.taps):
            hit = lag == offsets_ref[band, tap]
            value = value + jnp.where(hit, gains_ref[band, tap], 0.0)
        first, second, third = (t.astype(f32) for t in thirds(value))
        chosen = jnp.where(term == 0, first, jnp.where(term == 1, second, third))
        chosen = jnp.where(term > 2, 0.0, chosen)
        table_ref[band] = chosen.astype(bf16)


def owned_columns(z, owners_ref):
    owners = owners_ref[...]
    other = iota((z.voxels, z.blocks), 1)
    block = iota((z.voxels, 1), 0) // VB
    owner = jnp.sum(jnp.where(other == block, owners, 0), axis=1, keepdims=True)
    before = (owners == owner) & (other < block)
    rank = jnp.sum(before.astype(i32), axis=1, keepdims=True)
    place = (owner * CAP + rank) * VB + iota((z.voxels, 1), 0) % VB
    lane = iota((1, z.groups * LANES), 1)
    half = LANES // 2
    every = place == lane // LANES * half + lane % half
    group = lax.axis_index("tr") // GROUP
    mine = place == group * half + iota((1, LANES), 1) % half
    return every.astype(f32).astype(bf16), mine.astype(f32)


def first_kernel(
    z, offsets_hbm, gains_hbm, owners_hbm, x_hbm, w_hbm, signal_hbm, orders_hbm,
    table_ref, base_ref, mine_ref, total_ref, rest_ref, orders_ref, signal_ref,
    offsets_ref, gains_ref, owners_ref, x_ref, w_ref, rows_ref, sems,
):
    me = lax.axis_index("subj")

    def weight_rows(step):
        source = lax.rem(me + step, z.subjects)
        start = pl.multiple_of(source * z.width, z.width)
        return w_hbm.at[pl.ds(start, z.width), :]

    moves = [
        (offsets_hbm, offsets_ref),
        (gains_hbm, gains_ref),
        (x_hbm, x_ref),
        (weight_rows(0), w_ref),
        (owners_hbm, owners_ref),
        (signal_hbm, signal_ref),
        (orders_hbm, orders_ref),
    ]
    for step in range(1, z.subjects):
        rows = pl.ds((step - 1) * z.width, z.width)
        moves.append((weight_rows(step), rest_ref.at[rows, :]))
    copies = [
        pltpu.make_async_copy(origin, target, sems.at[index])
        for index, (origin, target) in enumerate(moves)
    ]
    for copy in copies:
        copy.start()
    copies[0].wait()
    copies[1].wait()
    fill_table(z, offsets_ref, gains_ref, table_ref)
    copies[2].wait()
    copies[3].wait()
    total_ref[...] = filtered_product(z, x_ref, w_ref, table_ref, me)
    copies[4].wait()
    every, mine = owned_columns(z, owners_ref)
    mine = jnp.concatenate([256.0 * mine, mine], axis=0)
    mine_ref[...] = mine.astype(bf16)
    copies[5].wait()
    for tile in range(z.tiles):
        lanes = slice(tile * LANES, (tile + 1) * LANES)
        rows = slice(tile * z.rows, (tile + 1) * z.rows)
        rows_ref[rows, :] = signal_ref[:, lanes].astype(f32)
    fill_signal(z, rows_ref, every, base_ref)
    for copy in copies[6:]:
        copy.wait()


def second_kernel(
    z, table_ref, w_ref, total_ref, base_ref, signal_ref, sibling_ref, *refs
):
    others, (out_ref, own_signal_ref) = refs[:-2], refs[-2:]
    me = lax.axis_index("subj")
    total = total_ref[...]
    for step, x_ref in enumerate(others):
        source = lax.rem(me + step + 1, z.subjects)
        rows = w_ref.at[step * z.width : (step + 1) * z.width, :]
        total = total + filtered_product(z, x_ref, rows, table_ref, source)
    value, power = coded(total)
    row = iota((8, LANES), 0)
    for member in range(GROUP):
        shared = []
        for tile in range(z.tiles):
            lanes = slice(tile * LANES, (tile + 1) * LANES)
            shared.append(value[member * z.own : (member + 1) * z.own, lanes])
        tails = [jnp.zeros((8, LANES), f32)] * (z.tiles * z.own_tail // 8)
        for tile in range(z.tiles):
            lanes = slice(tile * LANES, (tile + 1) * LANES)
            which, place = divmod(tile * z.own_tail, 8)
            shift = (place - member * z.own_tail) % 8
            tail = pltpu.roll(value[z.rows :, lanes], shift, 0)
            here = (row >= place) & (row < place + z.own_tail)
            tails[which] = jnp.where(here, tail, tails[which])
        powers = jnp.zeros((z.signal_at - z.scale_at, LANES), f32)
        place = iota(powers.shape, 0)
        for tile in range(z.tiles):
            lanes = slice(tile * LANES, (tile + 1) * LANES)
            powers = jnp.where(place == tile, power[:, lanes], powers)
        for index in range(member, z.n, GROUP):
            base = base_ref[index]
            last = [base[: powers.shape[0]] + powers, base[powers.shape[0] :]]
            message = jnp.concatenate(shared + tails + last, axis=0)
            out_ref[index] = message.astype(i32).astype(jnp.int16)
    member = lax.rem(lax.axis_index("tr"), GROUP)
    shape = (z.own, z.rows)
    pick = iota(shape, 1) == GROUP * iota(shape, 0) + member
    pick = pick.astype(f32).astype(bf16)
    own_signal_ref[0] = dot(pick, signal_ref[...])
    own_signal_ref[1] = dot(pick, sibling_ref[...])


def third_kernel(z, orders_in_ref, mine_ref, own_signal_ref, received_ref, *refs):
    out_refs, (terms_ref, placed_ref, block_ref, tail_ref, *more) = (
        refs[:GROUP],
        refs[GROUP:],
    )
    orders = orders_in_ref[...]
    if more:
        orders_ref, sem = more
        copy = pltpu.make_async_copy(orders_in_ref, orders_ref, sem)
        copy.start()
    me = lax.axis_index("tr")
    row = iota((8, LANES), 0)
    left = iota((z.half, LANES), 1) < LANES // 2

    def integers(index, start, stop):
        return received_ref[index, start:stop, :].astype(i32)

    def numbers(index, start, stop):
        return integers(index, start, stop).astype(f32)

    def tails_of(x):
        tails = []
        for tile in range(z.tiles):
            which, place = divmod(tile * z.own_tail, 8)
            tail = x[which * 8 : which * 8 + 8]
            tails.append(pltpu.roll(tail, (8 - place) % 8, 0))
        return tails

    def unpack(index, carry):
        start = index * z.source
        start = start if isinstance(start, int) else pl.multiple_of(start, 16)
        body = integers(index, 0, z.tail_at)
        tails = tails_of(numbers(index, z.tail_at, z.scale_at))
        powers = numbers(index, z.scale_at, z.signal_at)
        for tile in range(z.tiles):
            x = body[tile * z.own : (tile + 1) * z.own]
            upper = lax.shift_right_arithmetic(x, jnp.full_like(x, 8))
            lower = x - upper * 256
            tail = tails[tile]
            high = jnp.floor(tail * (1.0 / 256.0))
            low = tail - 256.0 * high
            power = powers[tile : tile + 1]
            none = jnp.zeros((8, LANES), f32)
            power = jnp.broadcast_to(power, none.shape)
            first = jnp.concatenate([upper.astype(f32), high, none], axis=0)
            second = jnp.concatenate([lower.astype(f32), low, power], axis=0)
            lanes = slice(tile * LANES, (tile + 1) * LANES)
            terms_ref[pl.ds(start, z.source), lanes] = first.astype(bf16)
            lanes = slice(z.voxels + lanes.start, z.voxels + lanes.stop)
            terms_ref[pl.ds(start, z.source), lanes] = second.astype(bf16)
        return carry

    def place_block(index, carry):
        start = index * z.source
        start = start if isinstance(start, int) else pl.multiple_of(start, 16)
        x = placed_ref[pl.ds(start, z.source), :]
        scale = jnp.exp2(x[z.own + 8 : z.own + 9] - 15.0)
        block_ref[index] = jnp.where(left, x[: z.half], x[z.half : z.own]) * scale
        first = left[:8] & (row < z.own_tail)
        tail_ref[index] = jnp.where(first, x[z.own : z.own + 8] * scale, 0.0)
        return carry

    def add_position(position, sums):
        added = []
        at = z.scale_at + z.signal_scale
        power = numbers(position, at // 8 * 8, z.signal_at)[at % 8 : at % 8 + 1]
        signal = numbers(position, z.signal_at, z.message) * jnp.exp2(power - 15.0)
        before = jnp.maximum(position - 1, 0)
        for condition in range(z.conditions + 1):
            if condition == z.conditions:
                residual = signal
            else:
                if condition == 0:
                    here, ahead = position, before
                elif more:
                    here = orders_ref[condition - 1, position]
                    ahead = orders_ref[condition - 1, before]
                else:
                    here = orders[condition - 1, position]
                    ahead = orders[condition - 1, max(position - 1, 0)]
                tail = tail_ref[jnp.where(position == 0, z.n, ahead)]
                residual = signal - block_ref[here]
                parts = [residual[:8] - tail, residual[8:]]
                residual = jnp.concatenate(parts, axis=0)
            value = residual * residual
            total = sums[condition]
            for start in range(0, z.half, 8):
                total = total + value[start : start + 8]
            added.append(total)
        return tuple(added)

    def loop(body, carry):
        if more:
            return lax.fori_loop(0, z.n, body, carry)
        for index in range(z.n):
            carry = body(index, carry)
        return carry

    def scales_of(index):
        powers = numbers(index, z.scale_at, z.signal_at)
        return jnp.exp2(powers[: z.tiles] - 15.0)

    def energy_of(step, here, ahead, kept):
        scale, scale_ahead = scales_of(here), scales_of(ahead) * kept
        body = numbers(here, 0, z.tail_at)
        tails = tails_of(numbers(ahead, z.tail_at, z.scale_at))
        total = jnp.zeros((z.own, LANES), f32)
        for tile in range(z.tiles):
            lanes = slice(tile * LANES, (tile + 1) * LANES)
            block = body[tile * z.own : (tile + 1) * z.own] * scale[tile : tile + 1]
            residual = own_signal_ref[step, :, lanes] - block
            tail = tails[tile] * scale_ahead[tile : tile + 1]
            tail = jnp.where(row < z.own_tail, tail, 0.0)
            residual = jnp.concatenate([residual[:8] - tail, residual[8:]], axis=0)
            total = total + residual * residual
        return jnp.sum(total, axis=1, keepdims=True)

    loop(unpack, 0)
    chunk = 16 * z.source
    for start in range(0, z.n * z.source, chunk):
        stop = min(start + chunk, z.n * z.source)
        placed_ref[start:stop, :] = dot(terms_ref[start:stop, :], mine_ref[...])
    lanes = iota((z.own, LANES), 1)
    place = iota(orders.shape, 1)
    energies = []
    for step in range(GROUP):
        energy = jnp.zeros((z.own, LANES), f32)
        position = jnp.bitwise_xor(me, step)
        kept = jnp.where(position == 0, 0.0, 1.0)
        before = jnp.maximum(position - 1, 0)
        own = jnp.where(place == position, orders, 0)
        own = jnp.sum(own, axis=1, keepdims=True)
        preceding = jnp.where(place == before, orders, 0)
        preceding = jnp.sum(preceding, axis=1, keepdims=True)
        for condition in range(z.conditions):
            if condition == 0:
                here, ahead = position, before
            else:
                here, ahead = own[condition - 1, 0], preceding[condition - 1, 0]
            value = energy_of(step, here, ahead, kept) * (1.0 / z.voxels)
            energy = jnp.where(lanes == condition, value, energy)
        energies.append(energy)
    loop(place_block, 0)
    tail_ref[z.n] = jnp.zeros((8, LANES), f32)
    if more:
        copy.wait()
    zero = jnp.zeros((8, LANES), f32)
    sums = loop(add_position, (zero,) * (z.conditions + 1))
    stats = zero
    for condition, value in enumerate(sums):
        stat = jnp.sum(value, axis=0, keepdims=True)
        stats = jnp.where(row == condition, stat, stats)
    for energy, out_ref in zip(energies, out_refs):
        out_ref[: z.own, :] = energy
        out_ref[z.own :, :] = stats


def fourth_kernel(z, *refs):
    parts, (energy_ref, scores_ref) = refs[:GROUP], refs[GROUP:]
    member = lax.rem(lax.axis_index("tr"), GROUP)
    sums = sum(p[z.own :, :] for p in parts)
    sums = sums + pltpu.roll(sums, LANES // 2, 1)
    signal = sums[z.conditions : z.conditions + 1]
    fit = jnp.log((sums + EPSILON) / (signal + EPSILON))
    terms = [t.astype(f32) for t in thirds(fit)]
    square = (LANES, LANES)
    place = iota(square, 0) // VB - member * CAP
    mean = (place == iota(square, 1)) & (place >= 0) & (place < CAP)
    mean = mean & (iota(square, 0) < LANES // 2)
    mean = jnp.where(mean, 1.0 / VB, 0.0).astype(bf16)
    score = dot(jnp.concatenate(terms, axis=0).astype(bf16), mean)
    turned = jnp.transpose(jnp.concatenate([p[: z.own, :] for p in parts], axis=0))
    column = iota((z.rows, LANES), 0)
    owner = jnp.bitwise_xor(column // z.own, member)
    order = iota((z.rows, LANES), 1) == owner + GROUP * (column % z.own)
    order = order.astype(f32).astype(bf16)
    terms = [t.astype(f32) for t in thirds(turned[:8, : z.rows])]
    energy = dot(jnp.concatenate(terms, axis=0).astype(bf16), order)
    energy = energy[:8] + energy[8:16] + energy[16:]
    score = score[:8] + score[8:16] + score[16:]
    for index in range(z.conditions):
        energy_ref[index] = energy[index : index + 1, : z.rows]
        scores_ref[index] = score[index : index + 1, :CAP]


def on_device(features, block_orders, offsets, tap_gains, weights, signal, block_owner):
    z = Sizes(features, block_orders, offsets, weights, block_owner)
    owners = block_owner.reshape(1, z.blocks)
    siblings = [(i, i ^ 1) for i in range(z.n)]
    others = [
        lax.ppermute(
            features,
            "subj",
            [((i + step) % z.subjects, i) for i in range(z.subjects)],
        )
        for step in range(1, z.subjects)
    ]
    sibling_signal = lax.ppermute(signal[0], "tr", siblings)
    term_lanes = -(-3 * z.rows // LANES) * LANES
    work = 2 * z.ext * z.width * z.voxels
    shapes = [
        jax.ShapeDtypeStruct((z.bands, z.ext, term_lanes), bf16),
        jax.ShapeDtypeStruct((z.n, z.message - z.scale_at, LANES), f32),
        jax.ShapeDtypeStruct((2 * z.voxels, LANES), bf16),
        jax.ShapeDtypeStruct((z.ext, z.voxels), f32),
        jax.ShapeDtypeStruct((z.columns - z.width, z.voxels), bf16),
        jax.ShapeDtypeStruct(block_orders.shape, i32),
        jax.ShapeDtypeStruct((z.rows, z.voxels), bf16),
    ]
    scratch = [
        pltpu.SMEM(offsets.shape, i32),
        pltpu.SMEM(tap_gains.shape, f32),
        pltpu.VMEM(owners.shape, i32),
        pltpu.VMEM(features.shape, bf16),
        pltpu.VMEM((z.width, z.voxels), bf16),
        pltpu.VMEM((z.tiles * z.rows, LANES), f32),
        pltpu.SemaphoreType.DMA((6 + z.subjects,)),
    ]
    operands = (offsets, tap_gains, owners, features, weights[0], signal[0], block_orders)
    operands = [pltpu.with_memory_space_constraint(x, pltpu.HBM) for x in operands]
    table, base, mine, total, rest, orders, signal = pl.pallas_call(
        functools.partial(first_kernel, z),
        out_shape=shapes,
        in_specs=[HBM] * len(operands),
        out_specs=[VMEM] * len(shapes),
        scratch_shapes=scratch,
        compiler_params=params(),
        cost_estimate=cost(work, 3 << 20),
        name="prepare_and_own_columns",
    )(*operands)
    outgoing, own_signal = pl.pallas_call(
        functools.partial(second_kernel, z),
        out_shape=[
            jax.ShapeDtypeStruct((z.n, z.message, LANES), jnp.int16),
            jax.ShapeDtypeStruct((GROUP, z.own, z.voxels), f32),
        ],
        in_specs=[VMEM] * (6 + len(others)),
        out_specs=[VMEM, VMEM],
        compiler_params=params(),
        cost_estimate=cost(work, 2 << 20),
        name="other_columns",
    )(table, rest, total, base, signal, sibling_signal, *others)
    received = lax.all_to_all(outgoing, "tr", 0, 0, tiled=True)
    more = [pltpu.SMEM(block_orders.shape, i32), pltpu.SemaphoreType.DMA]
    more = more if z.n > 16 else []
    part = jax.ShapeDtypeStruct((z.own + 8, LANES), f32)
    parts = pl.pallas_call(
        functools.partial(third_kernel, z),
        out_shape=[part] * GROUP,
        in_specs=[VMEM] * 4,
        out_specs=[VMEM] * GROUP,
        scratch_shapes=[
            pltpu.VMEM((z.n * z.source, 2 * z.voxels), bf16),
            pltpu.VMEM((z.n * z.source, LANES), f32),
            pltpu.VMEM((z.n, z.half, LANES), f32),
            pltpu.VMEM((z.n + 1, 8, LANES), f32),
            *more,
        ],
        compiler_params=params(),
        cost_estimate=cost(work, 1 << 20),
        name="residuals",
    )(orders, mine, own_signal, received)
    parts = [parts[0], lax.ppermute(parts[1], "tr", siblings)]
    energy, scores = pl.pallas_call(
        functools.partial(fourth_kernel, z),
        out_shape=[
            jax.ShapeDtypeStruct((z.conditions, 1, z.rows), f32),
            jax.ShapeDtypeStruct((z.conditions, 1, CAP), f32),
        ],
        in_specs=[VMEM] * GROUP,
        out_specs=[VMEM, VMEM],
        compiler_params=params(),
        cost_estimate=cost(1 << 20, 1 << 16),
        name="scores",
    )(*parts)
    return energy.transpose(1, 2, 0), scores.transpose(1, 2, 0)


def solution(mesh):
    placed = (
        P("tr", "subj"),
        P(),
        P(),
        P(),
        P("subj", None, None),
        P("subj", "tr", None),
        P("subj", None, None),
    )
    return jax.shard_map(
        on_device,
        mesh=mesh,
        in_specs=placed,
        out_specs=(P("subj", "tr", None), P("subj", "tr", None)),
        check_vma=False,
    )
```

```python
import functools

import jax
import jax.numpy as jnp
from jax import lax
from jax.experimental import pallas as pl
from jax.experimental.pallas import tpu as pltpu
from jax.sharding import PartitionSpec as P

MAXLAG = 8
VB = 4
CAP = 8
LANES = 128
GROUP = 2
EPSILON = 1e-6

f32 = jnp.float32
bf16 = jnp.bfloat16
i32 = jnp.int32

VMEM = pl.BlockSpec(memory_space=pltpu.VMEM)
HBM = pl.BlockSpec(memory_space=pltpu.HBM)


def iota(shape, axis):
    return lax.broadcasted_iota(i32, shape, axis)


def dot(a, b):
    return jnp.dot(a, b, preferred_element_type=f32)


def thirds(x):
    first = x.astype(bf16)
    rest = x - first.astype(f32)
    second = rest.astype(bf16)
    return first, second, (rest - second.astype(f32)).astype(bf16)


def params(**more):
    return pltpu.CompilerParams(vmem_limit_bytes=48 * 1024 * 1024, **more)


def cost(flops, nbytes):
    return pl.CostEstimate(flops=flops, bytes_accessed=nbytes, transcendentals=0)


class Sizes:
    def __init__(self, features, block_orders, offsets, weights, block_owner):
        self.subjects = lax.axis_size("subj")
        self.n = lax.axis_size("tr")
        self.rows, self.width = features.shape
        self.columns, self.voxels = weights.shape[1:]
        self.bands, self.taps = offsets.shape
        self.band_width = self.columns // self.bands
        self.piece = min(self.width, self.band_width)
        self.conditions = block_orders.shape[0] + 1
        self.blocks = block_owner.shape[1]
        self.ext = self.rows + MAXLAG
        self.own = self.rows // GROUP
        self.own_tail = MAXLAG // GROUP
        self.tiles = self.voxels // LANES
        self.groups = self.n // GROUP
        self.half = self.own // 2
        self.tail_at = self.tiles * self.own
        self.signal_at = self.tail_at + self.tiles * self.own_tail
        self.message = self.signal_at + self.half
        self.pair = 2 * (self.own + 8)
        assert GROUP * CAP * VB * 2 == LANES and self.n % GROUP == 0
        assert self.half % 8 == 0 and self.conditions < 8 and 8 % self.own_tail == 0
        assert self.tiles * self.own_tail % 8 == 0


BITS, LEAST = 7, -126
STEPS, SMALLEST = 512.0, -50.0


def coded_signal(x):
    size = jnp.abs(x)
    power = jnp.floor(jnp.log2(jnp.maximum(size, 2.0**LEAST)))
    half = jnp.floor(power * 0.5)
    significand = size * jnp.exp2(-half) * jnp.exp2(half - power)
    code = jnp.round((power - LEAST + significand - 1.0) * 2.0**BITS)
    code = jnp.clip(code, 0.0, 32767.0)
    return jnp.where(x < 0.0, -code, code)


def decoded_signal(code):
    size = jnp.abs(code)
    power = lax.shift_right_logical(size, jnp.full_like(size, BITS))
    significand = (size & (2**BITS - 1)) + 2**BITS
    scale = jnp.exp2((power + (LEAST - BITS)).astype(f32))
    value = significand.astype(f32) * scale
    return jnp.where(code < 0, -value, value)


def coded_prediction(x):
    size = jnp.maximum(jnp.abs(x), 2.0**SMALLEST)
    code = jnp.round((jnp.log2(size) - SMALLEST) * STEPS)
    code = jnp.minimum(code, 32767.0)
    return jnp.where(x < 0.0, -code, code)


def decoded_prediction(code):
    value = jnp.exp2(jnp.abs(code) * (1.0 / STEPS) + SMALLEST)
    return jnp.where(code < 0.0, -value, value)


def fill_signal(z, rows_ref, all_columns, base_ref):
    pieces = []
    for member in range(GROUP):
        for part in range(2):
            start = member + GROUP * part * z.half
            piece = [
                rows_ref[pl.ds(tile * z.rows + start, z.half, stride=GROUP), :]
                for tile in range(z.tiles)
            ]
            pieces.append(jnp.concatenate(piece, axis=1))
    value = coded_signal(jnp.concatenate(pieces, axis=0))
    upper = jnp.floor(value * (1.0 / 256.0))
    lower = value - 256.0 * upper
    picked = dot(jnp.concatenate([upper, lower], axis=0).astype(bf16), all_columns)
    value = 256.0 * picked[: z.rows] + picked[z.rows :]
    left = iota((z.half, LANES), 1) < LANES // 2
    for index in range(z.n):
        lanes = slice(index // GROUP * LANES, (index // GROUP + 1) * LANES)
        start = (index % GROUP) * z.own
        first = value[start : start + z.half, lanes]
        second = value[start + z.half : start + z.own, lanes]
        base_ref[index] = jnp.where(left, first, second)


def filtered_product(z, x_ref, w_ref, table_ref, source):
    total = jnp.zeros((z.ext, z.voxels), f32)
    early = iota((8, z.piece), 0) < z.own_tail
    for part in range(z.width // z.piece):
        columns = slice(part * z.piece, (part + 1) * z.piece)
        x = x_ref[:, columns]
        table = table_ref[lax.div(source * z.width + part * z.piece, z.band_width)]
        stacked = jnp.concatenate([x] * (table.shape[1] // z.rows), axis=0)
        filtered = dot(table, stacked)
        low = filtered - filtered.astype(bf16).astype(f32)
        edges = [filtered]
        for start in range(0, z.rows, z.own):
            edges.append(jnp.where(early, low[start : start + 8], 0.0))
        edges.append(low[z.rows :])
        edges = jnp.concatenate(edges, axis=0).astype(bf16)
        product = dot(edges, w_ref[columns, :])
        parts = []
        for member in range(GROUP):
            start, at = member * z.own, z.ext + member * 8
            parts.append(product[start : start + 8] + product[at : at + 8])
            parts.append(product[start + 8 : start + z.own])
        parts.append(product[z.rows : z.ext] + product[z.ext + GROUP * 8 :])
        total = total + jnp.concatenate(parts, axis=0)
    return total


def fill_table(z, offsets_ref, gains_ref, table_ref):
    lanes = table_ref.shape[2]
    column = iota((z.ext, lanes), 1)
    row = iota((z.ext, 1), 0)
    after = row - z.rows
    time = row // z.own + GROUP * (row % z.own)
    time_after = z.rows + after // z.own_tail + GROUP * (after % z.own_tail)
    lag = jnp.where(after < 0, time, time_after) - column % z.rows
    term = column // z.rows
    for band in range(z.bands):
        value = jnp.zeros((z.ext, lanes), f32)
        for tap in range(z.taps):
            hit = lag == offsets_ref[band, tap]
            value = value + jnp.where(hit, gains_ref[band, tap], 0.0)
        first, second, third = (t.astype(f32) for t in thirds(value))
        chosen = jnp.where(term == 0, first, jnp.where(term == 1, second, third))
        chosen = jnp.where(term > 2, 0.0, chosen)
        table_ref[band] = chosen.astype(bf16)


def owned_columns(z, owners_ref):
    owners = owners_ref[...]
    other = iota((z.voxels, z.blocks), 1)
    block = iota((z.voxels, 1), 0) // VB
    owner = jnp.sum(jnp.where(other == block, owners, 0), axis=1, keepdims=True)
    before = (owners == owner) & (other < block)
    rank = jnp.sum(before.astype(i32), axis=1, keepdims=True)
    place = (owner * CAP + rank) * VB + iota((z.voxels, 1), 0) % VB
    lane = iota((1, z.groups * LANES), 1)
    half = LANES // 2
    every = place == lane // LANES * half + lane % half
    group = lax.axis_index("tr") // GROUP
    mine = place == group * half + iota((1, LANES), 1) % half
    return every.astype(f32).astype(bf16), mine.astype(f32)


def first_kernel(
    z, offsets_hbm, gains_hbm, owners_hbm, x_hbm, w_hbm, signal_hbm, orders_hbm,
    table_ref, base_ref, mine_ref, total_ref, rest_ref, orders_ref, signal_ref,
    offsets_ref, gains_ref, owners_ref, x_ref, w_ref, rows_ref, sems,
):
    me = lax.axis_index("subj")

    def weight_rows(step):
        source = lax.rem(me + step, z.subjects)
        start = pl.multiple_of(source * z.width, z.width)
        return w_hbm.at[pl.ds(start, z.width), :]

    moves = [
        (offsets_hbm, offsets_ref),
        (gains_hbm, gains_ref),
        (x_hbm, x_ref),
        (weight_rows(0), w_ref),
        (owners_hbm, owners_ref),
        (signal_hbm, signal_ref),
        (orders_hbm, orders_ref),
    ]
    for step in range(1, z.subjects):
        rows = pl.ds((step - 1) * z.width, z.width)
        moves.append((weight_rows(step), rest_ref.at[rows, :]))
    copies = [
        pltpu.make_async_copy(origin, target, sems.at[index])
        for index, (origin, target) in enumerate(moves)
    ]
    for copy in copies:
        copy.start()
    copies[0].wait()
    copies[1].wait()
    fill_table(z, offsets_ref, gains_ref, table_ref)
    copies[2].wait()
    copies[3].wait()
    total_ref[...] = filtered_product(z, x_ref, w_ref, table_ref, me)
    copies[4].wait()
    every, mine = owned_columns(z, owners_ref)
    mine = jnp.concatenate([256.0 * mine, mine], axis=0)
    mine_ref[...] = mine.astype(bf16)
    copies[5].wait()
    for tile in range(z.tiles):
        lanes = slice(tile * LANES, (tile + 1) * LANES)
        rows = slice(tile * z.rows, (tile + 1) * z.rows)
        rows_ref[rows, :] = signal_ref[:, lanes].astype(f32)
    fill_signal(z, rows_ref, every, base_ref)
    for copy in copies[6:]:
        copy.wait()


def second_kernel(
    z, table_ref, w_ref, total_ref, base_ref, signal_ref, sibling_ref, *refs
):
    others, (out_ref, own_signal_ref) = refs[:-2], refs[-2:]
    me = lax.axis_index("subj")
    total = total_ref[...]
    for step, x_ref in enumerate(others):
        source = lax.rem(me + step + 1, z.subjects)
        rows = w_ref.at[step * z.width : (step + 1) * z.width, :]
        total = total + filtered_product(z, x_ref, rows, table_ref, source)
    value = coded_prediction(total)
    row = iota((8, LANES), 0)
    for member in range(GROUP):
        shared = []
        for tile in range(z.tiles):
            lanes = slice(tile * LANES, (tile + 1) * LANES)
            shared.append(value[member * z.own : (member + 1) * z.own, lanes])
        tails = [jnp.zeros((8, LANES), f32)] * (z.tiles * z.own_tail // 8)
        for tile in range(z.tiles):
            lanes = slice(tile * LANES, (tile + 1) * LANES)
            which, place = divmod(tile * z.own_tail, 8)
            shift = (place - member * z.own_tail) % 8
            tail = pltpu.roll(value[z.rows :, lanes], shift, 0)
            here = (row >= place) & (row < place + z.own_tail)
            tails[which] = jnp.where(here, tail, tails[which])
        for index in range(member, z.n, GROUP):
            message = jnp.concatenate(shared + tails + [base_ref[index]], axis=0)
            out_ref[index] = message.astype(i32).astype(jnp.int16)
    member = lax.rem(lax.axis_index("tr"), GROUP)
    shape = (z.own, z.rows)
    pick = iota(shape, 1) == GROUP * iota(shape, 0) + member
    pick = pick.astype(f32).astype(bf16)
    own_signal_ref[0] = dot(pick, signal_ref[...])
    own_signal_ref[1] = dot(pick, sibling_ref[...])


def third_kernel(z, orders_in_ref, mine_ref, own_signal_ref, received_ref, *refs):
    out_refs, (terms_ref, placed_ref, block_ref, tail_ref, *more) = (
        refs[:GROUP],
        refs[GROUP:],
    )
    orders = orders_in_ref[...]
    if more:
        orders_ref, sem = more
        copy = pltpu.make_async_copy(orders_in_ref, orders_ref, sem)
        copy.start()
    me = lax.axis_index("tr")
    row = iota((8, LANES), 0)
    left = iota((z.half, LANES), 1) < LANES // 2

    def integers(index, start, stop):
        return received_ref[index, start:stop, :].astype(i32)

    def tails_of(index):
        x = integers(index, z.tail_at, z.signal_at)
        tails = []
        for tile in range(z.tiles):
            which, place = divmod(tile * z.own_tail, 8)
            tail = pltpu.roll(x[which * 8 : which * 8 + 8], (8 - place) % 8, 0)
            tails.append(jnp.where(row < z.own_tail, tail, 0))
        return tails

    def unpack(pair, carry):
        start = pair * z.pair
        start = start if isinstance(start, int) else pl.multiple_of(start, 16)
        bodies = [integers(2 * pair + i, 0, z.tail_at) for i in range(2)]
        tails = [tails_of(2 * pair + i) for i in range(2)]
        for tile in range(z.tiles):
            rows = slice(tile * z.own, (tile + 1) * z.own)
            x = [body[rows] for body in bodies] + [tail[tile] for tail in tails]
            x = jnp.concatenate(x, axis=0)
            upper = lax.shift_right_arithmetic(x, jnp.full_like(x, 8))
            lower = x & 255
            lanes = slice(tile * LANES, (tile + 1) * LANES)
            terms_ref[pl.ds(start, z.pair), lanes] = upper.astype(f32).astype(bf16)
            lanes = slice(z.voxels + lanes.start, z.voxels + lanes.stop)
            terms_ref[pl.ds(start, z.pair), lanes] = lower.astype(f32).astype(bf16)
        return carry

    def place_pair(pair, carry):
        start = pair * z.pair
        start = start if isinstance(start, int) else pl.multiple_of(start, 16)
        x = placed_ref[pl.ds(start, z.pair), :]
        for i in range(2):
            first = x[i * z.own : i * z.own + z.half]
            second = x[i * z.own + z.half : (i + 1) * z.own]
            block = decoded_prediction(jnp.where(left, first, second))
            block_ref[2 * pair + i] = block
            at = 2 * z.own + 8 * i
            tail = decoded_prediction(x[at : at + 8])
            here = left[:8] & (row < z.own_tail)
            tail_ref[2 * pair + i] = jnp.where(here, tail, 0.0)
        return carry

    def add_position(position, sums):
        added = []
        signal = decoded_signal(integers(position, z.signal_at, z.message))
        before = jnp.maximum(position - 1, 0)
        for condition in range(z.conditions + 1):
            if condition == z.conditions:
                residual = signal
            else:
                if condition == 0:
                    here, ahead = position, before
                elif more:
                    here = orders_ref[condition - 1, position]
                    ahead = orders_ref[condition - 1, before]
                else:
                    here = orders[condition - 1, position]
                    ahead = orders[condition - 1, max(position - 1, 0)]
                tail = tail_ref[jnp.where(position == 0, z.n, ahead)]
                residual = signal - block_ref[here]
                parts = [residual[:8] - tail, residual[8:]]
                residual = jnp.concatenate(parts, axis=0)
            value = residual * residual
            total = sums[condition]
            for start in range(0, z.half, 8):
                total = total + value[start : start + 8]
            added.append(total)
        return tuple(added)

    def loop(count, body, carry):
        if more:
            return lax.fori_loop(0, count, body, carry)
        for index in range(count):
            carry = body(index, carry)
        return carry

    def energy_of(step, here, ahead, kept):
        body = decoded_prediction(integers(here, 0, z.tail_at).astype(f32))
        tails = tails_of(ahead)
        total = jnp.zeros((z.own, LANES), f32)
        for tile in range(z.tiles):
            lanes = slice(tile * LANES, (tile + 1) * LANES)
            block = body[tile * z.own : (tile + 1) * z.own]
            residual = own_signal_ref[step, :, lanes] - block
            tail = decoded_prediction(tails[tile].astype(f32)) * kept
            tail = jnp.where(row < z.own_tail, tail, 0.0)
            residual = jnp.concatenate([residual[:8] - tail, residual[8:]], axis=0)
            total = total + residual * residual
        return jnp.sum(total, axis=1, keepdims=True)

    loop(z.n // 2, unpack, 0)
    chunk = 8 * z.pair
    for start in range(0, z.n // 2 * z.pair, chunk):
        stop = min(start + chunk, z.n // 2 * z.pair)
        placed_ref[start:stop, :] = dot(terms_ref[start:stop, :], mine_ref[...])
    lanes = iota((z.own, LANES), 1)
    place = iota(orders.shape, 1)
    energies = []
    for step in range(GROUP):
        energy = jnp.zeros((z.own, LANES), f32)
        position = jnp.bitwise_xor(me, step)
        kept = jnp.where(position == 0, 0.0, 1.0)
        before = jnp.maximum(position - 1, 0)
        own = jnp.where(place == position, orders, 0)
        own = jnp.sum(own, axis=1, keepdims=True)
        preceding = jnp.where(place == before, orders, 0)
        preceding = jnp.sum(preceding, axis=1, keepdims=True)
        for condition in range(z.conditions):
            if condition == 0:
                here, ahead = position, before
            else:
                here, ahead = own[condition - 1, 0], preceding[condition - 1, 0]
            value = energy_of(step, here, ahead, kept) * (1.0 / z.voxels)
            energy = jnp.where(lanes == condition, value, energy)
        energies.append(energy)
    loop(z.n // 2, place_pair, 0)
    tail_ref[z.n] = jnp.zeros((8, LANES), f32)
    if more:
        copy.wait()
    zero = jnp.zeros((8, LANES), f32)
    sums = loop(z.n, add_position, (zero,) * (z.conditions + 1))
    stats = zero
    for condition, value in enumerate(sums):
        stat = jnp.sum(value, axis=0, keepdims=True)
        stats = jnp.where(row == condition, stat, stats)
    for energy, out_ref in zip(energies, out_refs):
        out_ref[: z.own, :] = energy
        out_ref[z.own :, :] = stats


def fourth_kernel(z, *refs):
    parts, (energy_ref, scores_ref) = refs[:GROUP], refs[GROUP:]
    member = lax.rem(lax.axis_index("tr"), GROUP)
    sums = sum(p[z.own :, :] for p in parts)
    sums = sums + pltpu.roll(sums, LANES // 2, 1)
    signal = sums[z.conditions : z.conditions + 1]
    fit = jnp.log((sums + EPSILON) / (signal + EPSILON))
    terms = [t.astype(f32) for t in thirds(fit)]
    square = (LANES, LANES)
    place = iota(square, 0) // VB - member * CAP
    mean = (place == iota(square, 1)) & (place >= 0) & (place < CAP)
    mean = mean & (iota(square, 0) < LANES // 2)
    mean = jnp.where(mean, 1.0 / VB, 0.0).astype(bf16)
    score = dot(jnp.concatenate(terms, axis=0).astype(bf16), mean)
    turned = jnp.transpose(jnp.concatenate([p[: z.own, :] for p in parts], axis=0))
    column = iota((z.rows, LANES), 0)
    owner = jnp.bitwise_xor(column // z.own, member)
    order = iota((z.rows, LANES), 1) == owner + GROUP * (column % z.own)
    order = order.astype(f32).astype(bf16)
    terms = [t.astype(f32) for t in thirds(turned[:8, : z.rows])]
    energy = dot(jnp.concatenate(terms, axis=0).astype(bf16), order)
    energy = energy[:8] + energy[8:16] + energy[16:]
    score = score[:8] + score[8:16] + score[16:]
    for index in range(z.conditions):
        energy_ref[index] = energy[index : index + 1, : z.rows]
        scores_ref[index] = score[index : index + 1, :CAP]


def on_device(features, block_orders, offsets, tap_gains, weights, signal, block_owner):
    z = Sizes(features, block_orders, offsets, weights, block_owner)
    owners = block_owner.reshape(1, z.blocks)
    siblings = [(i, i ^ 1) for i in range(z.n)]
    others = [
        lax.ppermute(
            features,
            "subj",
            [((i + step) % z.subjects, i) for i in range(z.subjects)],
        )
        for step in range(1, z.subjects)
    ]
    sibling_signal = lax.ppermute(signal[0], "tr", siblings)
    term_lanes = -(-3 * z.rows // LANES) * LANES
    work = 2 * z.ext * z.width * z.voxels
    shapes = [
        jax.ShapeDtypeStruct((z.bands, z.ext, term_lanes), bf16),
        jax.ShapeDtypeStruct((z.n, z.half, LANES), f32),
        jax.ShapeDtypeStruct((2 * z.voxels, LANES), bf16),
        jax.ShapeDtypeStruct((z.ext, z.voxels), f32),
        jax.ShapeDtypeStruct((z.columns - z.width, z.voxels), bf16),
        jax.ShapeDtypeStruct(block_orders.shape, i32),
        jax.ShapeDtypeStruct((z.rows, z.voxels), bf16),
    ]
    scratch = [
        pltpu.SMEM(offsets.shape, i32),
        pltpu.SMEM(tap_gains.shape, f32),
        pltpu.VMEM(owners.shape, i32),
        pltpu.VMEM(features.shape, bf16),
        pltpu.VMEM((z.width, z.voxels), bf16),
        pltpu.VMEM((z.tiles * z.rows, LANES), f32),
        pltpu.SemaphoreType.DMA((6 + z.subjects,)),
    ]
    operands = (offsets, tap_gains, owners, features, weights[0], signal[0], block_orders)
    operands = [pltpu.with_memory_space_constraint(x, pltpu.HBM) for x in operands]
    table, base, mine, total, rest, orders, signal = pl.pallas_call(
        functools.partial(first_kernel, z),
        out_shape=shapes,
        in_specs=[HBM] * len(operands),
        out_specs=[VMEM] * len(shapes),
        scratch_shapes=scratch,
        compiler_params=params(),
        cost_estimate=cost(work, 3 << 20),
        name="prepare_and_own_columns",
    )(*operands)
    outgoing, own_signal = pl.pallas_call(
        functools.partial(second_kernel, z),
        out_shape=[
            jax.ShapeDtypeStruct((z.n, z.message, LANES), jnp.int16),
            jax.ShapeDtypeStruct((GROUP, z.own, z.voxels), f32),
        ],
        in_specs=[VMEM] * (6 + len(others)),
        out_specs=[VMEM, VMEM],
        compiler_params=params(),
        cost_estimate=cost(work, 2 << 20),
        name="other_columns",
    )(table, rest, total, base, signal, sibling_signal, *others)
    received = lax.all_to_all(outgoing, "tr", 0, 0, tiled=True)
    more = [pltpu.SMEM(block_orders.shape, i32), pltpu.SemaphoreType.DMA]
    more = more if z.n > 16 else []
    part = jax.ShapeDtypeStruct((z.own + 8, LANES), f32)
    parts = pl.pallas_call(
        functools.partial(third_kernel, z),
        out_shape=[part] * GROUP,
        in_specs=[VMEM] * 4,
        out_specs=[VMEM] * GROUP,
        scratch_shapes=[
            pltpu.VMEM((z.n // 2 * z.pair, 2 * z.voxels), bf16),
            pltpu.VMEM((z.n // 2 * z.pair, LANES), f32),
            pltpu.VMEM((z.n, z.half, LANES), f32),
            pltpu.VMEM((z.n + 1, 8, LANES), f32),
            *more,
        ],
        compiler_params=params(),
        cost_estimate=cost(work, 1 << 20),
        name="residuals",
    )(orders, mine, own_signal, received)
    parts = [parts[0], lax.ppermute(parts[1], "tr", siblings)]
    energy, scores = pl.pallas_call(
        functools.partial(fourth_kernel, z),
        out_shape=[
            jax.ShapeDtypeStruct((z.conditions, 1, z.rows), f32),
            jax.ShapeDtypeStruct((z.conditions, 1, CAP), f32),
        ],
        in_specs=[VMEM] * GROUP,
        out_specs=[VMEM, VMEM],
        compiler_params=params(),
        cost_estimate=cost(1 << 20, 1 << 16),
        name="scores",
    )(*parts)
    return energy.transpose(1, 2, 0), scores.transpose(1, 2, 0)


def solution(mesh):
    placed = (
        P("tr", "subj"),
        P(),
        P(),
        P(),
        P("subj", None, None),
        P("subj", "tr", None),
        P("subj", None, None),
    )
    return jax.shard_map(
        on_device,
        mesh=mesh,
        in_specs=placed,
        out_specs=(P("subj", "tr", None), P("subj", "tr", None)),
        check_vma=False,
    )
```

```python
import functools

import jax
import jax.numpy as jnp
from jax import lax
from jax.experimental import pallas as pl
from jax.experimental.pallas import tpu as pltpu
from jax.sharding import PartitionSpec as P

MAXLAG = 8
VB = 4
CAP = 8
LANES = 128
GROUP = 2
EPSILON = 1e-6

f32 = jnp.float32
bf16 = jnp.bfloat16
i32 = jnp.int32

VMEM = pl.BlockSpec(memory_space=pltpu.VMEM)
HBM = pl.BlockSpec(memory_space=pltpu.HBM)


def iota(shape, axis):
    return lax.broadcasted_iota(i32, shape, axis)


def dot(a, b):
    return jnp.dot(a, b, preferred_element_type=f32)


def thirds(x):
    first = x.astype(bf16)
    rest = x - first.astype(f32)
    second = rest.astype(bf16)
    return first, second, (rest - second.astype(f32)).astype(bf16)


def params(**more):
    return pltpu.CompilerParams(vmem_limit_bytes=48 * 1024 * 1024, **more)


def cost(flops, nbytes):
    return pl.CostEstimate(flops=flops, bytes_accessed=nbytes, transcendentals=0)


class Sizes:
    def __init__(self, features, block_orders, offsets, weights, block_owner):
        self.subjects = lax.axis_size("subj")
        self.n = lax.axis_size("tr")
        self.rows, self.width = features.shape
        self.columns, self.voxels = weights.shape[1:]
        self.bands, self.taps = offsets.shape
        self.band_width = self.columns // self.bands
        self.piece = min(self.width, self.band_width)
        self.conditions = block_orders.shape[0] + 1
        self.blocks = block_owner.shape[1]
        self.ext = self.rows + MAXLAG
        self.own = self.rows // GROUP
        self.own_tail = MAXLAG // GROUP
        self.tiles = self.voxels // LANES
        self.groups = self.n // GROUP
        self.half = self.own // 2
        self.tail_at = self.tiles * self.own
        self.signal_at = self.tail_at + self.tiles * self.own_tail
        self.message = self.signal_at + self.half
        self.pair = 2 * (self.own + 8)
        assert GROUP * CAP * VB * 2 == LANES and self.n % GROUP == 0
        assert self.half % 8 == 0 and self.conditions < 8 and 8 % self.own_tail == 0
        assert self.tiles * self.own_tail % 8 == 0


BITS, LEAST = 7, -126
STEPS, SMALLEST = 668.0, -36.0


def coded_signal(x):
    size = jnp.abs(x)
    power = jnp.floor(jnp.log2(jnp.maximum(size, 2.0**LEAST)))
    half = jnp.floor(power * 0.5)
    significand = size * jnp.exp2(-half) * jnp.exp2(half - power)
    code = jnp.round((power - LEAST + significand - 1.0) * 2.0**BITS)
    code = jnp.clip(code, 0.0, 32767.0)
    return jnp.where(x < 0.0, -code, code)


def decoded_signal(code):
    size = jnp.abs(code)
    power = lax.shift_right_logical(size, jnp.full_like(size, BITS))
    significand = (size & (2**BITS - 1)) + 2**BITS
    scale = jnp.exp2((power + (LEAST - BITS)).astype(f32))
    value = significand.astype(f32) * scale
    return jnp.where(code < 0, -value, value)


def coded_prediction(x):
    size = jnp.maximum(jnp.abs(x), 2.0**SMALLEST)
    code = jnp.round((jnp.log2(size) - SMALLEST) * STEPS)
    code = jnp.minimum(code, 32767.0)
    return jnp.where(x < 0.0, -code, code)


def decoded_prediction(code):
    value = jnp.exp2(jnp.abs(code) * (1.0 / STEPS) + SMALLEST)
    return jnp.where(code < 0.0, -value, value)


def fill_signal(z, rows_ref, all_columns, base_ref):
    pieces = []
    for member in range(GROUP):
        for part in range(2):
            start = member + GROUP * part * z.half
            piece = [
                rows_ref[pl.ds(tile * z.rows + start, z.half, stride=GROUP), :]
                for tile in range(z.tiles)
            ]
            pieces.append(jnp.concatenate(piece, axis=1))
    value = coded_signal(jnp.concatenate(pieces, axis=0))
    upper = jnp.floor(value * (1.0 / 256.0))
    lower = value - 256.0 * upper
    picked = dot(jnp.concatenate([upper, lower], axis=0).astype(bf16), all_columns)
    value = 256.0 * picked[: z.rows] + picked[z.rows :]
    left = iota((z.half, LANES), 1) < LANES // 2
    for index in range(z.n):
        lanes = slice(index // GROUP * LANES, (index // GROUP + 1) * LANES)
        start = (index % GROUP) * z.own
        first = value[start : start + z.half, lanes]
        second = value[start + z.half : start + z.own, lanes]
        base_ref[index] = jnp.where(left, first, second)


def filtered_product(z, x_ref, w_ref, table_ref, source):
    total = jnp.zeros((z.ext, z.voxels), f32)
    early = iota((8, z.piece), 0) < z.own_tail
    for part in range(z.width // z.piece):
        columns = slice(part * z.piece, (part + 1) * z.piece)
        x = x_ref[:, columns]
        table = table_ref[lax.div(source * z.width + part * z.piece, z.band_width)]
        stacked = jnp.concatenate([x] * (table.shape[1] // z.rows), axis=0)
        filtered = dot(table, stacked)
        low = filtered - filtered.astype(bf16).astype(f32)
        edges = [filtered]
        for start in range(0, z.rows, z.own):
            edges.append(jnp.where(early, low[start : start + 8], 0.0))
        edges.append(low[z.rows :])
        edges = jnp.concatenate(edges, axis=0).astype(bf16)
        product = dot(edges, w_ref[columns, :])
        parts = []
        for member in range(GROUP):
            start, at = member * z.own, z.ext + member * 8
            parts.append(product[start : start + 8] + product[at : at + 8])
            parts.append(product[start + 8 : start + z.own])
        parts.append(product[z.rows : z.ext] + product[z.ext + GROUP * 8 :])
        total = total + jnp.concatenate(parts, axis=0)
    return total


def fill_table(z, offsets_ref, gains_ref, table_ref):
    lanes = table_ref.shape[2]
    column = iota((z.ext, lanes), 1)
    row = iota((z.ext, 1), 0)
    after = row - z.rows
    time = row // z.own + GROUP * (row % z.own)
    time_after = z.rows + after // z.own_tail + GROUP * (after % z.own_tail)
    lag = jnp.where(after < 0, time, time_after) - column % z.rows
    term = column // z.rows
    for band in range(z.bands):
        value = jnp.zeros((z.ext, lanes), f32)
        for tap in range(z.taps):
            hit = lag == offsets_ref[band, tap]
            value = value + jnp.where(hit, gains_ref[band, tap], 0.0)
        first, second, third = (t.astype(f32) for t in thirds(value))
        chosen = jnp.where(term == 0, first, jnp.where(term == 1, second, third))
        chosen = jnp.where(term > 2, 0.0, chosen)
        table_ref[band] = chosen.astype(bf16)


def owned_columns(z, owners_ref):
    owners = owners_ref[...]
    other = iota((z.voxels, z.blocks), 1)
    block = iota((z.voxels, 1), 0) // VB
    owner = jnp.sum(jnp.where(other == block, owners, 0), axis=1, keepdims=True)
    before = (owners == owner) & (other < block)
    rank = jnp.sum(before.astype(i32), axis=1, keepdims=True)
    place = (owner * CAP + rank) * VB + iota((z.voxels, 1), 0) % VB
    lane = iota((1, z.groups * LANES), 1)
    half = LANES // 2
    every = place == lane // LANES * half + lane % half
    group = lax.axis_index("tr") // GROUP
    mine = place == group * half + iota((1, LANES), 1) % half
    voxel = jnp.sum(jnp.where(mine, iota(mine.shape, 0) + 1, 0), axis=0, keepdims=True)
    return every.astype(f32).astype(bf16), voxel - 1


def first_kernel(
    z, offsets_hbm, gains_hbm, owners_hbm, x_hbm, w_hbm, signal_hbm, orders_hbm,
    table_ref, base_ref, mine_ref, total_ref, rest_ref, orders_ref, signal_ref,
    offsets_ref, gains_ref, owners_ref, x_ref, w_ref, rows_ref, sems,
):
    me = lax.axis_index("subj")

    def weight_rows(step):
        source = lax.rem(me + step, z.subjects)
        start = pl.multiple_of(source * z.width, z.width)
        return w_hbm.at[pl.ds(start, z.width), :]

    moves = [
        (offsets_hbm, offsets_ref),
        (gains_hbm, gains_ref),
        (x_hbm, x_ref),
        (weight_rows(0), w_ref),
        (owners_hbm, owners_ref),
        (signal_hbm, signal_ref),
        (orders_hbm, orders_ref),
    ]
    for step in range(1, z.subjects):
        rows = pl.ds((step - 1) * z.width, z.width)
        moves.append((weight_rows(step), rest_ref.at[rows, :]))
    copies = [
        pltpu.make_async_copy(origin, target, sems.at[index])
        for index, (origin, target) in enumerate(moves)
    ]
    for copy in copies:
        copy.start()
    copies[0].wait()
    copies[1].wait()
    fill_table(z, offsets_ref, gains_ref, table_ref)
    copies[2].wait()
    copies[3].wait()
    total_ref[...] = filtered_product(z, x_ref, w_ref, table_ref, me)
    copies[4].wait()
    every, mine = owned_columns(z, owners_ref)
    mine_ref[...] = jnp.broadcast_to(mine, (8, LANES))
    copies[5].wait()
    for tile in range(z.tiles):
        lanes = slice(tile * LANES, (tile + 1) * LANES)
        rows = slice(tile * z.rows, (tile + 1) * z.rows)
        rows_ref[rows, :] = signal_ref[:, lanes].astype(f32)
    fill_signal(z, rows_ref, every, base_ref)
    for copy in copies[6:]:
        copy.wait()


def second_kernel(
    z, table_ref, w_ref, total_ref, base_ref, signal_ref, sibling_ref, *refs
):
    others, (out_ref, own_signal_ref) = refs[:-2], refs[-2:]
    me = lax.axis_index("subj")
    total = total_ref[...]
    for step, x_ref in enumerate(others):
        source = lax.rem(me + step + 1, z.subjects)
        rows = w_ref.at[step * z.width : (step + 1) * z.width, :]
        total = total + filtered_product(z, x_ref, rows, table_ref, source)
    value = coded_prediction(total)
    row = iota((8, LANES), 0)
    for member in range(GROUP):
        shared = []
        for tile in range(z.tiles):
            lanes = slice(tile * LANES, (tile + 1) * LANES)
            shared.append(value[member * z.own : (member + 1) * z.own, lanes])
        tails = [jnp.zeros((8, LANES), f32)] * (z.tiles * z.own_tail // 8)
        for tile in range(z.tiles):
            lanes = slice(tile * LANES, (tile + 1) * LANES)
            which, place = divmod(tile * z.own_tail, 8)
            shift = (place - member * z.own_tail) % 8
            tail = pltpu.roll(value[z.rows :, lanes], shift, 0)
            here = (row >= place) & (row < place + z.own_tail)
            tails[which] = jnp.where(here, tail, tails[which])
        for index in range(member, z.n, GROUP):
            message = jnp.concatenate(shared + tails + [base_ref[index]], axis=0)
            out_ref[index] = message.astype(i32).astype(jnp.int16)
    member = lax.rem(lax.axis_index("tr"), GROUP)
    shape = (z.own, z.rows)
    pick = iota(shape, 1) == GROUP * iota(shape, 0) + member
    pick = pick.astype(f32).astype(bf16)
    own_signal_ref[0] = dot(pick, signal_ref[...])
    own_signal_ref[1] = dot(pick, sibling_ref[...])


def third_kernel(z, orders_in_ref, mine_ref, own_signal_ref, received_ref, *refs):
    out_refs, (block_ref, tail_ref, *more) = (
        refs[:GROUP],
        refs[GROUP:],
    )
    orders = orders_in_ref[...]
    if more:
        orders_ref, sem = more
        copy = pltpu.make_async_copy(orders_in_ref, orders_ref, sem)
        copy.start()
    me = lax.axis_index("tr")
    row = iota((8, LANES), 0)
    left = iota((z.half, LANES), 1) < LANES // 2

    def integers(index, start, stop):
        return received_ref[index, start:stop, :].astype(i32)

    def tails_of(index):
        x = integers(index, z.tail_at, z.signal_at)
        tails = []
        for tile in range(z.tiles):
            which, place = divmod(tile * z.own_tail, 8)
            tail = pltpu.roll(x[which * 8 : which * 8 + 8], (8 - place) % 8, 0)
            tails.append(jnp.where(row < z.own_tail, tail, 0))
        return tails

    voxel = mine_ref[...]
    tile_of = voxel // LANES
    lane_of = jnp.maximum(voxel, 0) % LANES

    def picked(parts):
        value = jnp.zeros((8, LANES), i32)
        for tile, part in enumerate(parts):
            found = jnp.take_along_axis(part, lane_of, axis=1)
            value = jnp.where(tile_of == tile, found, value)
        return value

    def place(index, carry):
        x = integers(index, 0, z.tail_at)
        for start in range(0, z.half, 8):
            halves = []
            for first in (start, start + z.half):
                at = [tile * z.own + first for tile in range(z.tiles)]
                halves.append(picked([x[i : i + 8] for i in at]))
            value = jnp.where(left[:8], *halves).astype(f32)
            value = jnp.where(voxel >= 0, decoded_prediction(value), 0.0)
            block_ref[index, start : start + 8, :] = value
        tail = decoded_prediction(picked(tails_of(index)).astype(f32))
        here = left[:8] & (row < z.own_tail) & (voxel >= 0)
        tail_ref[index] = jnp.where(here, tail, 0.0)
        return carry

    def add_position(position, sums):
        added = []
        signal = decoded_signal(integers(position, z.signal_at, z.message))
        before = jnp.maximum(position - 1, 0)
        for condition in range(z.conditions + 1):
            if condition == z.conditions:
                residual = signal
            else:
                if condition == 0:
                    here, ahead = position, before
                elif more:
                    here = orders_ref[condition - 1, position]
                    ahead = orders_ref[condition - 1, before]
                else:
                    here = orders[condition - 1, position]
                    ahead = orders[condition - 1, max(position - 1, 0)]
                tail = tail_ref[jnp.where(position == 0, z.n, ahead)]
                residual = signal - block_ref[here]
                parts = [residual[:8] - tail, residual[8:]]
                residual = jnp.concatenate(parts, axis=0)
            value = residual * residual
            total = sums[condition]
            for start in range(0, z.half, 8):
                total = total + value[start : start + 8]
            added.append(total)
        return tuple(added)

    def loop(count, body, carry):
        if more:
            return lax.fori_loop(0, count, body, carry)
        for index in range(count):
            carry = body(index, carry)
        return carry

    def energy_of(step, here, ahead, kept):
        body = decoded_prediction(integers(here, 0, z.tail_at).astype(f32))
        tails = tails_of(ahead)
        total = jnp.zeros((z.own, LANES), f32)
        for tile in range(z.tiles):
            lanes = slice(tile * LANES, (tile + 1) * LANES)
            block = body[tile * z.own : (tile + 1) * z.own]
            residual = own_signal_ref[step, :, lanes] - block
            tail = decoded_prediction(tails[tile].astype(f32)) * kept
            tail = jnp.where(row < z.own_tail, tail, 0.0)
            residual = jnp.concatenate([residual[:8] - tail, residual[8:]], axis=0)
            total = total + residual * residual
        return jnp.sum(total, axis=1, keepdims=True)

    lanes = iota((z.own, LANES), 1)
    column = iota(orders.shape, 1)
    energies = []
    for step in range(GROUP):
        energy = jnp.zeros((z.own, LANES), f32)
        position = jnp.bitwise_xor(me, step)
        kept = jnp.where(position == 0, 0.0, 1.0)
        before = jnp.maximum(position - 1, 0)
        own = jnp.where(column == position, orders, 0)
        own = jnp.sum(own, axis=1, keepdims=True)
        preceding = jnp.where(column == before, orders, 0)
        preceding = jnp.sum(preceding, axis=1, keepdims=True)
        for condition in range(z.conditions):
            if condition == 0:
                here, ahead = position, before
            else:
                here, ahead = own[condition - 1, 0], preceding[condition - 1, 0]
            value = energy_of(step, here, ahead, kept) * (1.0 / z.voxels)
            energy = jnp.where(lanes == condition, value, energy)
        energies.append(energy)
    loop(z.n, place, 0)
    tail_ref[z.n] = jnp.zeros((8, LANES), f32)
    if more:
        copy.wait()
    zero = jnp.zeros((8, LANES), f32)
    sums = loop(z.n, add_position, (zero,) * (z.conditions + 1))
    stats = zero
    for condition, value in enumerate(sums):
        stat = jnp.sum(value, axis=0, keepdims=True)
        stats = jnp.where(row == condition, stat, stats)
    for energy, out_ref in zip(energies, out_refs):
        out_ref[: z.own, :] = energy
        out_ref[z.own :, :] = stats


def fourth_kernel(z, *refs):
    parts, (energy_ref, scores_ref) = refs[:GROUP], refs[GROUP:]
    member = lax.rem(lax.axis_index("tr"), GROUP)
    sums = sum(p[z.own :, :] for p in parts)
    sums = sums + pltpu.roll(sums, LANES // 2, 1)
    signal = sums[z.conditions : z.conditions + 1]
    fit = jnp.log((sums + EPSILON) / (signal + EPSILON))
    terms = [t.astype(f32) for t in thirds(fit)]
    square = (LANES, LANES)
    place = iota(square, 0) // VB - member * CAP
    mean = (place == iota(square, 1)) & (place >= 0) & (place < CAP)
    mean = mean & (iota(square, 0) < LANES // 2)
    mean = jnp.where(mean, 1.0 / VB, 0.0).astype(bf16)
    score = dot(jnp.concatenate(terms, axis=0).astype(bf16), mean)
    turned = jnp.transpose(jnp.concatenate([p[: z.own, :] for p in parts], axis=0))
    column = iota((z.rows, LANES), 0)
    owner = jnp.bitwise_xor(column // z.own, member)
    order = iota((z.rows, LANES), 1) == owner + GROUP * (column % z.own)
    order = order.astype(f32).astype(bf16)
    terms = [t.astype(f32) for t in thirds(turned[:8, : z.rows])]
    energy = dot(jnp.concatenate(terms, axis=0).astype(bf16), order)
    energy = energy[:8] + energy[8:16] + energy[16:]
    score = score[:8] + score[8:16] + score[16:]
    for index in range(z.conditions):
        energy_ref[index] = energy[index : index + 1, : z.rows]
        scores_ref[index] = score[index : index + 1, :CAP]


def on_device(features, block_orders, offsets, tap_gains, weights, signal, block_owner):
    z = Sizes(features, block_orders, offsets, weights, block_owner)
    owners = block_owner.reshape(1, z.blocks)
    siblings = [(i, i ^ 1) for i in range(z.n)]
    others = [
        lax.ppermute(
            features,
            "subj",
            [((i + step) % z.subjects, i) for i in range(z.subjects)],
        )
        for step in range(1, z.subjects)
    ]
    sibling_signal = lax.ppermute(signal[0], "tr", siblings)
    term_lanes = -(-3 * z.rows // LANES) * LANES
    work = 2 * z.ext * z.width * z.voxels
    shapes = [
        jax.ShapeDtypeStruct((z.bands, z.ext, term_lanes), bf16),
        jax.ShapeDtypeStruct((z.n, z.half, LANES), f32),
        jax.ShapeDtypeStruct((8, LANES), i32),
        jax.ShapeDtypeStruct((z.ext, z.voxels), f32),
        jax.ShapeDtypeStruct((z.columns - z.width, z.voxels), bf16),
        jax.ShapeDtypeStruct(block_orders.shape, i32),
        jax.ShapeDtypeStruct((z.rows, z.voxels), bf16),
    ]
    scratch = [
        pltpu.SMEM(offsets.shape, i32),
        pltpu.SMEM(tap_gains.shape, f32),
        pltpu.VMEM(owners.shape, i32),
        pltpu.VMEM(features.shape, bf16),
        pltpu.VMEM((z.width, z.voxels), bf16),
        pltpu.VMEM((z.tiles * z.rows, LANES), f32),
        pltpu.SemaphoreType.DMA((6 + z.subjects,)),
    ]
    operands = (offsets, tap_gains, owners, features, weights[0], signal[0], block_orders)
    operands = [pltpu.with_memory_space_constraint(x, pltpu.HBM) for x in operands]
    table, base, mine, total, rest, orders, signal = pl.pallas_call(
        functools.partial(first_kernel, z),
        out_shape=shapes,
        in_specs=[HBM] * len(operands),
        out_specs=[VMEM] * len(shapes),
        scratch_shapes=scratch,
        compiler_params=params(),
        cost_estimate=cost(work, 3 << 20),
        name="prepare_and_own_columns",
    )(*operands)
    outgoing, own_signal = pl.pallas_call(
        functools.partial(second_kernel, z),
        out_shape=[
            jax.ShapeDtypeStruct((z.n, z.message, LANES), jnp.int16),
            jax.ShapeDtypeStruct((GROUP, z.own, z.voxels), f32),
        ],
        in_specs=[VMEM] * (6 + len(others)),
        out_specs=[VMEM, VMEM],
        compiler_params=params(),
        cost_estimate=cost(work, 2 << 20),
        name="other_columns",
    )(table, rest, total, base, signal, sibling_signal, *others)
    received = lax.all_to_all(outgoing, "tr", 0, 0, tiled=True)
    more = [pltpu.SMEM(block_orders.shape, i32), pltpu.SemaphoreType.DMA]
    more = more if z.n > 16 else []
    part = jax.ShapeDtypeStruct((z.own + 8, LANES), f32)
    parts = pl.pallas_call(
        functools.partial(third_kernel, z),
        out_shape=[part] * GROUP,
        in_specs=[VMEM] * 4,
        out_specs=[VMEM] * GROUP,
        scratch_shapes=[
            pltpu.VMEM((z.n, z.half, LANES), f32),
            pltpu.VMEM((z.n + 1, 8, LANES), f32),
            *more,
        ],
        compiler_params=params(),
        cost_estimate=cost(work, 1 << 20),
        name="residuals",
    )(orders, mine, own_signal, received)
    parts = [parts[0], lax.ppermute(parts[1], "tr", siblings)]
    energy, scores = pl.pallas_call(
        functools.partial(fourth_kernel, z),
        out_shape=[
            jax.ShapeDtypeStruct((z.conditions, 1, z.rows), f32),
            jax.ShapeDtypeStruct((z.conditions, 1, CAP), f32),
        ],
        in_specs=[VMEM] * GROUP,
        out_specs=[VMEM, VMEM],
        compiler_params=params(),
        cost_estimate=cost(1 << 20, 1 << 16),
        name="scores",
    )(*parts)
    return energy.transpose(1, 2, 0), scores.transpose(1, 2, 0)


def solution(mesh):
    placed = (
        P("tr", "subj"),
        P(),
        P(),
        P(),
        P("subj", None, None),
        P("subj", "tr", None),
        P("subj", None, None),
    )
    return jax.shard_map(
        on_device,
        mesh=mesh,
        in_specs=placed,
        out_specs=(P("subj", "tr", None), P("subj", "tr", None)),
        check_vma=False,
    )
```

```python
import functools

import jax
import jax.numpy as jnp
from jax import lax
from jax.experimental import pallas as pl
from jax.experimental.pallas import tpu as pltpu
from jax.sharding import PartitionSpec as P

MAXLAG = 8
VB = 4
CAP = 8
LANES = 128
GROUP = 2
EPSILON = 1e-6

f32 = jnp.float32
bf16 = jnp.bfloat16
i32 = jnp.int32

VMEM = pl.BlockSpec(memory_space=pltpu.VMEM)
HBM = pl.BlockSpec(memory_space=pltpu.HBM)


def iota(shape, axis):
    return lax.broadcasted_iota(i32, shape, axis)


def dot(a, b):
    return jnp.dot(a, b, preferred_element_type=f32)


def thirds(x):
    first = x.astype(bf16)
    rest = x - first.astype(f32)
    second = rest.astype(bf16)
    return first, second, (rest - second.astype(f32)).astype(bf16)


def params(**more):
    return pltpu.CompilerParams(vmem_limit_bytes=48 * 1024 * 1024, **more)


def cost(flops, nbytes):
    return pl.CostEstimate(flops=flops, bytes_accessed=nbytes, transcendentals=0)


class Sizes:
    def __init__(self, features, block_orders, offsets, weights, block_owner):
        self.subjects = lax.axis_size("subj")
        self.n = lax.axis_size("tr")
        self.middle = self.n // 8 * 4 + 1
        self.rows, self.width = features.shape
        self.columns, self.voxels = weights.shape[1:]
        self.bands, self.taps = offsets.shape
        self.band_width = self.columns // self.bands
        self.piece = min(self.width, self.band_width)
        self.conditions = block_orders.shape[0] + 1
        self.blocks = block_owner.shape[1]
        self.ext = self.rows + MAXLAG
        self.own = self.rows // GROUP
        self.own_tail = MAXLAG // GROUP
        self.tiles = self.voxels // LANES
        self.groups = self.n // GROUP
        self.half = self.own // 2
        self.tail_at = self.tiles * self.own
        self.signal_at = self.tail_at + self.tiles * self.own_tail
        self.message = self.signal_at + self.half
        self.pair = 2 * (self.own + 8)
        assert GROUP * CAP * VB * 2 == LANES and self.n % GROUP == 0
        assert self.n & (self.n - 1) == 0 and self.n >= 4
        assert self.half % 8 == 0 and self.conditions < 8 and 8 % self.own_tail == 0
        assert self.tiles * self.own_tail % 8 == 0


BITS, LEAST = 7, -126
STEPS, SMALLEST = 668.0, -36.0


def place_of(z, position):
    position = position ^ z.middle
    return (position >> 1 & 1) * (z.n // 2) + (position >> 2) * 2 + (position & 1)


def coded_signal(x):
    size = jnp.abs(x)
    power = jnp.floor(jnp.log2(jnp.maximum(size, 2.0**LEAST)))
    half = jnp.floor(power * 0.5)
    significand = size * jnp.exp2(-half) * jnp.exp2(half - power)
    code = jnp.round((power - LEAST + significand - 1.0) * 2.0**BITS)
    code = jnp.clip(code, 0.0, 32767.0)
    return jnp.where(x < 0.0, -code, code)


def decoded_signal(code):
    size = jnp.abs(code)
    power = lax.shift_right_logical(size, jnp.full_like(size, BITS))
    significand = (size & (2**BITS - 1)) + 2**BITS
    scale = jnp.exp2((power + (LEAST - BITS)).astype(f32))
    value = significand.astype(f32) * scale
    return jnp.where(code < 0, -value, value)


def coded_prediction(x):
    size = jnp.maximum(jnp.abs(x), 2.0**SMALLEST)
    code = jnp.round((jnp.log2(size) - SMALLEST) * STEPS)
    code = jnp.minimum(code, 32767.0)
    return jnp.where(x < 0.0, -code, code)


def decoded_prediction(code):
    value = jnp.exp2(jnp.abs(code) * (1.0 / STEPS) + SMALLEST)
    return jnp.where(code < 0.0, -value, value)


def fill_signal(z, rows_ref, all_columns, base_ref):
    pieces = []
    for member in range(GROUP):
        for part in range(2):
            start = member + GROUP * part * z.half
            piece = [
                rows_ref[pl.ds(tile * z.rows + start, z.half, stride=GROUP), :]
                for tile in range(z.tiles)
            ]
            pieces.append(jnp.concatenate(piece, axis=1))
    value = coded_signal(jnp.concatenate(pieces, axis=0))
    upper = jnp.floor(value * (1.0 / 256.0))
    lower = value - 256.0 * upper
    picked = dot(jnp.concatenate([upper, lower], axis=0).astype(bf16), all_columns)
    value = 256.0 * picked[: z.rows] + picked[z.rows :]
    left = iota((z.half, LANES), 1) < LANES // 2
    for index in range(z.n):
        lanes = slice(index // GROUP * LANES, (index // GROUP + 1) * LANES)
        start = (index % GROUP) * z.own
        first = value[start : start + z.half, lanes]
        second = value[start + z.half : start + z.own, lanes]
        base_ref[index] = jnp.where(left, first, second)


def filtered_product(z, x_ref, w_ref, table_ref, source):
    total = jnp.zeros((z.ext, z.voxels), f32)
    early = iota((8, z.piece), 0) < z.own_tail
    for part in range(z.width // z.piece):
        columns = slice(part * z.piece, (part + 1) * z.piece)
        x = x_ref[:, columns]
        table = table_ref[lax.div(source * z.width + part * z.piece, z.band_width)]
        stacked = jnp.concatenate([x] * (table.shape[1] // z.rows), axis=0)
        filtered = dot(table, stacked)
        low = filtered - filtered.astype(bf16).astype(f32)
        edges = [filtered]
        for start in range(0, z.rows, z.own):
            edges.append(jnp.where(early, low[start : start + 8], 0.0))
        edges.append(low[z.rows :])
        edges = jnp.concatenate(edges, axis=0).astype(bf16)
        product = dot(edges, w_ref[columns, :])
        parts = []
        for member in range(GROUP):
            start, at = member * z.own, z.ext + member * 8
            parts.append(product[start : start + 8] + product[at : at + 8])
            parts.append(product[start + 8 : start + z.own])
        parts.append(product[z.rows : z.ext] + product[z.ext + GROUP * 8 :])
        total = total + jnp.concatenate(parts, axis=0)
    return total


def fill_table(z, offsets_ref, gains_ref, table_ref):
    lanes = table_ref.shape[2]
    column = iota((z.ext, lanes), 1)
    row = iota((z.ext, 1), 0)
    after = row - z.rows
    time = row // z.own + GROUP * (row % z.own)
    time_after = z.rows + after // z.own_tail + GROUP * (after % z.own_tail)
    lag = jnp.where(after < 0, time, time_after) - column % z.rows
    term = column // z.rows
    for band in range(z.bands):
        value = jnp.zeros((z.ext, lanes), f32)
        for tap in range(z.taps):
            hit = lag == offsets_ref[band, tap]
            value = value + jnp.where(hit, gains_ref[band, tap], 0.0)
        first, second, third = (t.astype(f32) for t in thirds(value))
        chosen = jnp.where(term == 0, first, jnp.where(term == 1, second, third))
        chosen = jnp.where(term > 2, 0.0, chosen)
        table_ref[band] = chosen.astype(bf16)


def owned_columns(z, owners_ref):
    owners = owners_ref[...]
    other = iota((z.voxels, z.blocks), 1)
    block = iota((z.voxels, 1), 0) // VB
    owner = jnp.sum(jnp.where(other == block, owners, 0), axis=1, keepdims=True)
    before = (owners == owner) & (other < block)
    rank = jnp.sum(before.astype(i32), axis=1, keepdims=True)
    place = (owner * CAP + rank) * VB + iota((z.voxels, 1), 0) % VB
    lane = iota((1, z.groups * LANES), 1)
    half = LANES // 2
    every = place == lane // LANES * half + lane % half
    group = lax.axis_index("tr") // GROUP
    mine = place == group * half + iota((1, LANES), 1) % half
    voxel = jnp.sum(jnp.where(mine, iota(mine.shape, 0) + 1, 0), axis=0, keepdims=True)
    return every.astype(f32).astype(bf16), voxel - 1


def first_kernel(
    z, offsets_hbm, gains_hbm, owners_hbm, x_hbm, w_hbm, signal_hbm, orders_hbm,
    table_ref, base_ref, mine_ref, total_ref, rest_ref, orders_ref, signal_ref,
    offsets_ref, gains_ref, owners_ref, x_ref, w_ref, rows_ref, sems,
):
    me = lax.axis_index("subj")

    def weight_rows(step):
        source = lax.rem(me + step, z.subjects)
        start = pl.multiple_of(source * z.width, z.width)
        return w_hbm.at[pl.ds(start, z.width), :]

    moves = [
        (offsets_hbm, offsets_ref),
        (gains_hbm, gains_ref),
        (x_hbm, x_ref),
        (weight_rows(0), w_ref),
        (owners_hbm, owners_ref),
        (signal_hbm, signal_ref),
        (orders_hbm, orders_ref),
    ]
    for step in range(1, z.subjects):
        rows = pl.ds((step - 1) * z.width, z.width)
        moves.append((weight_rows(step), rest_ref.at[rows, :]))
    copies = [
        pltpu.make_async_copy(origin, target, sems.at[index])
        for index, (origin, target) in enumerate(moves)
    ]
    for copy in copies:
        copy.start()
    copies[0].wait()
    copies[1].wait()
    fill_table(z, offsets_ref, gains_ref, table_ref)
    copies[2].wait()
    copies[3].wait()
    total_ref[...] = filtered_product(z, x_ref, w_ref, table_ref, me)
    copies[4].wait()
    every, mine = owned_columns(z, owners_ref)
    mine_ref[...] = jnp.broadcast_to(mine, (8, LANES))
    copies[5].wait()
    for tile in range(z.tiles):
        lanes = slice(tile * LANES, (tile + 1) * LANES)
        rows = slice(tile * z.rows, (tile + 1) * z.rows)
        rows_ref[rows, :] = signal_ref[:, lanes].astype(f32)
    fill_signal(z, rows_ref, every, base_ref)
    for copy in copies[6:]:
        copy.wait()


def second_kernel(
    z, table_ref, w_ref, total_ref, base_ref, signal_ref, sibling_ref, *refs
):
    others, (out_ref, own_signal_ref) = refs[:-2], refs[-2:]
    me = lax.axis_index("subj")
    total = total_ref[...]
    for step, x_ref in enumerate(others):
        source = lax.rem(me + step + 1, z.subjects)
        rows = w_ref.at[step * z.width : (step + 1) * z.width, :]
        total = total + filtered_product(z, x_ref, rows, table_ref, source)
    value = coded_prediction(total)
    row = iota((8, LANES), 0)
    for member in range(GROUP):
        shared = []
        for tile in range(z.tiles):
            lanes = slice(tile * LANES, (tile + 1) * LANES)
            shared.append(value[member * z.own : (member + 1) * z.own, lanes])
        tails = [jnp.zeros((8, LANES), f32)] * (z.tiles * z.own_tail // 8)
        for tile in range(z.tiles):
            lanes = slice(tile * LANES, (tile + 1) * LANES)
            which, place = divmod(tile * z.own_tail, 8)
            shift = (place - member * z.own_tail) % 8
            tail = pltpu.roll(value[z.rows :, lanes], shift, 0)
            here = (row >= place) & (row < place + z.own_tail)
            tails[which] = jnp.where(here, tail, tails[which])
        for index in range(member, z.n, GROUP):
            message = jnp.concatenate(shared + tails + [base_ref[index]], axis=0)
            message = message.astype(i32).astype(jnp.int16)
            out_ref[place_of(z, index)] = message
    member = lax.rem(lax.axis_index("tr"), GROUP)
    shape = (z.own, z.rows)
    pick = iota(shape, 1) == GROUP * iota(shape, 0) + member
    pick = pick.astype(f32).astype(bf16)
    own_signal_ref[0] = dot(pick, signal_ref[...])
    own_signal_ref[1] = dot(pick, sibling_ref[...])


def third_kernel(z, orders_in_ref, mine_ref, own_signal_ref, received_ref, *refs):
    out_refs, (block_ref, tail_ref, *more) = (
        refs[:GROUP],
        refs[GROUP:],
    )
    orders = orders_in_ref[...]
    if more:
        orders_ref, sem = more
        copy = pltpu.make_async_copy(orders_in_ref, orders_ref, sem)
        copy.start()
    me = lax.axis_index("tr")
    row = iota((8, LANES), 0)
    left = iota((z.half, LANES), 1) < LANES // 2

    def integers(index, start, stop):
        return received_ref[place_of(z, index), start:stop, :].astype(i32)

    def tails_of(index):
        x = integers(index, z.tail_at, z.signal_at)
        tails = []
        for tile in range(z.tiles):
            which, place = divmod(tile * z.own_tail, 8)
            tail = pltpu.roll(x[which * 8 : which * 8 + 8], (8 - place) % 8, 0)
            tails.append(jnp.where(row < z.own_tail, tail, 0))
        return tails

    voxel = mine_ref[...]
    tile_of = voxel // LANES
    lane_of = jnp.maximum(voxel, 0) % LANES

    def picked(parts):
        value = jnp.zeros((8, LANES), i32)
        for tile, part in enumerate(parts):
            found = jnp.take_along_axis(part, lane_of, axis=1)
            value = jnp.where(tile_of == tile, found, value)
        return value

    def place(index, carry):
        x = integers(index, 0, z.tail_at)
        for start in range(0, z.half, 8):
            halves = []
            for first in (start, start + z.half):
                at = [tile * z.own + first for tile in range(z.tiles)]
                halves.append(picked([x[i : i + 8] for i in at]))
            value = jnp.where(left[:8], *halves).astype(f32)
            value = jnp.where(voxel >= 0, decoded_prediction(value), 0.0)
            block_ref[index, start : start + 8, :] = value
        tail = decoded_prediction(picked(tails_of(index)).astype(f32))
        here = left[:8] & (row < z.own_tail) & (voxel >= 0)
        tail_ref[index] = jnp.where(here, tail, 0.0)
        return carry

    def add_position(position, sums):
        added = []
        signal = decoded_signal(integers(position, z.signal_at, z.message))
        before = jnp.maximum(position - 1, 0)
        for condition in range(z.conditions + 1):
            if condition == z.conditions:
                residual = signal
            else:
                if condition == 0:
                    here, ahead = position, before
                elif more:
                    here = orders_ref[condition - 1, position]
                    ahead = orders_ref[condition - 1, before]
                else:
                    here = orders[condition - 1, position]
                    ahead = orders[condition - 1, max(position - 1, 0)]
                tail = tail_ref[jnp.where(position == 0, z.n, ahead)]
                residual = signal - block_ref[here]
                parts = [residual[:8] - tail, residual[8:]]
                residual = jnp.concatenate(parts, axis=0)
            value = residual * residual
            total = sums[condition]
            for start in range(0, z.half, 8):
                total = total + value[start : start + 8]
            added.append(total)
        return tuple(added)

    def loop(count, body, carry):
        if more:
            return lax.fori_loop(0, count, body, carry)
        for index in range(count):
            carry = body(index, carry)
        return carry

    def energy_of(step, here, ahead, kept):
        body = decoded_prediction(integers(here, 0, z.tail_at).astype(f32))
        tails = tails_of(ahead)
        total = jnp.zeros((z.own, LANES), f32)
        for tile in range(z.tiles):
            lanes = slice(tile * LANES, (tile + 1) * LANES)
            block = body[tile * z.own : (tile + 1) * z.own]
            residual = own_signal_ref[step, :, lanes] - block
            tail = decoded_prediction(tails[tile].astype(f32)) * kept
            tail = jnp.where(row < z.own_tail, tail, 0.0)
            residual = jnp.concatenate([residual[:8] - tail, residual[8:]], axis=0)
            total = total + residual * residual
        return jnp.sum(total, axis=1, keepdims=True)

    lanes = iota((z.own, LANES), 1)
    column = iota(orders.shape, 1)
    energies = []
    for step in range(GROUP):
        energy = jnp.zeros((z.own, LANES), f32)
        position = jnp.bitwise_xor(me, step)
        kept = jnp.where(position == 0, 0.0, 1.0)
        before = jnp.maximum(position - 1, 0)
        own = jnp.where(column == position, orders, 0)
        own = jnp.sum(own, axis=1, keepdims=True)
        preceding = jnp.where(column == before, orders, 0)
        preceding = jnp.sum(preceding, axis=1, keepdims=True)
        for condition in range(z.conditions):
            if condition == 0:
                here, ahead = position, before
            else:
                here, ahead = own[condition - 1, 0], preceding[condition - 1, 0]
            value = energy_of(step, here, ahead, kept) * (1.0 / z.voxels)
            energy = jnp.where(lanes == condition, value, energy)
        energies.append(energy)
    loop(z.n, place, 0)
    tail_ref[z.n] = jnp.zeros((8, LANES), f32)
    if more:
        copy.wait()
    zero = jnp.zeros((8, LANES), f32)
    sums = loop(z.n, add_position, (zero,) * (z.conditions + 1))
    stats = zero
    for condition, value in enumerate(sums):
        stat = jnp.sum(value, axis=0, keepdims=True)
        stats = jnp.where(row == condition, stat, stats)
    for energy, out_ref in zip(energies, out_refs):
        out_ref[: z.own, :] = energy
        out_ref[z.own :, :] = stats


def fourth_kernel(z, *refs):
    parts, (energy_ref, scores_ref) = refs[:GROUP], refs[GROUP:]
    member = lax.rem(lax.axis_index("tr"), GROUP)
    sums = sum(p[z.own :, :] for p in parts)
    sums = sums + pltpu.roll(sums, LANES // 2, 1)
    signal = sums[z.conditions : z.conditions + 1]
    fit = jnp.log((sums + EPSILON) / (signal + EPSILON))
    terms = [t.astype(f32) for t in thirds(fit)]
    square = (LANES, LANES)
    place = iota(square, 0) // VB - member * CAP
    mean = (place == iota(square, 1)) & (place >= 0) & (place < CAP)
    mean = mean & (iota(square, 0) < LANES // 2)
    mean = jnp.where(mean, 1.0 / VB, 0.0).astype(bf16)
    score = dot(jnp.concatenate(terms, axis=0).astype(bf16), mean)
    turned = jnp.transpose(jnp.concatenate([p[: z.own, :] for p in parts], axis=0))
    column = iota((z.rows, LANES), 0)
    owner = jnp.bitwise_xor(column // z.own, member)
    order = iota((z.rows, LANES), 1) == owner + GROUP * (column % z.own)
    order = order.astype(f32).astype(bf16)
    terms = [t.astype(f32) for t in thirds(turned[:8, : z.rows])]
    energy = dot(jnp.concatenate(terms, axis=0).astype(bf16), order)
    energy = energy[:8] + energy[8:16] + energy[16:]
    score = score[:8] + score[8:16] + score[16:]
    for index in range(z.conditions):
        energy_ref[index] = energy[index : index + 1, : z.rows]
        scores_ref[index] = score[index : index + 1, :CAP]


def on_device(features, block_orders, offsets, tap_gains, weights, signal, block_owner):
    z = Sizes(features, block_orders, offsets, weights, block_owner)
    owners = block_owner.reshape(1, z.blocks)
    siblings = [(i, i ^ 1) for i in range(z.n)]
    others = [
        lax.ppermute(
            features,
            "subj",
            [((i + step) % z.subjects, i) for i in range(z.subjects)],
        )
        for step in range(1, z.subjects)
    ]
    sibling_signal = lax.ppermute(signal[0], "tr", siblings)
    term_lanes = -(-3 * z.rows // LANES) * LANES
    work = 2 * z.ext * z.width * z.voxels
    shapes = [
        jax.ShapeDtypeStruct((z.bands, z.ext, term_lanes), bf16),
        jax.ShapeDtypeStruct((z.n, z.half, LANES), f32),
        jax.ShapeDtypeStruct((8, LANES), i32),
        jax.ShapeDtypeStruct((z.ext, z.voxels), f32),
        jax.ShapeDtypeStruct((z.columns - z.width, z.voxels), bf16),
        jax.ShapeDtypeStruct(block_orders.shape, i32),
        jax.ShapeDtypeStruct((z.rows, z.voxels), bf16),
    ]
    scratch = [
        pltpu.SMEM(offsets.shape, i32),
        pltpu.SMEM(tap_gains.shape, f32),
        pltpu.VMEM(owners.shape, i32),
        pltpu.VMEM(features.shape, bf16),
        pltpu.VMEM((z.width, z.voxels), bf16),
        pltpu.VMEM((z.tiles * z.rows, LANES), f32),
        pltpu.SemaphoreType.DMA((6 + z.subjects,)),
    ]
    operands = (offsets, tap_gains, owners, features, weights[0], signal[0], block_orders)
    operands = [pltpu.with_memory_space_constraint(x, pltpu.HBM) for x in operands]
    table, base, mine, total, rest, orders, signal = pl.pallas_call(
        functools.partial(first_kernel, z),
        out_shape=shapes,
        in_specs=[HBM] * len(operands),
        out_specs=[VMEM] * len(shapes),
        scratch_shapes=scratch,
        compiler_params=params(),
        cost_estimate=cost(work, 3 << 20),
        name="prepare_and_own_columns",
    )(*operands)
    outgoing, own_signal = pl.pallas_call(
        functools.partial(second_kernel, z),
        out_shape=[
            jax.ShapeDtypeStruct((z.n, z.message, LANES), jnp.int16),
            jax.ShapeDtypeStruct((GROUP, z.own, z.voxels), f32),
        ],
        in_specs=[VMEM] * (6 + len(others)),
        out_specs=[VMEM, VMEM],
        compiler_params=params(),
        cost_estimate=cost(work, 2 << 20),
        name="other_columns",
    )(table, rest, total, base, signal, sibling_signal, *others)
    order = sorted(range(z.n), key=functools.partial(place_of, z))
    received = lax.all_to_all(
        outgoing, "tr", 0, 0, axis_index_groups=[order], tiled=True
    )
    more = [pltpu.SMEM(block_orders.shape, i32), pltpu.SemaphoreType.DMA]
    more = more if z.n > 16 else []
    part = jax.ShapeDtypeStruct((z.own + 8, LANES), f32)
    parts = pl.pallas_call(
        functools.partial(third_kernel, z),
        out_shape=[part] * GROUP,
        in_specs=[VMEM] * 4,
        out_specs=[VMEM] * GROUP,
        scratch_shapes=[
            pltpu.VMEM((z.n, z.half, LANES), f32),
            pltpu.VMEM((z.n + 1, 8, LANES), f32),
            *more,
        ],
        compiler_params=params(),
        cost_estimate=cost(work, 1 << 20),
        name="residuals",
    )(orders, mine, own_signal, received)
    parts = [parts[0], lax.ppermute(parts[1], "tr", siblings)]
    energy, scores = pl.pallas_call(
        functools.partial(fourth_kernel, z),
        out_shape=[
            jax.ShapeDtypeStruct((z.conditions, 1, z.rows), f32),
            jax.ShapeDtypeStruct((z.conditions, 1, CAP), f32),
        ],
        in_specs=[VMEM] * GROUP,
        out_specs=[VMEM, VMEM],
        compiler_params=params(),
        cost_estimate=cost(1 << 20, 1 << 16),
        name="scores",
    )(*parts)
    return energy.transpose(1, 2, 0), scores.transpose(1, 2, 0)


def solution(mesh):
    placed = (
        P("tr", "subj"),
        P(),
        P(),
        P(),
        P("subj", None, None),
        P("subj", "tr", None),
        P("subj", None, None),
    )
    return jax.shard_map(
        on_device,
        mesh=mesh,
        in_specs=placed,
        out_specs=(P("subj", "tr", None), P("subj", "tr", None)),
        check_vma=False,
    )
```

```python
import functools

import jax
import jax.numpy as jnp
from jax import lax
from jax.experimental import pallas as pl
from jax.experimental.pallas import tpu as pltpu
from jax.sharding import PartitionSpec as P

MAXLAG = 8
VB = 4
CAP = 8
LANES = 128
GROUP = 2
EPSILON = 1e-6

f32 = jnp.float32
bf16 = jnp.bfloat16
i32 = jnp.int32

VMEM = pl.BlockSpec(memory_space=pltpu.VMEM)
HBM = pl.BlockSpec(memory_space=pltpu.HBM)


def iota(shape, axis):
    return lax.broadcasted_iota(i32, shape, axis)


def dot(a, b):
    return jnp.dot(a, b, preferred_element_type=f32)


def thirds(x):
    first = x.astype(bf16)
    rest = x - first.astype(f32)
    second = rest.astype(bf16)
    return first, second, (rest - second.astype(f32)).astype(bf16)


def params(**more):
    return pltpu.CompilerParams(vmem_limit_bytes=48 * 1024 * 1024, **more)


def cost(flops, nbytes):
    return pl.CostEstimate(flops=flops, bytes_accessed=nbytes, transcendentals=0)


class Sizes:
    def __init__(self, features, block_orders, offsets, weights, block_owner):
        self.subjects = lax.axis_size("subj")
        self.n = lax.axis_size("tr")
        self.middle = self.n // 8 * 4 + 3
        self.rows, self.width = features.shape
        self.columns, self.voxels = weights.shape[1:]
        self.bands, self.taps = offsets.shape
        self.band_width = self.columns // self.bands
        self.piece = min(self.width, self.band_width)
        self.conditions = block_orders.shape[0] + 1
        self.blocks = block_owner.shape[1]
        self.ext = self.rows + MAXLAG
        self.own = self.rows // GROUP
        self.own_tail = MAXLAG // GROUP
        self.tiles = self.voxels // LANES
        self.groups = self.n // GROUP
        self.half = self.own // 2
        self.tail_at = self.tiles * self.own
        self.signal_at = self.tail_at + self.tiles * self.own_tail
        self.message = self.signal_at + self.half
        self.pair = 2 * (self.own + 8)
        assert GROUP * CAP * VB * 2 == LANES and self.n % GROUP == 0
        assert self.n & (self.n - 1) == 0 and self.n >= 4
        assert self.half % 8 == 0 and self.conditions < 8 and 8 % self.own_tail == 0
        assert self.tiles * self.own_tail % 8 == 0


BITS, LEAST = 7, -126
STEPS, SMALLEST = 668.0, -36.0


def place_of(z, position):
    position = position ^ z.middle
    return (position >> 1 & 1) * (z.n // 2) + (position >> 2) * 2 + (position & 1)


def coded_signal(x):
    size = jnp.abs(x)
    power = jnp.floor(jnp.log2(jnp.maximum(size, 2.0**LEAST)))
    half = jnp.floor(power * 0.5)
    significand = size * jnp.exp2(-half) * jnp.exp2(half - power)
    code = jnp.round((power - LEAST + significand - 1.0) * 2.0**BITS)
    code = jnp.clip(code, 0.0, 32767.0)
    return jnp.where(x < 0.0, -code, code)


def decoded_signal(code):
    size = jnp.abs(code)
    power = lax.shift_right_logical(size, jnp.full_like(size, BITS))
    significand = (size & (2**BITS - 1)) + 2**BITS
    scale = jnp.exp2((power + (LEAST - BITS)).astype(f32))
    value = significand.astype(f32) * scale
    return jnp.where(code < 0, -value, value)


def coded_prediction(x):
    size = jnp.maximum(jnp.abs(x), 2.0**SMALLEST)
    code = jnp.round((jnp.log2(size) - SMALLEST) * STEPS)
    code = jnp.minimum(code, 32767.0)
    return jnp.where(x < 0.0, -code, code)


def decoded_prediction(code):
    value = jnp.exp2(jnp.abs(code) * (1.0 / STEPS) + SMALLEST)
    return jnp.where(code < 0.0, -value, value)


def fill_signal(z, rows_ref, all_columns, base_ref):
    pieces = []
    for member in range(GROUP):
        for part in range(2):
            start = member + GROUP * part * z.half
            piece = [
                rows_ref[pl.ds(tile * z.rows + start, z.half, stride=GROUP), :]
                for tile in range(z.tiles)
            ]
            pieces.append(jnp.concatenate(piece, axis=1))
    value = coded_signal(jnp.concatenate(pieces, axis=0))
    upper = jnp.floor(value * (1.0 / 256.0))
    lower = value - 256.0 * upper
    picked = dot(jnp.concatenate([upper, lower], axis=0).astype(bf16), all_columns)
    value = 256.0 * picked[: z.rows] + picked[z.rows :]
    left = iota((z.half, LANES), 1) < LANES // 2
    for index in range(z.n):
        lanes = slice(index // GROUP * LANES, (index // GROUP + 1) * LANES)
        start = (index % GROUP) * z.own
        first = value[start : start + z.half, lanes]
        second = value[start + z.half : start + z.own, lanes]
        base_ref[index] = jnp.where(left, first, second)


def filtered_product(z, x_ref, w_ref, table_ref, source):
    total = jnp.zeros((z.ext, z.voxels), f32)
    early = iota((8, z.piece), 0) < z.own_tail
    for part in range(z.width // z.piece):
        columns = slice(part * z.piece, (part + 1) * z.piece)
        x = x_ref[:, columns]
        table = table_ref[lax.div(source * z.width + part * z.piece, z.band_width)]
        stacked = jnp.concatenate([x] * (table.shape[1] // z.rows), axis=0)
        filtered = dot(table, stacked)
        low = filtered - filtered.astype(bf16).astype(f32)
        edges = [filtered]
        for start in range(0, z.rows, z.own):
            edges.append(jnp.where(early, low[start : start + 8], 0.0))
        edges.append(low[z.rows :])
        edges = jnp.concatenate(edges, axis=0).astype(bf16)
        product = dot(edges, w_ref[columns, :])
        parts = []
        for member in range(GROUP):
            start, at = member * z.own, z.ext + member * 8
            parts.append(product[start : start + 8] + product[at : at + 8])
            parts.append(product[start + 8 : start + z.own])
        parts.append(product[z.rows : z.ext] + product[z.ext + GROUP * 8 :])
        total = total + jnp.concatenate(parts, axis=0)
    return total


def fill_table(z, offsets_ref, gains_ref, table_ref):
    lanes = table_ref.shape[2]
    column = iota((z.ext, lanes), 1)
    row = iota((z.ext, 1), 0)
    after = row - z.rows
    time = row // z.own + GROUP * (row % z.own)
    time_after = z.rows + after // z.own_tail + GROUP * (after % z.own_tail)
    lag = jnp.where(after < 0, time, time_after) - column % z.rows
    term = column // z.rows
    for band in range(z.bands):
        value = jnp.zeros((z.ext, lanes), f32)
        for tap in range(z.taps):
            hit = lag == offsets_ref[band, tap]
            value = value + jnp.where(hit, gains_ref[band, tap], 0.0)
        first, second, third = (t.astype(f32) for t in thirds(value))
        chosen = jnp.where(term == 0, first, jnp.where(term == 1, second, third))
        chosen = jnp.where(term > 2, 0.0, chosen)
        table_ref[band] = chosen.astype(bf16)


def owned_columns(z, owners_ref):
    owners = owners_ref[...]
    other = iota((z.voxels, z.blocks), 1)
    block = iota((z.voxels, 1), 0) // VB
    owner = jnp.sum(jnp.where(other == block, owners, 0), axis=1, keepdims=True)
    before = (owners == owner) & (other < block)
    rank = jnp.sum(before.astype(i32), axis=1, keepdims=True)
    place = (owner * CAP + rank) * VB + iota((z.voxels, 1), 0) % VB
    lane = iota((1, z.groups * LANES), 1)
    half = LANES // 2
    every = place == lane // LANES * half + lane % half
    group = lax.axis_index("tr") // GROUP
    mine = place == group * half + iota((1, LANES), 1) % half
    voxel = jnp.sum(jnp.where(mine, iota(mine.shape, 0) + 1, 0), axis=0, keepdims=True)
    return every.astype(f32).astype(bf16), voxel - 1


def first_kernel(
    z, offsets_hbm, gains_hbm, owners_hbm, x_hbm, w_hbm, signal_hbm, orders_hbm,
    table_ref, base_ref, mine_ref, total_ref, rest_ref, orders_ref, signal_ref,
    offsets_ref, gains_ref, owners_ref, x_ref, w_ref, rows_ref, sems,
):
    me = lax.axis_index("subj")

    def weight_rows(step):
        source = lax.rem(me + step, z.subjects)
        start = pl.multiple_of(source * z.width, z.width)
        return w_hbm.at[pl.ds(start, z.width), :]

    moves = [
        (offsets_hbm, offsets_ref),
        (gains_hbm, gains_ref),
        (x_hbm, x_ref),
        (weight_rows(0), w_ref),
        (owners_hbm, owners_ref),
        (signal_hbm, signal_ref),
        (orders_hbm, orders_ref),
    ]
    for step in range(1, z.subjects):
        rows = pl.ds((step - 1) * z.width, z.width)
        moves.append((weight_rows(step), rest_ref.at[rows, :]))
    copies = [
        pltpu.make_async_copy(origin, target, sems.at[index])
        for index, (origin, target) in enumerate(moves)
    ]
    for copy in copies:
        copy.start()
    copies[0].wait()
    copies[1].wait()
    fill_table(z, offsets_ref, gains_ref, table_ref)
    copies[2].wait()
    copies[3].wait()
    total_ref[...] = filtered_product(z, x_ref, w_ref, table_ref, me)
    copies[4].wait()
    every, mine = owned_columns(z, owners_ref)
    mine_ref[...] = jnp.broadcast_to(mine, (8, LANES))
    copies[5].wait()
    for tile in range(z.tiles):
        lanes = slice(tile * LANES, (tile + 1) * LANES)
        rows = slice(tile * z.rows, (tile + 1) * z.rows)
        rows_ref[rows, :] = signal_ref[:, lanes].astype(f32)
    fill_signal(z, rows_ref, every, base_ref)
    for copy in copies[6:]:
        copy.wait()


def second_kernel(
    z, table_ref, w_ref, total_ref, base_ref, signal_ref, sibling_ref, *refs
):
    others, (out_ref, own_signal_ref) = refs[:-2], refs[-2:]
    me = lax.axis_index("subj")
    total = total_ref[...]
    for step, x_ref in enumerate(others):
        source = lax.rem(me + step + 1, z.subjects)
        rows = w_ref.at[step * z.width : (step + 1) * z.width, :]
        total = total + filtered_product(z, x_ref, rows, table_ref, source)
    value = coded_prediction(total)
    row = iota((8, LANES), 0)
    for member in range(GROUP):
        shared = []
        for tile in range(z.tiles):
            lanes = slice(tile * LANES, (tile + 1) * LANES)
            shared.append(value[member * z.own : (member + 1) * z.own, lanes])
        tails = [jnp.zeros((8, LANES), f32)] * (z.tiles * z.own_tail // 8)
        for tile in range(z.tiles):
            lanes = slice(tile * LANES, (tile + 1) * LANES)
            which, place = divmod(tile * z.own_tail, 8)
            shift = (place - member * z.own_tail) % 8
            tail = pltpu.roll(value[z.rows :, lanes], shift, 0)
            here = (row >= place) & (row < place + z.own_tail)
            tails[which] = jnp.where(here, tail, tails[which])
        for index in range(member, z.n, GROUP):
            message = jnp.concatenate(shared + tails + [base_ref[index]], axis=0)
            message = message.astype(i32).astype(jnp.int16)
            out_ref[place_of(z, index)] = message
    member = lax.rem(lax.axis_index("tr"), GROUP)
    shape = (z.own, z.rows)
    pick = iota(shape, 1) == GROUP * iota(shape, 0) + member
    pick = pick.astype(f32).astype(bf16)
    own_signal_ref[0] = dot(pick, signal_ref[...])
    own_signal_ref[1] = dot(pick, sibling_ref[...])


def third_kernel(z, orders_in_ref, mine_ref, own_signal_ref, received_ref, *refs):
    out_refs, (block_ref, tail_ref, *more) = (
        refs[:GROUP],
        refs[GROUP:],
    )
    orders = orders_in_ref[...]
    if more:
        orders_ref, sem = more
        copy = pltpu.make_async_copy(orders_in_ref, orders_ref, sem)
        copy.start()
    me = lax.axis_index("tr")
    row = iota((8, LANES), 0)
    left = iota((z.half, LANES), 1) < LANES // 2

    def integers(index, start, stop):
        return received_ref[place_of(z, index), start:stop, :].astype(i32)

    def tails_of(index):
        x = integers(index, z.tail_at, z.signal_at)
        tails = []
        for tile in range(z.tiles):
            which, place = divmod(tile * z.own_tail, 8)
            tail = pltpu.roll(x[which * 8 : which * 8 + 8], (8 - place) % 8, 0)
            tails.append(jnp.where(row < z.own_tail, tail, 0))
        return tails

    voxel = mine_ref[...]
    tile_of = voxel // LANES
    lane_of = jnp.maximum(voxel, 0) % LANES

    def picked(parts):
        value = jnp.zeros((8, LANES), i32)
        for tile, part in enumerate(parts):
            found = jnp.take_along_axis(part, lane_of, axis=1)
            value = jnp.where(tile_of == tile, found, value)
        return value

    def place(index, carry):
        x = integers(index, 0, z.tail_at)
        for start in range(0, z.half, 8):
            halves = []
            for first in (start, start + z.half):
                at = [tile * z.own + first for tile in range(z.tiles)]
                halves.append(picked([x[i : i + 8] for i in at]))
            value = jnp.where(left[:8], *halves).astype(f32)
            value = jnp.where(voxel >= 0, decoded_prediction(value), 0.0)
            block_ref[index, start : start + 8, :] = value
        tail = decoded_prediction(picked(tails_of(index)).astype(f32))
        here = left[:8] & (row < z.own_tail) & (voxel >= 0)
        tail_ref[index] = jnp.where(here, tail, 0.0)
        return carry

    def add_position(position, sums):
        added = []
        signal = decoded_signal(integers(position, z.signal_at, z.message))
        before = jnp.maximum(position - 1, 0)
        for condition in range(z.conditions + 1):
            if condition == z.conditions:
                residual = signal
            else:
                if condition == 0:
                    here, ahead = position, before
                elif more:
                    here = orders_ref[condition - 1, position]
                    ahead = orders_ref[condition - 1, before]
                else:
                    here = orders[condition - 1, position]
                    ahead = orders[condition - 1, max(position - 1, 0)]
                tail = tail_ref[jnp.where(position == 0, z.n, ahead)]
                residual = signal - block_ref[here]
                parts = [residual[:8] - tail, residual[8:]]
                residual = jnp.concatenate(parts, axis=0)
            value = residual * residual
            total = sums[condition]
            for start in range(0, z.half, 8):
                total = total + value[start : start + 8]
            added.append(total)
        return tuple(added)

    def loop(count, body, carry):
        if more:
            return lax.fori_loop(0, count, body, carry)
        for index in range(count):
            carry = body(index, carry)
        return carry

    def energy_of(step, here, ahead, kept):
        body = decoded_prediction(integers(here, 0, z.tail_at).astype(f32))
        tails = tails_of(ahead)
        total = jnp.zeros((z.own, LANES), f32)
        for tile in range(z.tiles):
            lanes = slice(tile * LANES, (tile + 1) * LANES)
            block = body[tile * z.own : (tile + 1) * z.own]
            residual = own_signal_ref[step, :, lanes] - block
            tail = decoded_prediction(tails[tile].astype(f32)) * kept
            tail = jnp.where(row < z.own_tail, tail, 0.0)
            residual = jnp.concatenate([residual[:8] - tail, residual[8:]], axis=0)
            total = total + residual * residual
        return jnp.sum(total, axis=1, keepdims=True)

    lanes = iota((z.own, LANES), 1)
    column = iota(orders.shape, 1)
    energies = []
    for step in range(GROUP):
        energy = jnp.zeros((z.own, LANES), f32)
        position = jnp.bitwise_xor(me, step)
        kept = jnp.where(position == 0, 0.0, 1.0)
        before = jnp.maximum(position - 1, 0)
        own = jnp.where(column == position, orders, 0)
        own = jnp.sum(own, axis=1, keepdims=True)
        preceding = jnp.where(column == before, orders, 0)
        preceding = jnp.sum(preceding, axis=1, keepdims=True)
        for condition in range(z.conditions):
            if condition == 0:
                here, ahead = position, before
            else:
                here, ahead = own[condition - 1, 0], preceding[condition - 1, 0]
            value = energy_of(step, here, ahead, kept) * (1.0 / z.voxels)
            energy = jnp.where(lanes == condition, value, energy)
        energies.append(energy)
    loop(z.n, place, 0)
    tail_ref[z.n] = jnp.zeros((8, LANES), f32)
    if more:
        copy.wait()
    zero = jnp.zeros((8, LANES), f32)
    sums = loop(z.n, add_position, (zero,) * (z.conditions + 1))
    stats = zero
    for condition, value in enumerate(sums):
        stat = jnp.sum(value, axis=0, keepdims=True)
        stats = jnp.where(row == condition, stat, stats)
    for energy, out_ref in zip(energies, out_refs):
        out_ref[: z.own, :] = energy
        out_ref[z.own :, :] = stats


def fourth_kernel(z, *refs):
    parts, (energy_ref, scores_ref) = refs[:GROUP], refs[GROUP:]
    member = lax.rem(lax.axis_index("tr"), GROUP)
    sums = sum(p[z.own :, :] for p in parts)
    sums = sums + pltpu.roll(sums, LANES // 2, 1)
    signal = sums[z.conditions : z.conditions + 1]
    fit = jnp.log((sums + EPSILON) / (signal + EPSILON))
    terms = [t.astype(f32) for t in thirds(fit)]
    square = (LANES, LANES)
    place = iota(square, 0) // VB - member * CAP
    mean = (place == iota(square, 1)) & (place >= 0) & (place < CAP)
    mean = mean & (iota(square, 0) < LANES // 2)
    mean = jnp.where(mean, 1.0 / VB, 0.0).astype(bf16)
    score = dot(jnp.concatenate(terms, axis=0).astype(bf16), mean)
    turned = jnp.transpose(jnp.concatenate([p[: z.own, :] for p in parts], axis=0))
    column = iota((z.rows, LANES), 0)
    owner = jnp.bitwise_xor(column // z.own, member)
    order = iota((z.rows, LANES), 1) == owner + GROUP * (column % z.own)
    order = order.astype(f32).astype(bf16)
    terms = [t.astype(f32) for t in thirds(turned[:8, : z.rows])]
    energy = dot(jnp.concatenate(terms, axis=0).astype(bf16), order)
    energy = energy[:8] + energy[8:16] + energy[16:]
    score = score[:8] + score[8:16] + score[16:]
    for index in range(z.conditions):
        energy_ref[index] = energy[index : index + 1, : z.rows]
        scores_ref[index] = score[index : index + 1, :CAP]


def on_device(features, block_orders, offsets, tap_gains, weights, signal, block_owner):
    z = Sizes(features, block_orders, offsets, weights, block_owner)
    owners = block_owner.reshape(1, z.blocks)
    siblings = [(i, i ^ 1) for i in range(z.n)]
    others = [
        lax.ppermute(
            features,
            "subj",
            [((i + step) % z.subjects, i) for i in range(z.subjects)],
        )
        for step in range(1, z.subjects)
    ]
    sibling_signal = lax.ppermute(signal[0], "tr", siblings)
    term_lanes = -(-3 * z.rows // LANES) * LANES
    work = 2 * z.ext * z.width * z.voxels
    shapes = [
        jax.ShapeDtypeStruct((z.bands, z.ext, term_lanes), bf16),
        jax.ShapeDtypeStruct((z.n, z.half, LANES), f32),
        jax.ShapeDtypeStruct((8, LANES), i32),
        jax.ShapeDtypeStruct((z.ext, z.voxels), f32),
        jax.ShapeDtypeStruct((z.columns - z.width, z.voxels), bf16),
        jax.ShapeDtypeStruct(block_orders.shape, i32),
        jax.ShapeDtypeStruct((z.rows, z.voxels), bf16),
    ]
    scratch = [
        pltpu.SMEM(offsets.shape, i32),
        pltpu.SMEM(tap_gains.shape, f32),
        pltpu.VMEM(owners.shape, i32),
        pltpu.VMEM(features.shape, bf16),
        pltpu.VMEM((z.width, z.voxels), bf16),
        pltpu.VMEM((z.tiles * z.rows, LANES), f32),
        pltpu.SemaphoreType.DMA((6 + z.subjects,)),
    ]
    operands = (offsets, tap_gains, owners, features, weights[0], signal[0], block_orders)
    operands = [pltpu.with_memory_space_constraint(x, pltpu.HBM) for x in operands]
    table, base, mine, total, rest, orders, signal = pl.pallas_call(
        functools.partial(first_kernel, z),
        out_shape=shapes,
        in_specs=[HBM] * len(operands),
        out_specs=[VMEM] * len(shapes),
        scratch_shapes=scratch,
        compiler_params=params(),
        cost_estimate=cost(work, 3 << 20),
        name="prepare_and_own_columns",
    )(*operands)
    outgoing, own_signal = pl.pallas_call(
        functools.partial(second_kernel, z),
        out_shape=[
            jax.ShapeDtypeStruct((z.n, z.message, LANES), jnp.int16),
            jax.ShapeDtypeStruct((GROUP, z.own, z.voxels), f32),
        ],
        in_specs=[VMEM] * (6 + len(others)),
        out_specs=[VMEM, VMEM],
        compiler_params=params(),
        cost_estimate=cost(work, 2 << 20),
        name="other_columns",
    )(table, rest, total, base, signal, sibling_signal, *others)
    order = sorted(range(z.n), key=functools.partial(place_of, z))
    received = lax.all_to_all(
        outgoing, "tr", 0, 0, axis_index_groups=[order], tiled=True
    )
    more = [pltpu.SMEM(block_orders.shape, i32), pltpu.SemaphoreType.DMA]
    more = more if z.n > 16 else []
    part = jax.ShapeDtypeStruct((z.own + 8, LANES), f32)
    parts = pl.pallas_call(
        functools.partial(third_kernel, z),
        out_shape=[part] * GROUP,
        in_specs=[VMEM] * 4,
        out_specs=[VMEM] * GROUP,
        scratch_shapes=[
            pltpu.VMEM((z.n, z.half, LANES), f32),
            pltpu.VMEM((z.n + 1, 8, LANES), f32),
            *more,
        ],
        compiler_params=params(),
        cost_estimate=cost(work, 1 << 20),
        name="residuals",
    )(orders, mine, own_signal, received)
    parts = [parts[0], lax.ppermute(parts[1], "tr", siblings)]
    energy, scores = pl.pallas_call(
        functools.partial(fourth_kernel, z),
        out_shape=[
            jax.ShapeDtypeStruct((z.conditions, 1, z.rows), f32),
            jax.ShapeDtypeStruct((z.conditions, 1, CAP), f32),
        ],
        in_specs=[VMEM] * GROUP,
        out_specs=[VMEM, VMEM],
        compiler_params=params(),
        cost_estimate=cost(1 << 20, 1 << 16),
        name="scores",
    )(*parts)
    return energy.transpose(1, 2, 0), scores.transpose(1, 2, 0)


def solution(mesh):
    placed = (
        P("tr", "subj"),
        P(),
        P(),
        P(),
        P("subj", None, None),
        P("subj", "tr", None),
        P("subj", None, None),
    )
    return jax.shard_map(
        on_device,
        mesh=mesh,
        in_specs=placed,
        out_specs=(P("subj", "tr", None), P("subj", "tr", None)),
        check_vma=False,
    )
```

```python
import functools

import jax
import jax.numpy as jnp
from jax import lax
from jax.experimental import pallas as pl
from jax.experimental.pallas import tpu as pltpu
from jax.sharding import PartitionSpec as P

MAXLAG = 8
VB = 4
CAP = 8
LANES = 128
GROUP = 2
EPSILON = 1e-6

f32 = jnp.float32
bf16 = jnp.bfloat16
i32 = jnp.int32

VMEM = pl.BlockSpec(memory_space=pltpu.VMEM)
HBM = pl.BlockSpec(memory_space=pltpu.HBM)


def iota(shape, axis):
    return lax.broadcasted_iota(i32, shape, axis)


def dot(a, b):
    return jnp.dot(a, b, preferred_element_type=f32)


def thirds(x):
    first = x.astype(bf16)
    rest = x - first.astype(f32)
    second = rest.astype(bf16)
    return first, second, (rest - second.astype(f32)).astype(bf16)


def params(**more):
    return pltpu.CompilerParams(vmem_limit_bytes=48 * 1024 * 1024, **more)


def cost(flops, nbytes):
    return pl.CostEstimate(flops=flops, bytes_accessed=nbytes, transcendentals=0)


class Sizes:
    def __init__(self, features, block_orders, offsets, weights, block_owner):
        self.subjects = lax.axis_size("subj")
        self.n = lax.axis_size("tr")
        self.middle = self.n // 8 * 4 + 3
        self.rows, self.width = features.shape
        self.columns, self.voxels = weights.shape[1:]
        self.bands, self.taps = offsets.shape
        self.band_width = self.columns // self.bands
        self.piece = min(self.width, self.band_width)
        self.conditions = block_orders.shape[0] + 1
        self.blocks = block_owner.shape[1]
        self.ext = self.rows + MAXLAG
        self.own = self.rows // GROUP
        self.own_tail = MAXLAG // GROUP
        self.tiles = self.voxels // LANES
        self.groups = self.n // GROUP
        self.half = self.own // 2
        self.tail_at = self.tiles * self.own
        self.signal_at = self.tail_at + self.tiles * self.own_tail
        self.message = self.signal_at + self.half
        self.pair = 2 * (self.own + 8)
        assert GROUP * CAP * VB * 2 == LANES and self.n % GROUP == 0
        assert self.n & (self.n - 1) == 0 and self.n >= 8
        assert self.half % 8 == 0 and self.conditions < 8 and 8 % self.own_tail == 0
        assert self.tiles * self.own_tail % 8 == 0


BITS, LEAST = 7, -126
STEPS, SMALLEST = 668.0, -36.0


def place_of(z, position):
    position = position ^ z.middle
    low = (position >> 2 & 1) + (position & 2) + (position & 1) * 4
    return (position >> 3) * 8 + low


def coded_signal(x):
    size = jnp.abs(x)
    power = jnp.floor(jnp.log2(jnp.maximum(size, 2.0**LEAST)))
    half = jnp.floor(power * 0.5)
    significand = size * jnp.exp2(-half) * jnp.exp2(half - power)
    code = jnp.round((power - LEAST + significand - 1.0) * 2.0**BITS)
    code = jnp.clip(code, 0.0, 32767.0)
    return jnp.where(x < 0.0, -code, code)


def decoded_signal(code):
    size = jnp.abs(code)
    power = lax.shift_right_logical(size, jnp.full_like(size, BITS))
    significand = (size & (2**BITS - 1)) + 2**BITS
    scale = jnp.exp2((power + (LEAST - BITS)).astype(f32))
    value = significand.astype(f32) * scale
    return jnp.where(code < 0, -value, value)


def coded_prediction(x):
    size = jnp.maximum(jnp.abs(x), 2.0**SMALLEST)
    code = jnp.round((jnp.log2(size) - SMALLEST) * STEPS)
    code = jnp.minimum(code, 32767.0)
    return jnp.where(x < 0.0, -code, code)


def decoded_prediction(code):
    value = jnp.exp2(jnp.abs(code) * (1.0 / STEPS) + SMALLEST)
    return jnp.where(code < 0.0, -value, value)


def fill_signal(z, rows_ref, all_columns, base_ref):
    pieces = []
    for member in range(GROUP):
        for part in range(2):
            start = member + GROUP * part * z.half
            piece = [
                rows_ref[pl.ds(tile * z.rows + start, z.half, stride=GROUP), :]
                for tile in range(z.tiles)
            ]
            pieces.append(jnp.concatenate(piece, axis=1))
    value = coded_signal(jnp.concatenate(pieces, axis=0))
    upper = jnp.floor(value * (1.0 / 256.0))
    lower = value - 256.0 * upper
    picked = dot(jnp.concatenate([upper, lower], axis=0).astype(bf16), all_columns)
    value = 256.0 * picked[: z.rows] + picked[z.rows :]
    left = iota((z.half, LANES), 1) < LANES // 2
    for index in range(z.n):
        lanes = slice(index // GROUP * LANES, (index // GROUP + 1) * LANES)
        start = (index % GROUP) * z.own
        first = value[start : start + z.half, lanes]
        second = value[start + z.half : start + z.own, lanes]
        base_ref[index] = jnp.where(left, first, second)


def filtered_product(z, x_ref, w_ref, table_ref, source):
    total = jnp.zeros((z.ext, z.voxels), f32)
    early = iota((8, z.piece), 0) < z.own_tail
    for part in range(z.width // z.piece):
        columns = slice(part * z.piece, (part + 1) * z.piece)
        x = x_ref[:, columns]
        table = table_ref[lax.div(source * z.width + part * z.piece, z.band_width)]
        stacked = jnp.concatenate([x] * (table.shape[1] // z.rows), axis=0)
        filtered = dot(table, stacked)
        low = filtered - filtered.astype(bf16).astype(f32)
        edges = [filtered]
        for start in range(0, z.rows, z.own):
            edges.append(jnp.where(early, low[start : start + 8], 0.0))
        edges.append(low[z.rows :])
        edges = jnp.concatenate(edges, axis=0).astype(bf16)
        product = dot(edges, w_ref[columns, :])
        parts = []
        for member in range(GROUP):
            start, at = member * z.own, z.ext + member * 8
            parts.append(product[start : start + 8] + product[at : at + 8])
            parts.append(product[start + 8 : start + z.own])
        parts.append(product[z.rows : z.ext] + product[z.ext + GROUP * 8 :])
        total = total + jnp.concatenate(parts, axis=0)
    return total


def fill_table(z, offsets_ref, gains_ref, table_ref):
    lanes = table_ref.shape[2]
    column = iota((z.ext, lanes), 1)
    row = iota((z.ext, 1), 0)
    after = row - z.rows
    time = row // z.own + GROUP * (row % z.own)
    time_after = z.rows + after // z.own_tail + GROUP * (after % z.own_tail)
    lag = jnp.where(after < 0, time, time_after) - column % z.rows
    term = column // z.rows
    for band in range(z.bands):
        value = jnp.zeros((z.ext, lanes), f32)
        for tap in range(z.taps):
            hit = lag == offsets_ref[band, tap]
            value = value + jnp.where(hit, gains_ref[band, tap], 0.0)
        first, second, third = (t.astype(f32) for t in thirds(value))
        chosen = jnp.where(term == 0, first, jnp.where(term == 1, second, third))
        chosen = jnp.where(term > 2, 0.0, chosen)
        table_ref[band] = chosen.astype(bf16)


def owned_columns(z, owners_ref):
    owners = owners_ref[...]
    other = iota((z.voxels, z.blocks), 1)
    block = iota((z.voxels, 1), 0) // VB
    owner = jnp.sum(jnp.where(other == block, owners, 0), axis=1, keepdims=True)
    before = (owners == owner) & (other < block)
    rank = jnp.sum(before.astype(i32), axis=1, keepdims=True)
    place = (owner * CAP + rank) * VB + iota((z.voxels, 1), 0) % VB
    lane = iota((1, z.groups * LANES), 1)
    half = LANES // 2
    every = place == lane // LANES * half + lane % half
    group = lax.axis_index("tr") // GROUP
    mine = place == group * half + iota((1, LANES), 1) % half
    voxel = jnp.sum(jnp.where(mine, iota(mine.shape, 0) + 1, 0), axis=0, keepdims=True)
    return every.astype(f32).astype(bf16), voxel - 1


def first_kernel(
    z, offsets_hbm, gains_hbm, owners_hbm, x_hbm, w_hbm, signal_hbm, orders_hbm,
    table_ref, base_ref, mine_ref, total_ref, rest_ref, orders_ref, signal_ref,
    offsets_ref, gains_ref, owners_ref, x_ref, w_ref, rows_ref, sems,
):
    me = lax.axis_index("subj")

    def weight_rows(step):
        source = lax.rem(me + step, z.subjects)
        start = pl.multiple_of(source * z.width, z.width)
        return w_hbm.at[pl.ds(start, z.width), :]

    moves = [
        (offsets_hbm, offsets_ref),
        (gains_hbm, gains_ref),
        (x_hbm, x_ref),
        (weight_rows(0), w_ref),
        (owners_hbm, owners_ref),
        (signal_hbm, signal_ref),
        (orders_hbm, orders_ref),
    ]
    for step in range(1, z.subjects):
        rows = pl.ds((step - 1) * z.width, z.width)
        moves.append((weight_rows(step), rest_ref.at[rows, :]))
    copies = [
        pltpu.make_async_copy(origin, target, sems.at[index])
        for index, (origin, target) in enumerate(moves)
    ]
    for copy in copies:
        copy.start()
    copies[0].wait()
    copies[1].wait()
    fill_table(z, offsets_ref, gains_ref, table_ref)
    copies[2].wait()
    copies[3].wait()
    total_ref[...] = filtered_product(z, x_ref, w_ref, table_ref, me)
    copies[4].wait()
    every, mine = owned_columns(z, owners_ref)
    mine_ref[...] = jnp.broadcast_to(mine, (8, LANES))
    copies[5].wait()
    for tile in range(z.tiles):
        lanes = slice(tile * LANES, (tile + 1) * LANES)
        rows = slice(tile * z.rows, (tile + 1) * z.rows)
        rows_ref[rows, :] = signal_ref[:, lanes].astype(f32)
    fill_signal(z, rows_ref, every, base_ref)
    for copy in copies[6:]:
        copy.wait()


def second_kernel(
    z, table_ref, w_ref, total_ref, base_ref, signal_ref, sibling_ref, *refs
):
    others, (out_ref, own_signal_ref) = refs[:-2], refs[-2:]
    me = lax.axis_index("subj")
    total = total_ref[...]
    for step, x_ref in enumerate(others):
        source = lax.rem(me + step + 1, z.subjects)
        rows = w_ref.at[step * z.width : (step + 1) * z.width, :]
        total = total + filtered_product(z, x_ref, rows, table_ref, source)
    value = coded_prediction(total)
    row = iota((8, LANES), 0)
    for member in range(GROUP):
        shared = []
        for tile in range(z.tiles):
            lanes = slice(tile * LANES, (tile + 1) * LANES)
            shared.append(value[member * z.own : (member + 1) * z.own, lanes])
        tails = [jnp.zeros((8, LANES), f32)] * (z.tiles * z.own_tail // 8)
        for tile in range(z.tiles):
            lanes = slice(tile * LANES, (tile + 1) * LANES)
            which, place = divmod(tile * z.own_tail, 8)
            shift = (place - member * z.own_tail) % 8
            tail = pltpu.roll(value[z.rows :, lanes], shift, 0)
            here = (row >= place) & (row < place + z.own_tail)
            tails[which] = jnp.where(here, tail, tails[which])
        for index in range(member, z.n, GROUP):
            message = jnp.concatenate(shared + tails + [base_ref[index]], axis=0)
            message = message.astype(i32).astype(jnp.int16)
            out_ref[place_of(z, index)] = message
    member = lax.rem(lax.axis_index("tr"), GROUP)
    shape = (z.own, z.rows)
    pick = iota(shape, 1) == GROUP * iota(shape, 0) + member
    pick = pick.astype(f32).astype(bf16)
    own_signal_ref[0] = dot(pick, signal_ref[...])
    own_signal_ref[1] = dot(pick, sibling_ref[...])


def third_kernel(z, orders_in_ref, mine_ref, own_signal_ref, received_ref, *refs):
    out_refs, (block_ref, tail_ref, *more) = (
        refs[:GROUP],
        refs[GROUP:],
    )
    orders = orders_in_ref[...]
    if more:
        orders_ref, sem = more
        copy = pltpu.make_async_copy(orders_in_ref, orders_ref, sem)
        copy.start()
    me = lax.axis_index("tr")
    row = iota((8, LANES), 0)
    left = iota((z.half, LANES), 1) < LANES // 2

    def integers(index, start, stop):
        return received_ref[place_of(z, index), start:stop, :].astype(i32)

    def tails_of(index):
        x = integers(index, z.tail_at, z.signal_at)
        tails = []
        for tile in range(z.tiles):
            which, place = divmod(tile * z.own_tail, 8)
            tail = pltpu.roll(x[which * 8 : which * 8 + 8], (8 - place) % 8, 0)
            tails.append(jnp.where(row < z.own_tail, tail, 0))
        return tails

    voxel = mine_ref[...]
    tile_of = voxel // LANES
    lane_of = jnp.maximum(voxel, 0) % LANES

    def picked(parts):
        value = jnp.zeros((8, LANES), i32)
        for tile, part in enumerate(parts):
            found = jnp.take_along_axis(part, lane_of, axis=1)
            value = jnp.where(tile_of == tile, found, value)
        return value

    def place(index, carry):
        x = integers(index, 0, z.tail_at)
        for start in range(0, z.half, 8):
            halves = []
            for first in (start, start + z.half):
                at = [tile * z.own + first for tile in range(z.tiles)]
                halves.append(picked([x[i : i + 8] for i in at]))
            value = jnp.where(left[:8], *halves).astype(f32)
            value = jnp.where(voxel >= 0, decoded_prediction(value), 0.0)
            block_ref[index, start : start + 8, :] = value
        tail = decoded_prediction(picked(tails_of(index)).astype(f32))
        here = left[:8] & (row < z.own_tail) & (voxel >= 0)
        tail_ref[index] = jnp.where(here, tail, 0.0)
        return carry

    def add_position(position, sums):
        added = []
        signal = decoded_signal(integers(position, z.signal_at, z.message))
        before = jnp.maximum(position - 1, 0)
        for condition in range(z.conditions + 1):
            if condition == z.conditions:
                residual = signal
            else:
                if condition == 0:
                    here, ahead = position, before
                elif more:
                    here = orders_ref[condition - 1, position]
                    ahead = orders_ref[condition - 1, before]
                else:
                    here = orders[condition - 1, position]
                    ahead = orders[condition - 1, max(position - 1, 0)]
                tail = tail_ref[jnp.where(position == 0, z.n, ahead)]
                residual = signal - block_ref[here]
                parts = [residual[:8] - tail, residual[8:]]
                residual = jnp.concatenate(parts, axis=0)
            value = residual * residual
            total = sums[condition]
            for start in range(0, z.half, 8):
                total = total + value[start : start + 8]
            added.append(total)
        return tuple(added)

    def loop(count, body, carry):
        if more:
            return lax.fori_loop(0, count, body, carry)
        for index in range(count):
            carry = body(index, carry)
        return carry

    def energy_of(step, here, ahead, kept):
        body = decoded_prediction(integers(here, 0, z.tail_at).astype(f32))
        tails = tails_of(ahead)
        total = jnp.zeros((z.own, LANES), f32)
        for tile in range(z.tiles):
            lanes = slice(tile * LANES, (tile + 1) * LANES)
            block = body[tile * z.own : (tile + 1) * z.own]
            residual = own_signal_ref[step, :, lanes] - block
            tail = decoded_prediction(tails[tile].astype(f32)) * kept
            tail = jnp.where(row < z.own_tail, tail, 0.0)
            residual = jnp.concatenate([residual[:8] - tail, residual[8:]], axis=0)
            total = total + residual * residual
        return jnp.sum(total, axis=1, keepdims=True)

    lanes = iota((z.own, LANES), 1)
    column = iota(orders.shape, 1)
    energies = []
    for step in range(GROUP):
        energy = jnp.zeros((z.own, LANES), f32)
        position = jnp.bitwise_xor(me, step)
        kept = jnp.where(position == 0, 0.0, 1.0)
        before = jnp.maximum(position - 1, 0)
        own = jnp.where(column == position, orders, 0)
        own = jnp.sum(own, axis=1, keepdims=True)
        preceding = jnp.where(column == before, orders, 0)
        preceding = jnp.sum(preceding, axis=1, keepdims=True)
        for condition in range(z.conditions):
            if condition == 0:
                here, ahead = position, before
            else:
                here, ahead = own[condition - 1, 0], preceding[condition - 1, 0]
            value = energy_of(step, here, ahead, kept) * (1.0 / z.voxels)
            energy = jnp.where(lanes == condition, value, energy)
        energies.append(energy)
    loop(z.n, place, 0)
    tail_ref[z.n] = jnp.zeros((8, LANES), f32)
    if more:
        copy.wait()
    zero = jnp.zeros((8, LANES), f32)
    sums = loop(z.n, add_position, (zero,) * (z.conditions + 1))
    stats = zero
    for condition, value in enumerate(sums):
        stat = jnp.sum(value, axis=0, keepdims=True)
        stats = jnp.where(row == condition, stat, stats)
    for energy, out_ref in zip(energies, out_refs):
        out_ref[: z.own, :] = energy
        out_ref[z.own :, :] = stats


def fourth_kernel(z, *refs):
    parts, (energy_ref, scores_ref) = refs[:GROUP], refs[GROUP:]
    member = lax.rem(lax.axis_index("tr"), GROUP)
    sums = sum(p[z.own :, :] for p in parts)
    sums = sums + pltpu.roll(sums, LANES // 2, 1)
    signal = sums[z.conditions : z.conditions + 1]
    fit = jnp.log((sums + EPSILON) / (signal + EPSILON))
    terms = [t.astype(f32) for t in thirds(fit)]
    square = (LANES, LANES)
    place = iota(square, 0) // VB - member * CAP
    mean = (place == iota(square, 1)) & (place >= 0) & (place < CAP)
    mean = mean & (iota(square, 0) < LANES // 2)
    mean = jnp.where(mean, 1.0 / VB, 0.0).astype(bf16)
    score = dot(jnp.concatenate(terms, axis=0).astype(bf16), mean)
    turned = jnp.transpose(jnp.concatenate([p[: z.own, :] for p in parts], axis=0))
    column = iota((z.rows, LANES), 0)
    owner = jnp.bitwise_xor(column // z.own, member)
    order = iota((z.rows, LANES), 1) == owner + GROUP * (column % z.own)
    order = order.astype(f32).astype(bf16)
    terms = [t.astype(f32) for t in thirds(turned[:8, : z.rows])]
    energy = dot(jnp.concatenate(terms, axis=0).astype(bf16), order)
    energy = energy[:8] + energy[8:16] + energy[16:]
    score = score[:8] + score[8:16] + score[16:]
    for index in range(z.conditions):
        energy_ref[index] = energy[index : index + 1, : z.rows]
        scores_ref[index] = score[index : index + 1, :CAP]


def on_device(features, block_orders, offsets, tap_gains, weights, signal, block_owner):
    z = Sizes(features, block_orders, offsets, weights, block_owner)
    owners = block_owner.reshape(1, z.blocks)
    siblings = [(i, i ^ 1) for i in range(z.n)]
    others = [
        lax.ppermute(
            features,
            "subj",
            [((i + step) % z.subjects, i) for i in range(z.subjects)],
        )
        for step in range(1, z.subjects)
    ]
    sibling_signal = lax.ppermute(signal[0], "tr", siblings)
    term_lanes = -(-3 * z.rows // LANES) * LANES
    work = 2 * z.ext * z.width * z.voxels
    shapes = [
        jax.ShapeDtypeStruct((z.bands, z.ext, term_lanes), bf16),
        jax.ShapeDtypeStruct((z.n, z.half, LANES), f32),
        jax.ShapeDtypeStruct((8, LANES), i32),
        jax.ShapeDtypeStruct((z.ext, z.voxels), f32),
        jax.ShapeDtypeStruct((z.columns - z.width, z.voxels), bf16),
        jax.ShapeDtypeStruct(block_orders.shape, i32),
        jax.ShapeDtypeStruct((z.rows, z.voxels), bf16),
    ]
    scratch = [
        pltpu.SMEM(offsets.shape, i32),
        pltpu.SMEM(tap_gains.shape, f32),
        pltpu.VMEM(owners.shape, i32),
        pltpu.VMEM(features.shape, bf16),
        pltpu.VMEM((z.width, z.voxels), bf16),
        pltpu.VMEM((z.tiles * z.rows, LANES), f32),
        pltpu.SemaphoreType.DMA((6 + z.subjects,)),
    ]
    operands = (offsets, tap_gains, owners, features, weights[0], signal[0], block_orders)
    operands = [pltpu.with_memory_space_constraint(x, pltpu.HBM) for x in operands]
    table, base, mine, total, rest, orders, signal = pl.pallas_call(
        functools.partial(first_kernel, z),
        out_shape=shapes,
        in_specs=[HBM] * len(operands),
        out_specs=[VMEM] * len(shapes),
        scratch_shapes=scratch,
        compiler_params=params(),
        cost_estimate=cost(work, 3 << 20),
        name="prepare_and_own_columns",
    )(*operands)
    outgoing, own_signal = pl.pallas_call(
        functools.partial(second_kernel, z),
        out_shape=[
            jax.ShapeDtypeStruct((z.n, z.message, LANES), jnp.int16),
            jax.ShapeDtypeStruct((GROUP, z.own, z.voxels), f32),
        ],
        in_specs=[VMEM] * (6 + len(others)),
        out_specs=[VMEM, VMEM],
        compiler_params=params(),
        cost_estimate=cost(work, 2 << 20),
        name="other_columns",
    )(table, rest, total, base, signal, sibling_signal, *others)
    order = sorted(range(z.n), key=functools.partial(place_of, z))
    received = lax.all_to_all(
        outgoing, "tr", 0, 0, axis_index_groups=[order], tiled=True
    )
    more = [pltpu.SMEM(block_orders.shape, i32), pltpu.SemaphoreType.DMA]
    more = more if z.n > 16 else []
    part = jax.ShapeDtypeStruct((z.own + 8, LANES), f32)
    parts = pl.pallas_call(
        functools.partial(third_kernel, z),
        out_shape=[part] * GROUP,
        in_specs=[VMEM] * 4,
        out_specs=[VMEM] * GROUP,
        scratch_shapes=[
            pltpu.VMEM((z.n, z.half, LANES), f32),
            pltpu.VMEM((z.n + 1, 8, LANES), f32),
            *more,
        ],
        compiler_params=params(),
        cost_estimate=cost(work, 1 << 20),
        name="residuals",
    )(orders, mine, own_signal, received)
    parts = [parts[0], lax.ppermute(parts[1], "tr", siblings)]
    energy, scores = pl.pallas_call(
        functools.partial(fourth_kernel, z),
        out_shape=[
            jax.ShapeDtypeStruct((z.conditions, 1, z.rows), f32),
            jax.ShapeDtypeStruct((z.conditions, 1, CAP), f32),
        ],
        in_specs=[VMEM] * GROUP,
        out_specs=[VMEM, VMEM],
        compiler_params=params(),
        cost_estimate=cost(1 << 20, 1 << 16),
        name="scores",
    )(*parts)
    return energy.transpose(1, 2, 0), scores.transpose(1, 2, 0)


def solution(mesh):
    placed = (
        P("tr", "subj"),
        P(),
        P(),
        P(),
        P("subj", None, None),
        P("subj", "tr", None),
        P("subj", None, None),
    )
    return jax.shard_map(
        on_device,
        mesh=mesh,
        in_specs=placed,
        out_specs=(P("subj", "tr", None), P("subj", "tr", None)),
        check_vma=False,
    )
```

```python
import functools

import jax
import jax.numpy as jnp
from jax import lax
from jax.experimental import pallas as pl
from jax.experimental.pallas import tpu as pltpu
from jax.sharding import PartitionSpec as P

MAXLAG = 8
VB = 4
CAP = 8
LANES = 128
GROUP = 2
EPSILON = 1e-6

f32 = jnp.float32
bf16 = jnp.bfloat16
i32 = jnp.int32

VMEM = pl.BlockSpec(memory_space=pltpu.VMEM)
HBM = pl.BlockSpec(memory_space=pltpu.HBM)


def iota(shape, axis):
    return lax.broadcasted_iota(i32, shape, axis)


def dot(a, b):
    return jnp.dot(a, b, preferred_element_type=f32)


def thirds(x):
    first = x.astype(bf16)
    rest = x - first.astype(f32)
    second = rest.astype(bf16)
    return first, second, (rest - second.astype(f32)).astype(bf16)


def params(**more):
    return pltpu.CompilerParams(vmem_limit_bytes=48 * 1024 * 1024, **more)


def cost(flops, nbytes):
    return pl.CostEstimate(flops=flops, bytes_accessed=nbytes, transcendentals=0)


class Sizes:
    def __init__(self, features, block_orders, offsets, weights, block_owner):
        self.subjects = lax.axis_size("subj")
        self.n = lax.axis_size("tr")
        self.middle = self.n // 8 * 4 + 3
        self.rows, self.width = features.shape
        self.columns, self.voxels = weights.shape[1:]
        self.bands, self.taps = offsets.shape
        self.band_width = self.columns // self.bands
        self.piece = min(self.width, self.band_width)
        self.conditions = block_orders.shape[0] + 1
        self.blocks = block_owner.shape[1]
        self.ext = self.rows + MAXLAG
        self.own = self.rows // GROUP
        self.own_tail = MAXLAG // GROUP
        self.tiles = self.voxels // LANES
        self.groups = self.n // GROUP
        self.half = self.own // 2
        self.tail_at = self.tiles * self.own
        self.signal_at = self.tail_at + self.tiles * self.own_tail
        self.message = self.signal_at + self.half
        self.pair = 2 * (self.own + 8)
        assert GROUP * CAP * VB * 2 == LANES and self.n % GROUP == 0
        assert self.n & (self.n - 1) == 0 and self.n >= 8
        assert self.half % 8 == 0 and self.conditions < 8 and 8 % self.own_tail == 0
        assert self.tiles * self.own_tail % 8 == 0


BITS, LEAST = 7, -126
STEPS, SMALLEST = 668.0, -36.0


def place_of(z, position):
    position = position ^ z.middle
    low = (position >> 2 & 1) + (position & 2) + (position & 1) * 4
    return (position >> 3) * 8 + low


def coded_signal(x):
    size = jnp.abs(x)
    power = jnp.floor(jnp.log2(jnp.maximum(size, 2.0**LEAST)))
    half = jnp.floor(power * 0.5)
    significand = size * jnp.exp2(-half) * jnp.exp2(half - power)
    code = jnp.round((power - LEAST + significand - 1.0) * 2.0**BITS)
    code = jnp.clip(code, 0.0, 32767.0)
    return jnp.where(x < 0.0, -code, code)


def decoded_signal(code):
    size = jnp.abs(code)
    power = lax.shift_right_logical(size, jnp.full_like(size, BITS))
    significand = (size & (2**BITS - 1)) + 2**BITS
    scale = jnp.exp2((power + (LEAST - BITS)).astype(f32))
    value = significand.astype(f32) * scale
    return jnp.where(code < 0, -value, value)


def coded_prediction(x):
    size = jnp.maximum(jnp.abs(x), 2.0**SMALLEST)
    code = jnp.round((jnp.log2(size) - SMALLEST) * STEPS)
    code = jnp.minimum(code, 32767.0)
    return jnp.where(x < 0.0, -code, code)


def decoded_prediction(code):
    value = jnp.exp2(jnp.abs(code) * (1.0 / STEPS) + SMALLEST)
    return jnp.where(code < 0.0, -value, value)


def fill_signal(z, rows_ref, all_columns, base_ref):
    pieces = []
    for member in range(GROUP):
        for part in range(2):
            start = member + GROUP * part * z.half
            piece = [
                rows_ref[pl.ds(tile * z.rows + start, z.half, stride=GROUP), :]
                for tile in range(z.tiles)
            ]
            pieces.append(jnp.concatenate(piece, axis=1))
    value = coded_signal(jnp.concatenate(pieces, axis=0))
    upper = jnp.floor(value * (1.0 / 256.0))
    lower = value - 256.0 * upper
    picked = dot(jnp.concatenate([upper, lower], axis=0).astype(bf16), all_columns)
    value = 256.0 * picked[: z.rows] + picked[z.rows :]
    left = iota((z.half, LANES), 1) < LANES // 2
    for index in range(z.n):
        lanes = slice(index // GROUP * LANES, (index // GROUP + 1) * LANES)
        start = (index % GROUP) * z.own
        first = value[start : start + z.half, lanes]
        second = value[start + z.half : start + z.own, lanes]
        base_ref[index] = jnp.where(left, first, second)


def filtered_product(z, x_ref, w_ref, table_ref, source):
    total = jnp.zeros((z.ext, z.voxels), f32)
    early = iota((8, z.piece), 0) < z.own_tail
    for part in range(z.width // z.piece):
        columns = slice(part * z.piece, (part + 1) * z.piece)
        x = x_ref[:, columns]
        table = table_ref[lax.div(source * z.width + part * z.piece, z.band_width)]
        stacked = jnp.concatenate([x] * (table.shape[1] // z.rows), axis=0)
        filtered = dot(table, stacked)
        low = filtered - filtered.astype(bf16).astype(f32)
        edges = [filtered]
        for start in range(0, z.rows, z.own):
            edges.append(jnp.where(early, low[start : start + 8], 0.0))
        edges.append(low[z.rows :])
        edges = jnp.concatenate(edges, axis=0).astype(bf16)
        product = dot(edges, w_ref[columns, :])
        parts = []
        for member in range(GROUP):
            start, at = member * z.own, z.ext + member * 8
            parts.append(product[start : start + 8] + product[at : at + 8])
            parts.append(product[start + 8 : start + z.own])
        parts.append(product[z.rows : z.ext] + product[z.ext + GROUP * 8 :])
        total = total + jnp.concatenate(parts, axis=0)
    return total


def fill_table(z, offsets_ref, gains_ref, table_ref):
    lanes = table_ref.shape[2]
    column = iota((z.ext, lanes), 1)
    row = iota((z.ext, 1), 0)
    after = row - z.rows
    time = row // z.own + GROUP * (row % z.own)
    time_after = z.rows + after // z.own_tail + GROUP * (after % z.own_tail)
    lag = jnp.where(after < 0, time, time_after) - column % z.rows
    term = column // z.rows
    for band in range(z.bands):
        value = jnp.zeros((z.ext, lanes), f32)
        for tap in range(z.taps):
            hit = lag == offsets_ref[band, tap]
            value = value + jnp.where(hit, gains_ref[band, tap], 0.0)
        first, second, third = (t.astype(f32) for t in thirds(value))
        chosen = jnp.where(term == 0, first, jnp.where(term == 1, second, third))
        chosen = jnp.where(term > 2, 0.0, chosen)
        table_ref[band] = chosen.astype(bf16)


def owned_columns(z, owners_ref):
    owners = owners_ref[...]
    other = iota((z.voxels, z.blocks), 1)
    block = iota((z.voxels, 1), 0) // VB
    owner = jnp.sum(jnp.where(other == block, owners, 0), axis=1, keepdims=True)
    before = (owners == owner) & (other < block)
    rank = jnp.sum(before.astype(i32), axis=1, keepdims=True)
    place = (owner * CAP + rank) * VB + iota((z.voxels, 1), 0) % VB
    lane = iota((1, z.groups * LANES), 1)
    half = LANES // 2
    every = place == lane // LANES * half + lane % half
    group = lax.axis_index("tr") // GROUP
    mine = place == group * half + iota((1, LANES), 1) % half
    voxel = jnp.sum(jnp.where(mine, iota(mine.shape, 0) + 1, 0), axis=0, keepdims=True)
    return every.astype(f32).astype(bf16), voxel - 1


def first_kernel(
    z, offsets_hbm, gains_hbm, owners_hbm, x_hbm, w_hbm, signal_hbm, orders_hbm,
    table_ref, base_ref, mine_ref, total_ref, rest_ref, orders_ref, signal_ref,
    offsets_ref, gains_ref, owners_ref, x_ref, w_ref, rows_ref, sems,
):
    me = lax.axis_index("subj")

    def weight_rows(step):
        source = lax.rem(me + step, z.subjects)
        start = pl.multiple_of(source * z.width, z.width)
        return w_hbm.at[pl.ds(start, z.width), :]

    moves = [
        (offsets_hbm, offsets_ref),
        (gains_hbm, gains_ref),
        (x_hbm, x_ref),
        (weight_rows(0), w_ref),
        (owners_hbm, owners_ref),
        (signal_hbm, signal_ref),
        (orders_hbm, orders_ref),
    ]
    for step in range(1, z.subjects):
        rows = pl.ds((step - 1) * z.width, z.width)
        moves.append((weight_rows(step), rest_ref.at[rows, :]))
    copies = [
        pltpu.make_async_copy(origin, target, sems.at[index])
        for index, (origin, target) in enumerate(moves)
    ]
    for copy in copies:
        copy.start()
    copies[0].wait()
    copies[1].wait()
    fill_table(z, offsets_ref, gains_ref, table_ref)
    copies[2].wait()
    copies[3].wait()
    total_ref[...] = filtered_product(z, x_ref, w_ref, table_ref, me)
    copies[4].wait()
    every, mine = owned_columns(z, owners_ref)
    mine_ref[...] = jnp.broadcast_to(mine, (8, LANES))
    copies[5].wait()
    for tile in range(z.tiles):
        lanes = slice(tile * LANES, (tile + 1) * LANES)
        rows = slice(tile * z.rows, (tile + 1) * z.rows)
        rows_ref[rows, :] = signal_ref[:, lanes].astype(f32)
    fill_signal(z, rows_ref, every, base_ref)
    for copy in copies[6:]:
        copy.wait()


def second_kernel(z, table_ref, w_ref, total_ref, base_ref, _, *refs):
    others, out_ref = refs[:-1], refs[-1]
    me = lax.axis_index("subj")
    total = total_ref[...]
    for step, x_ref in enumerate(others):
        source = lax.rem(me + step + 1, z.subjects)
        rows = w_ref.at[step * z.width : (step + 1) * z.width, :]
        total = total + filtered_product(z, x_ref, rows, table_ref, source)
    value = coded_prediction(total)
    row = iota((8, LANES), 0)
    for member in range(GROUP):
        shared = []
        for tile in range(z.tiles):
            lanes = slice(tile * LANES, (tile + 1) * LANES)
            shared.append(value[member * z.own : (member + 1) * z.own, lanes])
        tails = [jnp.zeros((8, LANES), f32)] * (z.tiles * z.own_tail // 8)
        for tile in range(z.tiles):
            lanes = slice(tile * LANES, (tile + 1) * LANES)
            which, place = divmod(tile * z.own_tail, 8)
            shift = (place - member * z.own_tail) % 8
            tail = pltpu.roll(value[z.rows :, lanes], shift, 0)
            here = (row >= place) & (row < place + z.own_tail)
            tails[which] = jnp.where(here, tail, tails[which])
        for index in range(member, z.n, GROUP):
            message = jnp.concatenate(shared + tails + [base_ref[index]], axis=0)
            message = message.astype(i32).astype(jnp.int16)
            out_ref[place_of(z, index)] = message


def signal_kernel(z, signal_ref, sibling_ref, own_signal_ref):
    member = lax.rem(lax.axis_index("tr"), GROUP)
    shape = (z.own, z.rows)
    pick = iota(shape, 1) == GROUP * iota(shape, 0) + member
    pick = pick.astype(f32).astype(bf16)
    own_signal_ref[0] = dot(pick, signal_ref[...])
    own_signal_ref[1] = dot(pick, sibling_ref[...])


def third_kernel(z, orders_in_ref, mine_ref, own_signal_ref, received_ref, *refs):
    out_refs, (block_ref, tail_ref, *more) = (
        refs[:GROUP],
        refs[GROUP:],
    )
    orders = orders_in_ref[...]
    if more:
        orders_ref, sem = more
        copy = pltpu.make_async_copy(orders_in_ref, orders_ref, sem)
        copy.start()
    me = lax.axis_index("tr")
    row = iota((8, LANES), 0)
    left = iota((z.half, LANES), 1) < LANES // 2

    def integers(index, start, stop):
        return received_ref[place_of(z, index), start:stop, :].astype(i32)

    def tails_of(index):
        x = integers(index, z.tail_at, z.signal_at)
        tails = []
        for tile in range(z.tiles):
            which, place = divmod(tile * z.own_tail, 8)
            tail = pltpu.roll(x[which * 8 : which * 8 + 8], (8 - place) % 8, 0)
            tails.append(jnp.where(row < z.own_tail, tail, 0))
        return tails

    voxel = mine_ref[...]
    tile_of = voxel // LANES
    lane_of = jnp.maximum(voxel, 0) % LANES

    def picked(parts):
        value = jnp.zeros((8, LANES), i32)
        for tile, part in enumerate(parts):
            found = jnp.take_along_axis(part, lane_of, axis=1)
            value = jnp.where(tile_of == tile, found, value)
        return value

    def place(index, carry):
        x = integers(index, 0, z.tail_at)
        for start in range(0, z.half, 8):
            halves = []
            for first in (start, start + z.half):
                at = [tile * z.own + first for tile in range(z.tiles)]
                halves.append(picked([x[i : i + 8] for i in at]))
            value = jnp.where(left[:8], *halves).astype(f32)
            value = jnp.where(voxel >= 0, decoded_prediction(value), 0.0)
            block_ref[index, start : start + 8, :] = value
        tail = decoded_prediction(picked(tails_of(index)).astype(f32))
        here = left[:8] & (row < z.own_tail) & (voxel >= 0)
        tail_ref[index] = jnp.where(here, tail, 0.0)
        return carry

    def add_position(position, sums):
        added = []
        signal = decoded_signal(integers(position, z.signal_at, z.message))
        before = jnp.maximum(position - 1, 0)
        for condition in range(z.conditions + 1):
            if condition == z.conditions:
                residual = signal
            else:
                if condition == 0:
                    here, ahead = position, before
                elif more:
                    here = orders_ref[condition - 1, position]
                    ahead = orders_ref[condition - 1, before]
                else:
                    here = orders[condition - 1, position]
                    ahead = orders[condition - 1, max(position - 1, 0)]
                tail = tail_ref[jnp.where(position == 0, z.n, ahead)]
                residual = signal - block_ref[here]
                parts = [residual[:8] - tail, residual[8:]]
                residual = jnp.concatenate(parts, axis=0)
            value = residual * residual
            total = sums[condition]
            for start in range(0, z.half, 8):
                total = total + value[start : start + 8]
            added.append(total)
        return tuple(added)

    def loop(count, body, carry):
        if more:
            return lax.fori_loop(0, count, body, carry)
        for index in range(count):
            carry = body(index, carry)
        return carry

    def energy_of(step, here, ahead, kept):
        body = decoded_prediction(integers(here, 0, z.tail_at).astype(f32))
        tails = tails_of(ahead)
        total = jnp.zeros((z.own, LANES), f32)
        for tile in range(z.tiles):
            lanes = slice(tile * LANES, (tile + 1) * LANES)
            block = body[tile * z.own : (tile + 1) * z.own]
            residual = own_signal_ref[step, :, lanes] - block
            tail = decoded_prediction(tails[tile].astype(f32)) * kept
            tail = jnp.where(row < z.own_tail, tail, 0.0)
            residual = jnp.concatenate([residual[:8] - tail, residual[8:]], axis=0)
            total = total + residual * residual
        return jnp.sum(total, axis=1, keepdims=True)

    lanes = iota((z.own, LANES), 1)
    column = iota(orders.shape, 1)
    energies = []
    for step in range(GROUP):
        energy = jnp.zeros((z.own, LANES), f32)
        position = jnp.bitwise_xor(me, step)
        kept = jnp.where(position == 0, 0.0, 1.0)
        before = jnp.maximum(position - 1, 0)
        own = jnp.where(column == position, orders, 0)
        own = jnp.sum(own, axis=1, keepdims=True)
        preceding = jnp.where(column == before, orders, 0)
        preceding = jnp.sum(preceding, axis=1, keepdims=True)
        for condition in range(z.conditions):
            if condition == 0:
                here, ahead = position, before
            else:
                here, ahead = own[condition - 1, 0], preceding[condition - 1, 0]
            value = energy_of(step, here, ahead, kept) * (1.0 / z.voxels)
            energy = jnp.where(lanes == condition, value, energy)
        energies.append(energy)
    loop(z.n, place, 0)
    tail_ref[z.n] = jnp.zeros((8, LANES), f32)
    if more:
        copy.wait()
    zero = jnp.zeros((8, LANES), f32)
    sums = loop(z.n, add_position, (zero,) * (z.conditions + 1))
    stats = zero
    for condition, value in enumerate(sums):
        stat = jnp.sum(value, axis=0, keepdims=True)
        stats = jnp.where(row == condition, stat, stats)
    for energy, out_ref in zip(energies, out_refs):
        out_ref[: z.own, :] = energy
        out_ref[z.own :, :] = stats


def fourth_kernel(z, *refs):
    parts, (energy_ref, scores_ref) = refs[:GROUP], refs[GROUP:]
    member = lax.rem(lax.axis_index("tr"), GROUP)
    sums = sum(p[z.own :, :] for p in parts)
    sums = sums + pltpu.roll(sums, LANES // 2, 1)
    signal = sums[z.conditions : z.conditions + 1]
    fit = jnp.log((sums + EPSILON) / (signal + EPSILON))
    terms = [t.astype(f32) for t in thirds(fit)]
    square = (LANES, LANES)
    place = iota(square, 0) // VB - member * CAP
    mean = (place == iota(square, 1)) & (place >= 0) & (place < CAP)
    mean = mean & (iota(square, 0) < LANES // 2)
    mean = jnp.where(mean, 1.0 / VB, 0.0).astype(bf16)
    score = dot(jnp.concatenate(terms, axis=0).astype(bf16), mean)
    turned = jnp.transpose(jnp.concatenate([p[: z.own, :] for p in parts], axis=0))
    column = iota((z.rows, LANES), 0)
    owner = jnp.bitwise_xor(column // z.own, member)
    order = iota((z.rows, LANES), 1) == owner + GROUP * (column % z.own)
    order = order.astype(f32).astype(bf16)
    terms = [t.astype(f32) for t in thirds(turned[:8, : z.rows])]
    energy = dot(jnp.concatenate(terms, axis=0).astype(bf16), order)
    energy = energy[:8] + energy[8:16] + energy[16:]
    score = score[:8] + score[8:16] + score[16:]
    for index in range(z.conditions):
        energy_ref[index] = energy[index : index + 1, : z.rows]
        scores_ref[index] = score[index : index + 1, :CAP]


def on_device(features, block_orders, offsets, tap_gains, weights, signal, block_owner):
    z = Sizes(features, block_orders, offsets, weights, block_owner)
    owners = block_owner.reshape(1, z.blocks)
    siblings = [(i, i ^ 1) for i in range(z.n)]
    others = [
        lax.ppermute(
            features,
            "subj",
            [((i + step) % z.subjects, i) for i in range(z.subjects)],
        )
        for step in range(1, z.subjects)
    ]
    sibling_signal = lax.ppermute(signal[0], "tr", siblings)
    term_lanes = -(-3 * z.rows // LANES) * LANES
    work = 2 * z.ext * z.width * z.voxels
    shapes = [
        jax.ShapeDtypeStruct((z.bands, z.ext, term_lanes), bf16),
        jax.ShapeDtypeStruct((z.n, z.half, LANES), f32),
        jax.ShapeDtypeStruct((8, LANES), i32),
        jax.ShapeDtypeStruct((z.ext, z.voxels), f32),
        jax.ShapeDtypeStruct((z.columns - z.width, z.voxels), bf16),
        jax.ShapeDtypeStruct(block_orders.shape, i32),
        jax.ShapeDtypeStruct((z.rows, z.voxels), bf16),
    ]
    scratch = [
        pltpu.SMEM(offsets.shape, i32),
        pltpu.SMEM(tap_gains.shape, f32),
        pltpu.VMEM(owners.shape, i32),
        pltpu.VMEM(features.shape, bf16),
        pltpu.VMEM((z.width, z.voxels), bf16),
        pltpu.VMEM((z.tiles * z.rows, LANES), f32),
        pltpu.SemaphoreType.DMA((6 + z.subjects,)),
    ]
    operands = (offsets, tap_gains, owners, features, weights[0], signal[0], block_orders)
    operands = [pltpu.with_memory_space_constraint(x, pltpu.HBM) for x in operands]
    table, base, mine, total, rest, orders, signal = pl.pallas_call(
        functools.partial(first_kernel, z),
        out_shape=shapes,
        in_specs=[HBM] * len(operands),
        out_specs=[VMEM] * len(shapes),
        scratch_shapes=scratch,
        compiler_params=params(),
        cost_estimate=cost(work, 3 << 20),
        name="prepare_and_own_columns",
    )(*operands)
    own_signal = pl.pallas_call(
        functools.partial(signal_kernel, z),
        out_shape=jax.ShapeDtypeStruct((GROUP, z.own, z.voxels), f32),
        in_specs=[VMEM, VMEM],
        out_specs=VMEM,
        compiler_params=params(),
        cost_estimate=cost(work // 8, 1 << 18),
        name="signal_rows",
    )(signal, sibling_signal)
    outgoing = pl.pallas_call(
        functools.partial(second_kernel, z),
        out_shape=jax.ShapeDtypeStruct((z.n, z.message, LANES), jnp.int16),
        in_specs=[VMEM] * (5 + len(others)),
        out_specs=VMEM,
        compiler_params=params(),
        cost_estimate=cost(work, 2 << 20),
        name="other_columns",
    )(table, rest, total, base, own_signal, *others)
    order = sorted(range(z.n), key=functools.partial(place_of, z))
    received = lax.all_to_all(
        outgoing, "tr", 0, 0, axis_index_groups=[order], tiled=True
    )
    more = [pltpu.SMEM(block_orders.shape, i32), pltpu.SemaphoreType.DMA]
    more = more if z.n > 16 else []
    part = jax.ShapeDtypeStruct((z.own + 8, LANES), f32)
    parts = pl.pallas_call(
        functools.partial(third_kernel, z),
        out_shape=[part] * GROUP,
        in_specs=[VMEM] * 4,
        out_specs=[VMEM] * GROUP,
        scratch_shapes=[
            pltpu.VMEM((z.n, z.half, LANES), f32),
            pltpu.VMEM((z.n + 1, 8, LANES), f32),
            *more,
        ],
        compiler_params=params(),
        cost_estimate=cost(work, 1 << 20),
        name="residuals",
    )(orders, mine, own_signal, received)
    parts = [parts[0], lax.ppermute(parts[1], "tr", siblings)]
    energy, scores = pl.pallas_call(
        functools.partial(fourth_kernel, z),
        out_shape=[
            jax.ShapeDtypeStruct((z.conditions, 1, z.rows), f32),
            jax.ShapeDtypeStruct((z.conditions, 1, CAP), f32),
        ],
        in_specs=[VMEM] * GROUP,
        out_specs=[VMEM, VMEM],
        compiler_params=params(),
        cost_estimate=cost(1 << 20, 1 << 16),
        name="scores",
    )(*parts)
    return energy.transpose(1, 2, 0), scores.transpose(1, 2, 0)


def solution(mesh):
    placed = (
        P("tr", "subj"),
        P(),
        P(),
        P(),
        P("subj", None, None),
        P("subj", "tr", None),
        P("subj", None, None),
    )
    return jax.shard_map(
        on_device,
        mesh=mesh,
        in_specs=placed,
        out_specs=(P("subj", "tr", None), P("subj", "tr", None)),
        check_vma=False,
    )
```

```python
import functools

import jax
import jax.numpy as jnp
from jax import lax
from jax.experimental import pallas as pl
from jax.experimental.pallas import tpu as pltpu
from jax.sharding import PartitionSpec as P

MAXLAG = 8
VB = 4
CAP = 8
LANES = 128
GROUP = 2
EPSILON = 1e-6

f32 = jnp.float32
bf16 = jnp.bfloat16
i32 = jnp.int32

VMEM = pl.BlockSpec(memory_space=pltpu.VMEM)
HBM = pl.BlockSpec(memory_space=pltpu.HBM)


def iota(shape, axis):
    return lax.broadcasted_iota(i32, shape, axis)


def dot(a, b):
    return jnp.dot(a, b, preferred_element_type=f32)


def thirds(x):
    first = x.astype(bf16)
    rest = x - first.astype(f32)
    second = rest.astype(bf16)
    return first, second, (rest - second.astype(f32)).astype(bf16)


def params(**more):
    return pltpu.CompilerParams(vmem_limit_bytes=48 * 1024 * 1024, **more)


def cost(flops, nbytes):
    return pl.CostEstimate(flops=flops, bytes_accessed=nbytes, transcendentals=0)


class Sizes:
    def __init__(self, features, block_orders, offsets, weights, block_owner):
        self.subjects = lax.axis_size("subj")
        self.n = lax.axis_size("tr")
        self.middle = self.n // 8 * 4 + 3
        self.rows, self.width = features.shape
        self.columns, self.voxels = weights.shape[1:]
        self.bands, self.taps = offsets.shape
        self.band_width = self.columns // self.bands
        self.piece = min(self.width, self.band_width)
        self.conditions = block_orders.shape[0] + 1
        self.blocks = block_owner.shape[1]
        self.ext = self.rows + MAXLAG
        self.own = self.rows // GROUP
        self.own_tail = MAXLAG // GROUP
        self.tiles = self.voxels // LANES
        self.groups = self.n // GROUP
        self.half = self.own // 2
        self.tail_at = self.tiles * self.own
        self.signal_at = self.tail_at + self.tiles * self.own_tail
        self.message = self.signal_at + self.half
        self.pair = 2 * (self.own + 8)
        assert GROUP * CAP * VB * 2 == LANES and self.n % GROUP == 0
        assert self.n & (self.n - 1) == 0 and self.n >= 8
        assert self.half % 8 == 0 and self.conditions < 8 and 8 % self.own_tail == 0
        assert self.tiles * self.own_tail % 8 == 0


BITS, LEAST = 7, -126
STEPS, SMALLEST = 668.0, -36.0


def place_of(z, position):
    position = position ^ z.middle
    low = (position >> 2 & 1) + (position & 2) + (position & 1) * 4
    return (position >> 3) * 8 + low


def coded_signal(x):
    size = jnp.abs(x)
    power = jnp.floor(jnp.log2(jnp.maximum(size, 2.0**LEAST)))
    half = jnp.floor(power * 0.5)
    significand = size * jnp.exp2(-half) * jnp.exp2(half - power)
    code = jnp.round((power - LEAST + significand - 1.0) * 2.0**BITS)
    code = jnp.clip(code, 0.0, 32767.0)
    return jnp.where(x < 0.0, -code, code)


def decoded_signal(code):
    size = jnp.abs(code)
    power = lax.shift_right_logical(size, jnp.full_like(size, BITS))
    significand = (size & (2**BITS - 1)) + 2**BITS
    scale = jnp.exp2((power + (LEAST - BITS)).astype(f32))
    value = significand.astype(f32) * scale
    return jnp.where(code < 0, -value, value)


def coded_prediction(x):
    size = jnp.maximum(jnp.abs(x), 2.0**SMALLEST)
    code = jnp.round((jnp.log2(size) - SMALLEST) * STEPS)
    code = jnp.minimum(code, 32767.0)
    return jnp.where(x < 0.0, -code, code)


def decoded_prediction(code):
    value = jnp.exp2(jnp.abs(code) * (1.0 / STEPS) + SMALLEST)
    return jnp.where(code < 0.0, -value, value)


def fill_signal(z, rows_ref, all_columns, base_ref):
    pieces = []
    for member in range(GROUP):
        for part in range(2):
            start = member + GROUP * part * z.half
            piece = [
                rows_ref[pl.ds(tile * z.rows + start, z.half, stride=GROUP), :]
                for tile in range(z.tiles)
            ]
            pieces.append(jnp.concatenate(piece, axis=1))
    value = coded_signal(jnp.concatenate(pieces, axis=0))
    upper = jnp.floor(value * (1.0 / 256.0))
    lower = value - 256.0 * upper
    picked = dot(jnp.concatenate([upper, lower], axis=0).astype(bf16), all_columns)
    value = 256.0 * picked[: z.rows] + picked[z.rows :]
    left = iota((z.half, LANES), 1) < LANES // 2
    for index in range(z.n):
        lanes = slice(index // GROUP * LANES, (index // GROUP + 1) * LANES)
        start = (index % GROUP) * z.own
        first = value[start : start + z.half, lanes]
        second = value[start + z.half : start + z.own, lanes]
        base_ref[index] = jnp.where(left, first, second)


def filtered_product(z, x_ref, w_ref, table_ref, source):
    total = jnp.zeros((z.ext, z.voxels), f32)
    early = iota((8, z.piece), 0) < z.own_tail
    for part in range(z.width // z.piece):
        columns = slice(part * z.piece, (part + 1) * z.piece)
        x = x_ref[:, columns]
        table = table_ref[lax.div(source * z.width + part * z.piece, z.band_width)]
        stacked = jnp.concatenate([x] * (table.shape[1] // z.rows), axis=0)
        filtered = dot(table, stacked)
        low = filtered - filtered.astype(bf16).astype(f32)
        edges = [filtered]
        for start in range(0, z.rows, z.own):
            edges.append(jnp.where(early, low[start : start + 8], 0.0))
        edges.append(low[z.rows :])
        edges = jnp.concatenate(edges, axis=0).astype(bf16)
        product = dot(edges, w_ref[columns, :])
        parts = []
        for member in range(GROUP):
            start, at = member * z.own, z.ext + member * 8
            parts.append(product[start : start + 8] + product[at : at + 8])
            parts.append(product[start + 8 : start + z.own])
        parts.append(product[z.rows : z.ext] + product[z.ext + GROUP * 8 :])
        total = total + jnp.concatenate(parts, axis=0)
    return total


def fill_table(z, offsets_ref, gains_ref, table_ref):
    lanes = table_ref.shape[2]
    column = iota((z.ext, lanes), 1)
    row = iota((z.ext, 1), 0)
    after = row - z.rows
    time = row // z.own + GROUP * (row % z.own)
    time_after = z.rows + after // z.own_tail + GROUP * (after % z.own_tail)
    lag = jnp.where(after < 0, time, time_after) - column % z.rows
    term = column // z.rows
    for band in range(z.bands):
        value = jnp.zeros((z.ext, lanes), f32)
        for tap in range(z.taps):
            hit = lag == offsets_ref[band, tap]
            value = value + jnp.where(hit, gains_ref[band, tap], 0.0)
        first, second, third = (t.astype(f32) for t in thirds(value))
        chosen = jnp.where(term == 0, first, jnp.where(term == 1, second, third))
        chosen = jnp.where(term > 2, 0.0, chosen)
        table_ref[band] = chosen.astype(bf16)


def owned_columns(z, owners_ref):
    owners = owners_ref[...]
    other = iota((z.voxels, z.blocks), 1)
    block = iota((z.voxels, 1), 0) // VB
    owner = jnp.sum(jnp.where(other == block, owners, 0), axis=1, keepdims=True)
    before = (owners == owner) & (other < block)
    rank = jnp.sum(before.astype(i32), axis=1, keepdims=True)
    place = (owner * CAP + rank) * VB + iota((z.voxels, 1), 0) % VB
    lane = iota((1, z.groups * LANES), 1)
    half = LANES // 2
    every = place == lane // LANES * half + lane % half
    group = lax.axis_index("tr") // GROUP
    mine = place == group * half + iota((1, LANES), 1) % half
    voxel = jnp.sum(jnp.where(mine, iota(mine.shape, 0) + 1, 0), axis=0, keepdims=True)
    return every.astype(f32).astype(bf16), voxel - 1


def first_kernel(
    z, offsets_hbm, gains_hbm, owners_hbm, x_hbm, w_hbm, signal_hbm, orders_hbm,
    table_ref, base_ref, mine_ref, total_ref, rest_ref, orders_ref, signal_ref,
    offsets_ref, gains_ref, owners_ref, x_ref, w_ref, rows_ref, sems,
):
    me = lax.axis_index("subj")

    def weight_rows(step):
        source = lax.rem(me + step, z.subjects)
        start = pl.multiple_of(source * z.width, z.width)
        return w_hbm.at[pl.ds(start, z.width), :]

    moves = [
        (offsets_hbm, offsets_ref),
        (gains_hbm, gains_ref),
        (x_hbm, x_ref),
        (weight_rows(0), w_ref),
        (owners_hbm, owners_ref),
        (signal_hbm, signal_ref),
        (orders_hbm, orders_ref),
    ]
    for step in range(1, z.subjects):
        rows = pl.ds((step - 1) * z.width, z.width)
        moves.append((weight_rows(step), rest_ref.at[rows, :]))
    copies = [
        pltpu.make_async_copy(origin, target, sems.at[index])
        for index, (origin, target) in enumerate(moves)
    ]
    for copy in copies:
        copy.start()
    copies[0].wait()
    copies[1].wait()
    fill_table(z, offsets_ref, gains_ref, table_ref)
    copies[2].wait()
    copies[3].wait()
    total_ref[...] = filtered_product(z, x_ref, w_ref, table_ref, me)
    copies[4].wait()
    every, mine = owned_columns(z, owners_ref)
    mine_ref[...] = jnp.broadcast_to(mine, (8, LANES))
    copies[5].wait()
    for tile in range(z.tiles):
        lanes = slice(tile * LANES, (tile + 1) * LANES)
        rows = slice(tile * z.rows, (tile + 1) * z.rows)
        rows_ref[rows, :] = signal_ref[:, lanes].astype(f32)
    fill_signal(z, rows_ref, every, base_ref)
    for copy in copies[6:]:
        copy.wait()


def second_kernel(
    z, table_ref, w_ref, total_ref, base_ref, signal_ref, sibling_ref, *refs
):
    others, (out_ref, own_signal_ref) = refs[:-2], refs[-2:]
    me = lax.axis_index("subj")
    total = total_ref[...]
    for step, x_ref in enumerate(others):
        source = lax.rem(me + step + 1, z.subjects)
        rows = w_ref.at[step * z.width : (step + 1) * z.width, :]
        total = total + filtered_product(z, x_ref, rows, table_ref, source)
    value = coded_prediction(total)
    row = iota((8, LANES), 0)
    for member in range(GROUP):
        shared = []
        for tile in range(z.tiles):
            lanes = slice(tile * LANES, (tile + 1) * LANES)
            shared.append(value[member * z.own : (member + 1) * z.own, lanes])
        tails = [jnp.zeros((8, LANES), f32)] * (z.tiles * z.own_tail // 8)
        for tile in range(z.tiles):
            lanes = slice(tile * LANES, (tile + 1) * LANES)
            which, place = divmod(tile * z.own_tail, 8)
            shift = (place - member * z.own_tail) % 8
            tail = pltpu.roll(value[z.rows :, lanes], shift, 0)
            here = (row >= place) & (row < place + z.own_tail)
            tails[which] = jnp.where(here, tail, tails[which])
        for index in range(member, z.n, GROUP):
            message = jnp.concatenate(shared + tails + [base_ref[index]], axis=0)
            message = message.astype(i32).astype(jnp.int16)
            out_ref[place_of(z, index)] = message
    member = lax.rem(lax.axis_index("tr"), GROUP)
    shape = (z.own, z.rows)
    pick = iota(shape, 1) == GROUP * iota(shape, 0) + member
    pick = pick.astype(f32).astype(bf16)
    own_signal_ref[0] = dot(pick, signal_ref[...])
    own_signal_ref[1] = dot(pick, sibling_ref[...])


def third_kernel(z, orders_in_ref, mine_ref, own_signal_ref, received_ref, *refs):
    out_refs, (block_ref, tail_ref, *more) = (
        refs[:GROUP],
        refs[GROUP:],
    )
    orders = orders_in_ref[...]
    if more:
        orders_ref, sem = more
        copy = pltpu.make_async_copy(orders_in_ref, orders_ref, sem)
        copy.start()
    me = lax.axis_index("tr")
    row = iota((8, LANES), 0)
    left = iota((z.half, LANES), 1) < LANES // 2

    def integers(index, start, stop):
        return received_ref[place_of(z, index), start:stop, :].astype(i32)

    def tails_of(index):
        x = integers(index, z.tail_at, z.signal_at)
        tails = []
        for tile in range(z.tiles):
            which, place = divmod(tile * z.own_tail, 8)
            tail = pltpu.roll(x[which * 8 : which * 8 + 8], (8 - place) % 8, 0)
            tails.append(jnp.where(row < z.own_tail, tail, 0))
        return tails

    voxel = mine_ref[...]
    tile_of = voxel // LANES
    lane_of = jnp.maximum(voxel, 0) % LANES

    def picked(parts):
        value = jnp.zeros((8, LANES), i32)
        for tile, part in enumerate(parts):
            found = jnp.take_along_axis(part, lane_of, axis=1)
            value = jnp.where(tile_of == tile, found, value)
        return value

    def place(index, carry):
        x = integers(index, 0, z.tail_at)
        for start in range(0, z.half, 8):
            halves = []
            for first in (start, start + z.half):
                at = [tile * z.own + first for tile in range(z.tiles)]
                halves.append(picked([x[i : i + 8] for i in at]))
            value = jnp.where(left[:8], *halves).astype(f32)
            value = jnp.where(voxel >= 0, decoded_prediction(value), 0.0)
            block_ref[index, start : start + 8, :] = value
        tail = decoded_prediction(picked(tails_of(index)).astype(f32))
        here = left[:8] & (row < z.own_tail) & (voxel >= 0)
        tail_ref[index] = jnp.where(here, tail, 0.0)
        return carry

    def add_position(position, sums):
        added = []
        signal = decoded_signal(integers(position, z.signal_at, z.message))
        before = jnp.maximum(position - 1, 0)
        for condition in range(z.conditions + 1):
            if condition == z.conditions:
                residual = signal
            else:
                if condition == 0:
                    here, ahead = position, before
                elif more:
                    here = orders_ref[condition - 1, position]
                    ahead = orders_ref[condition - 1, before]
                else:
                    here = orders[condition - 1, position]
                    ahead = orders[condition - 1, max(position - 1, 0)]
                tail = tail_ref[jnp.where(position == 0, z.n, ahead)]
                residual = signal - block_ref[here]
                parts = [residual[:8] - tail, residual[8:]]
                residual = jnp.concatenate(parts, axis=0)
            value = residual * residual
            total = sums[condition]
            for start in range(0, z.half, 8):
                total = total + value[start : start + 8]
            added.append(total)
        return tuple(added)

    def loop(count, body, carry):
        if more:
            return lax.fori_loop(0, count, body, carry)
        for index in range(count):
            carry = body(index, carry)
        return carry

    def energy_of(step, here, ahead, kept):
        body = decoded_prediction(integers(here, 0, z.tail_at).astype(f32))
        tails = tails_of(ahead)
        total = jnp.zeros((z.own, LANES), f32)
        for tile in range(z.tiles):
            lanes = slice(tile * LANES, (tile + 1) * LANES)
            block = body[tile * z.own : (tile + 1) * z.own]
            residual = own_signal_ref[step, :, lanes] - block
            tail = decoded_prediction(tails[tile].astype(f32)) * kept
            tail = jnp.where(row < z.own_tail, tail, 0.0)
            residual = jnp.concatenate([residual[:8] - tail, residual[8:]], axis=0)
            total = total + residual * residual
        return jnp.sum(total, axis=1, keepdims=True)

    lanes = iota((z.own, LANES), 1)
    column = iota(orders.shape, 1)
    energies = []
    for step in range(GROUP):
        energy = jnp.zeros((z.own, LANES), f32)
        position = jnp.bitwise_xor(me, step)
        kept = jnp.where(position == 0, 0.0, 1.0)
        before = jnp.maximum(position - 1, 0)
        own = jnp.where(column == position, orders, 0)
        own = jnp.sum(own, axis=1, keepdims=True)
        preceding = jnp.where(column == before, orders, 0)
        preceding = jnp.sum(preceding, axis=1, keepdims=True)
        for condition in range(z.conditions):
            if condition == 0:
                here, ahead = position, before
            else:
                here, ahead = own[condition - 1, 0], preceding[condition - 1, 0]
            value = energy_of(step, here, ahead, kept) * (1.0 / z.voxels)
            energy = jnp.where(lanes == condition, value, energy)
        energies.append(energy)
    loop(z.n, place, 0)
    tail_ref[z.n] = jnp.zeros((8, LANES), f32)
    if more:
        copy.wait()
    zero = jnp.zeros((8, LANES), f32)
    sums = loop(z.n, add_position, (zero,) * (z.conditions + 1))
    stats = zero
    for condition, value in enumerate(sums):
        stat = jnp.sum(value, axis=0, keepdims=True)
        stats = jnp.where(row == condition, stat, stats)
    for energy, out_ref in zip(energies, out_refs):
        out_ref[: z.own, :] = energy
        out_ref[z.own :, :] = stats


def fourth_kernel(z, *refs):
    parts, (energy_ref, scores_ref) = refs[:GROUP], refs[GROUP:]
    member = lax.rem(lax.axis_index("tr"), GROUP)
    sums = sum(p[z.own :, :] for p in parts)
    sums = sums + pltpu.roll(sums, LANES // 2, 1)
    signal = sums[z.conditions : z.conditions + 1]
    fit = jnp.log((sums + EPSILON) / (signal + EPSILON))
    slot = iota((8, LANES), 1) % CAP + member * CAP
    score = sum(jnp.take_along_axis(fit, slot * VB + i, axis=1) for i in range(VB))
    score = score * (1.0 / VB)
    turned = jnp.transpose(jnp.concatenate([p[: z.own, :] for p in parts], axis=0))
    column = iota((z.rows, LANES), 0)
    owner = jnp.bitwise_xor(column // z.own, member)
    order = iota((z.rows, LANES), 1) == owner + GROUP * (column % z.own)
    order = order.astype(f32).astype(bf16)
    terms = [t.astype(f32) for t in thirds(turned[:8, : z.rows])]
    energy = dot(jnp.concatenate(terms, axis=0).astype(bf16), order)
    energy = energy[:8] + energy[8:16] + energy[16:]
    for index in range(z.conditions):
        energy_ref[index] = energy[index : index + 1, : z.rows]
        scores_ref[index] = score[index : index + 1, :CAP]


def on_device(features, block_orders, offsets, tap_gains, weights, signal, block_owner):
    z = Sizes(features, block_orders, offsets, weights, block_owner)
    owners = block_owner.reshape(1, z.blocks)
    siblings = [(i, i ^ 1) for i in range(z.n)]
    others = [
        lax.ppermute(
            features,
            "subj",
            [((i + step) % z.subjects, i) for i in range(z.subjects)],
        )
        for step in range(1, z.subjects)
    ]
    sibling_signal = lax.ppermute(signal[0], "tr", siblings)
    term_lanes = -(-3 * z.rows // LANES) * LANES
    work = 2 * z.ext * z.width * z.voxels
    shapes = [
        jax.ShapeDtypeStruct((z.bands, z.ext, term_lanes), bf16),
        jax.ShapeDtypeStruct((z.n, z.half, LANES), f32),
        jax.ShapeDtypeStruct((8, LANES), i32),
        jax.ShapeDtypeStruct((z.ext, z.voxels), f32),
        jax.ShapeDtypeStruct((z.columns - z.width, z.voxels), bf16),
        jax.ShapeDtypeStruct(block_orders.shape, i32),
        jax.ShapeDtypeStruct((z.rows, z.voxels), bf16),
    ]
    scratch = [
        pltpu.SMEM(offsets.shape, i32),
        pltpu.SMEM(tap_gains.shape, f32),
        pltpu.VMEM(owners.shape, i32),
        pltpu.VMEM(features.shape, bf16),
        pltpu.VMEM((z.width, z.voxels), bf16),
        pltpu.VMEM((z.tiles * z.rows, LANES), f32),
        pltpu.SemaphoreType.DMA((6 + z.subjects,)),
    ]
    operands = (offsets, tap_gains, owners, features, weights[0], signal[0], block_orders)
    operands = [pltpu.with_memory_space_constraint(x, pltpu.HBM) for x in operands]
    table, base, mine, total, rest, orders, signal = pl.pallas_call(
        functools.partial(first_kernel, z),
        out_shape=shapes,
        in_specs=[HBM] * len(operands),
        out_specs=[VMEM] * len(shapes),
        scratch_shapes=scratch,
        compiler_params=params(),
        cost_estimate=cost(work, 3 << 20),
        name="prepare_and_own_columns",
    )(*operands)
    outgoing, own_signal = pl.pallas_call(
        functools.partial(second_kernel, z),
        out_shape=[
            jax.ShapeDtypeStruct((z.n, z.message, LANES), jnp.int16),
            jax.ShapeDtypeStruct((GROUP, z.own, z.voxels), f32),
        ],
        in_specs=[VMEM] * (6 + len(others)),
        out_specs=[VMEM, VMEM],
        compiler_params=params(),
        cost_estimate=cost(work, 2 << 20),
        name="other_columns",
    )(table, rest, total, base, signal, sibling_signal, *others)
    order = sorted(range(z.n), key=functools.partial(place_of, z))
    received = lax.all_to_all(
        outgoing, "tr", 0, 0, axis_index_groups=[order], tiled=True
    )
    more = [pltpu.SMEM(block_orders.shape, i32), pltpu.SemaphoreType.DMA]
    more = more if z.n > 16 else []
    part = jax.ShapeDtypeStruct((z.own + 8, LANES), f32)
    parts = pl.pallas_call(
        functools.partial(third_kernel, z),
        out_shape=[part] * GROUP,
        in_specs=[VMEM] * 4,
        out_specs=[VMEM] * GROUP,
        scratch_shapes=[
            pltpu.VMEM((z.n, z.half, LANES), f32),
            pltpu.VMEM((z.n + 1, 8, LANES), f32),
            *more,
        ],
        compiler_params=params(),
        cost_estimate=cost(work, 1 << 20),
        name="residuals",
    )(orders, mine, own_signal, received)
    parts = [parts[0], lax.ppermute(parts[1], "tr", siblings)]
    energy, scores = pl.pallas_call(
        functools.partial(fourth_kernel, z),
        out_shape=[
            jax.ShapeDtypeStruct((z.conditions, 1, z.rows), f32),
            jax.ShapeDtypeStruct((z.conditions, 1, CAP), f32),
        ],
        in_specs=[VMEM] * GROUP,
        out_specs=[VMEM, VMEM],
        compiler_params=params(),
        cost_estimate=cost(1 << 20, 1 << 16),
        name="scores",
    )(*parts)
    return energy.transpose(1, 2, 0), scores.transpose(1, 2, 0)


def solution(mesh):
    placed = (
        P("tr", "subj"),
        P(),
        P(),
        P(),
        P("subj", None, None),
        P("subj", "tr", None),
        P("subj", None, None),
    )
    return jax.shard_map(
        on_device,
        mesh=mesh,
        in_specs=placed,
        out_specs=(P("subj", "tr", None), P("subj", "tr", None)),
        check_vma=False,
    )
```
